32 devices in a mesh: dp: 16 (over z, x, core), fsdp: 2 (over y).
Axes of the slice: x: 2, y: 2, z: 4, core: 2. Of those that a mesh axis runs over, the one named last changes fastest.
Arguments:
- latents: bfloat16 [32, 256, 1024], P(('dp', 'fsdp')), may hold values from -6 to 6
- pixels: bfloat16 [32, 128, 1024], P(('dp', 'fsdp')), may hold values from -6 to 6
- visible: int32 [32], P(('dp', 'fsdp')), may hold values from 32 to 128, as said below
- out_grad: bfloat16 [32, 256, 1024], P(('dp', 'fsdp')), may hold values from -6 to 6
- panel: float32 [1024, 12288], P(('dp', 'fsdp')), may hold values from -0.75 to 0.75
- panel_moment: float32 [1024, 12288], P(('dp', 'fsdp')), may hold values from -0.625 to 0.625
- panel_square: float32 [1024, 12288], P(('dp', 'fsdp')), may hold values from 0.0004096 to 0.0065536
- down: float32 [4096, 1024], P(('dp', 'fsdp')), may hold values from -0.09375 to 0.09375
- down_moment: float32 [4096, 1024], P(('dp', 'fsdp')), may hold values from -0.625 to 0.625
- down_square: float32 [4096, 1024], P(('dp', 'fsdp')), may hold values from 0.0004096 to 0.0065536
- vectors: float32 [13312], P(('dp', 'fsdp')), may hold values from -1.2 to 4
- vector_moment: float32 [13312], P(('dp', 'fsdp')), may hold values from -1.75 to 1.75
- vector_square: float32 [13312], P(('dp', 'fsdp')), may hold values from 0.0036864 to 0.0589824
Outputs:
- latents_out: bfloat16 [32, 256, 1024], P(('dp', 'fsdp'))
- latents_grad: float32 [32, 256, 1024], P(('dp', 'fsdp'))
- grad_norm: float32 [], replicated
- panel_after: float32 [1024, 12288], P(('dp', 'fsdp'))
- panel_moment_after: float32 [1024, 12288], P(('dp', 'fsdp'))
- panel_square_after: float32 [1024, 12288], P(('dp', 'fsdp'))
- down_after: float32 [4096, 1024], P(('dp', 'fsdp'))
- down_moment_after: float32 [4096, 1024], P(('dp', 'fsdp'))
- down_square_after: float32 [4096, 1024], P(('dp', 'fsdp'))
- vectors_after: float32 [13312], P(('dp', 'fsdp'))
- vector_moment_after: float32 [13312], P(('dp', 'fsdp'))
- vector_square_after: float32 [13312], P(('dp', 'fsdp'))
The draws below stay inside these ranges and needn't reach their ends.
Inputs may be any that keep to these rules, and one draw needn't show every extreme that they name: Rows of an image at or after its count are padding; some image has all 128 rows visible.
All inputs are finite; a program needn't handle non-finite values.
Results may differ from the reference program's by a relative error of at most 0.015.
Values may be sent and summed in bfloat16 or wider, within the bound.
A program may use at most 320 MiB of HBM per device.

```python
import math
from functools import partial
import jax
import jax.numpy as jnp
from jax import lax

D = 1024
FF = 4096
HEADS = 8
HEAD_DIM = 128
LAT = 256
PIX = 128
STEP = 10
IMAGES = 32
TOKENS = 8192
VEC = 13312
PARAMS = 16790528
N_DP = 16


def draw_visible(key, part):
    key = jax.random.fold_in(key, 1)
    drawn_counts = jax.random.randint(key, (IMAGES,), PIX // 4, PIX + 1, dtype=jnp.int32)
    return jnp.where(jnp.arange(IMAGES) == 0, PIX, drawn_counts).astype(jnp.int32)


def draw_panel(key, part):
    key = jax.random.fold_in(key, 2)
    total_columns = 8 * D + FF
    column = jnp.arange(total_columns)
    column_scale = jnp.where((column >= 3 * D) & (column < 4 * D), 4.0, 1.0)
    column_scale = jnp.where((column >= 7 * D) & (column < 8 * D), 6.0, column_scale)
    base_draw = jnp.clip(jax.random.normal(key, (D, total_columns), jnp.float32), -4.0, 4.0)
    return (base_draw * column_scale[None, :] * D ** (-0.5)).astype(jnp.float32)


def draw_vectors(key, part):
    key = jax.random.fold_in(key, 3)
    position = jnp.arange(D)
    block_rows = D // N_DP
    within = (position % block_rows).astype(jnp.float32) / block_rows
    across = position.astype(jnp.float32) / D
    rise_factor = 3.0
    centre_scale = 0.5 * 3.0 ** 0.6 / rise_factor ** 0.6
    jitter = jax.random.uniform(jax.random.fold_in(key, 11), (4, D), jnp.float32, 0.85, 1.15)
    gain_rows = centre_scale * (rise_factor ** (0.6 * within + 0.6 * across))[None, :] * jitter
    biases = 0.2 * jnp.clip(jax.random.normal(jax.random.fold_in(key, 12), (5, D), jnp.float32), -4.0, 4.0)
    up_bias = 0.3 * jnp.clip(jax.random.normal(jax.random.fold_in(key, 13), (FF,), jnp.float32), -4.0, 4.0)
    pieces = [gain_rows[0], biases[0], gain_rows[1], biases[1], gain_rows[2], biases[2], gain_rows[3], biases[3], biases[4], up_bias]
    return jnp.concatenate(pieces).astype(jnp.float32)


def steps_of(key, extent, shards, low, high):
    loudness, own = 1.0, jax.random.fold_in(key, 6)
    for axis_at, shards_of in shards:
        draws = jnp.exp(jax.random.uniform(jax.random.fold_in(own, axis_at), (shards_of,), jnp.float32, low / len(shards), high / len(shards)))
        loudness = loudness * jnp.repeat(draws, extent[axis_at] // shards_of).reshape([-1 if axis == axis_at else 1 for axis in range(len(extent))])
    return loudness


def bell_draw(own_key, shape, spread, bound, split=(), held_as=jnp.bfloat16):
    result = jax.random.normal(own_key, shape, jnp.float32) * spread
    if len(split) > 0:
        result = steps_of(own_key, shape, split, -0.22, 0.18) * result
    return jnp.clip(result, min=-bound, max=bound).astype(held_as)


def setup_inputs(seed: int = 0) -> dict:
    key_of = jax.random.split(jax.random.key(seed), 14)
    return {
        "latents": bell_draw(key_of[0], (IMAGES, LAT, D), 1.0, 6.0, ((0, 32),)),
        "pixels": bell_draw(key_of[1], (IMAGES, PIX, D), 1.0, 6.0, ((0, 32),)),
        "visible": draw_visible(jax.random.fold_in(key_of[13], 71), 0),
        "out_grad": bell_draw(key_of[3], (IMAGES, LAT, D), 1.0, 6.0, ((0, 32),)),
        "panel": draw_panel(jax.random.fold_in(key_of[13], 71), 0),
        "panel_moment": bell_draw(key_of[5], (D, 8 * D + FF), (0.00111 * TOKENS ** 0.5), 0.625, ((0, 32),), jnp.float32),
        "panel_square": jnp.clip(jnp.exp(math.log(0.0065536) - 2.7725887 * jax.random.uniform(key_of[6], (D, 8 * D + FF), jnp.float32) ** steps_of(key_of[6], (D, 8 * D + FF), ((0, 32),), -0.2, 0.2)), 0.0004096, 0.0065536),
        "down": bell_draw(key_of[7], (FF, D), FF ** -0.5, 0.09375, ((0, 32),), jnp.float32),
        "down_moment": bell_draw(key_of[8], (FF, D), (0.00111 * TOKENS ** 0.5), 0.625, ((0, 32),), jnp.float32),
        "down_square": jnp.clip(jnp.exp(math.log(0.0065536) - 2.7725887 * jax.random.uniform(key_of[9], (FF, D), jnp.float32) ** steps_of(key_of[9], (FF, D), ((0, 32),), -0.2, 0.2)), 0.0004096, 0.0065536),
        "vectors": draw_vectors(jax.random.fold_in(key_of[13], 71), 0),
        "vector_moment": bell_draw(key_of[11], (VEC,), (0.00333 * TOKENS ** 0.5), 1.75, ((0, 32),), jnp.float32),
        "vector_square": jnp.clip(jnp.exp(math.log(0.0589824) - 2.7725887 * jax.random.uniform(key_of[12], (VEC,), jnp.float32) ** steps_of(key_of[12], (VEC,), ((0, 32),), -0.2, 0.2)), 0.0036864, 0.0589824),
    }


@jax.custom_vjp
def low(v):
    return lax.optimization_barrier(v.astype(jnp.bfloat16)).astype(jnp.float32)

@jax.custom_vjp
def low_back(v):
    return v

def low_keep(v):
    return (low(v), None)

def low_pass(kept, grad):
    return (grad,)

def back_keep(v):
    return (v, None)

def back_low(kept, grad):
    return (low(grad),)
low.defvjp(low_keep, low_pass)
low_back.defvjp(back_keep, back_low)
norm_eps = 1e-05
beta_first = 0.9
beta_second = 0.999
adam_eps = 1e-08
rate_matrix = 0.05
rate_vector = 0.5
weight_decay = 0.1
clip_coeff = 0.01
masked_fill = -1e+30
precise = lax.Precision.HIGHEST

def both_ways(values):
    return low_back(low(values))

def matmul_high(left, right):
    return jnp.dot(left, right, precision=precise, preferred_element_type=jnp.float32)

def layer_norm(values, gain_row, shift_row):
    centre = values - lax.optimization_barrier(jnp.mean(values, axis=-1, keepdims=True))
    inverse = lax.rsqrt(lax.optimization_barrier(jnp.mean(centre * centre, axis=-1, keepdims=True)) + norm_eps)
    return centre * inverse * gain_row + shift_row

def attend(queries, key_rows, value_rows, visible_mask):
    query_heads = queries.reshape(queries.shape[0], HEADS, HEAD_DIM)
    key_heads = key_rows.reshape(key_rows.shape[0], HEADS, HEAD_DIM)
    value_heads = value_rows.reshape(value_rows.shape[0], HEADS, HEAD_DIM)
    scores = jnp.einsum('qhd,khd->hqk', query_heads, key_heads, precision=precise) * HEAD_DIM ** (-0.5)
    scores = low_back(scores)
    masked = jnp.where(visible_mask[None, None, :], scores, masked_fill)
    row_top = lax.optimization_barrier(jnp.max(masked, axis=-1, keepdims=True))
    powers = jnp.exp(masked - row_top)
    probability = low(powers / lax.optimization_barrier(jnp.sum(powers, axis=-1, keepdims=True)))
    mixture = jnp.einsum('hqk,khd->qhd', probability, value_heads, precision=precise)
    return both_ways(mixture.reshape(queries.shape[0], D))

def image_forward(weights, latent, pixel, count):
    panel_w, down_w, vector_w = weights
    gain_pixel = vector_w[0:D]
    shift_pixel = vector_w[D:2 * D]
    gain_cross = vector_w[2 * D:3 * D]
    shift_cross = vector_w[3 * D:4 * D]
    gain_self = vector_w[4 * D:5 * D]
    shift_self = vector_w[5 * D:6 * D]
    gain_feed = vector_w[6 * D:7 * D]
    shift_feed = vector_w[7 * D:8 * D]
    bias_down = vector_w[8 * D:9 * D]
    bias_up = vector_w[9 * D:]
    pixel_norm = low(layer_norm(pixel, gain_pixel, shift_pixel))
    cross_norm = low(layer_norm(latent, gain_cross, shift_cross))
    cross_query = both_ways(matmul_high(cross_norm, panel_w[:, :D]))
    cross_pair = both_ways(matmul_high(pixel_norm, panel_w[:, D:3 * D]))
    visible_mask = jnp.arange(PIX, dtype=jnp.int32) < count
    cross_mix = attend(cross_query, cross_pair[:, :D], cross_pair[:, D:], visible_mask)
    first_sum = latent + low_back(matmul_high(cross_mix, panel_w[:, 3 * D:4 * D]))
    self_norm = low(layer_norm(first_sum, gain_self, shift_self))
    triple = both_ways(matmul_high(self_norm, panel_w[:, 4 * D:7 * D]))
    every_key = jnp.ones((LAT,), dtype=jnp.bool_)
    self_mix = attend(triple[:, :D], triple[:, D:2 * D], triple[:, 2 * D:], every_key)
    second_sum = first_sum + low_back(matmul_high(self_mix, panel_w[:, 7 * D:8 * D]))
    feed_norm = low(layer_norm(second_sum, gain_feed, shift_feed))
    upper_in = low_back(matmul_high(feed_norm, panel_w[:, 8 * D:]) + bias_up)
    hidden = low(jax.nn.gelu(upper_in, approximate=False))
    return second_sum + low_back(matmul_high(hidden, down_w) + bias_down)

def adam_update(weight, moment, square, grad, rate, decay):
    moment_after = beta_first * moment + (1.0 - beta_first) * grad
    square_after = beta_second * square + (1.0 - beta_second) * grad * grad
    fixed_moment = moment_after / (1.0 - beta_first ** STEP)
    fixed_square = square_after / (1.0 - beta_second ** STEP)
    weight_after = weight - rate * (fixed_moment / (jnp.sqrt(fixed_square) + adam_eps) + decay * weight)
    return (weight_after, moment_after, square_after)

def reference(latents, pixels, visible, out_grad, panel, panel_moment, panel_square, down, down_moment, down_square, vectors, vector_moment, vector_square):
    group_size = math.gcd(IMAGES, 16)
    block_count = IMAGES // group_size
    masters = (panel, down, vectors)

    def group_forward(weights, latent_rows, pixel_rows, count_rows):
        lowered = jax.tree.map(low, weights)
        return jax.vmap(partial(image_forward, lowered))(latent_rows, pixel_rows, count_rows)

    def scan_step(running, inputs):
        latent_rows, pixel_rows, count_rows, grad_rows = inputs

        def closed(weights, latent_in):
            return group_forward(weights, latent_in, pixel_rows.astype(jnp.float32), count_rows)
        output, pullback = jax.vjp(closed, masters, latent_rows.astype(jnp.float32))
        weight_grads, latent_grad = pullback(grad_rows.astype(jnp.float32))
        running = jax.tree.map(jnp.add, running, weight_grads)
        return (running, (output.astype(jnp.bfloat16), latent_grad))
    stacked = (latents.reshape(block_count, group_size, LAT, D), pixels.reshape(block_count, group_size, PIX, D), visible.reshape(block_count, group_size), out_grad.reshape(block_count, group_size, LAT, D))
    starting = jax.tree.map(jnp.zeros_like, masters)
    grads, (outputs, latent_grads) = lax.scan(scan_step, starting, stacked)
    panel_grad, down_grad, vector_grad = grads
    squares = jnp.sum(panel_grad * panel_grad) + jnp.sum(down_grad * down_grad) + jnp.sum(vector_grad * vector_grad)
    grad_norm = jnp.sqrt(squares)
    threshold = clip_coeff * (TOKENS * PARAMS) ** 0.5
    factor = threshold / jnp.maximum(grad_norm, threshold)
    panel_after, panel_moment_after, panel_square_after = adam_update(panel, panel_moment, panel_square, panel_grad * factor, rate_matrix, weight_decay)
    down_after, down_moment_after, down_square_after = adam_update(down, down_moment, down_square, down_grad * factor, rate_matrix, weight_decay)
    vectors_after, vector_moment_after, vector_square_after = adam_update(vectors, vector_moment, vector_square, vector_grad * factor, rate_vector, 0.0)
    latents_out = outputs.reshape(IMAGES, LAT, D)
    latents_grad = latent_grads.reshape(IMAGES, LAT, D)
    return (latents_out, latents_grad, grad_norm, panel_after, panel_moment_after, panel_square_after, down_after, down_moment_after, down_square_after, vectors_after, vector_moment_after, vector_square_after)
```

```python
import functools

import jax
import jax.numpy as jnp
from jax import lax
from jax.experimental import pallas as pl
from jax.experimental.pallas import tpu as pltpu
from jax.sharding import PartitionSpec as P

HEADS = 8
STEP = 10


norm_eps = 1e-05
beta_first = 0.9
beta_second = 0.999
adam_eps = 1e-08
rate_matrix = 0.05
rate_vector = 0.5
weight_decay = 0.1
clip_coeff = 0.01
masked_fill = -1e30


def matmul_low(left, right):
    return jnp.dot(left, right, preferred_element_type=jnp.float32)


def rows_inner(left, right):
    return lax.dot_general(
        left, right, (((0,), (0,)), ((), ())), preferred_element_type=jnp.float32
    )


def times_transposed(left, right):
    return lax.dot_general(
        left, right, (((1,), (1,)), ((), ())), preferred_element_type=jnp.float32
    )


def gelu_exact(values):
    return jax.nn.gelu(values, approximate=False)


def norm_forward(values, gain_row, shift_row):
    centre = values - jnp.mean(values, axis=-1, keepdims=True)
    inverse = lax.rsqrt(jnp.mean(centre * centre, axis=-1, keepdims=True) + norm_eps)
    normed = centre * inverse
    return (normed * gain_row + shift_row, normed, inverse)


def norm_backward(grad_out, normed, inverse, gain_row):
    grad_normed = grad_out * gain_row
    grad_values = inverse * (
        grad_normed
        - jnp.mean(grad_normed, axis=-1, keepdims=True)
        - normed * jnp.mean(grad_normed * normed, axis=-1, keepdims=True)
    )
    return (grad_values, jnp.sum(grad_out * normed, axis=0), jnp.sum(grad_out, axis=0))


def to_heads(rows, images, head_count):
    return rows.reshape(images, -1, head_count, rows.shape[1] // head_count)


def masked_scores(queries, key_rows, visible_mask):
    score_scale = queries.shape[-1] ** (-0.5)
    scores = (
        jnp.einsum("bqhd,bkhd->bhqk", queries, key_rows, preferred_element_type=jnp.float32)
        * score_scale
    )
    if visible_mask is not None:
        scores = jnp.where(visible_mask[:, None, None, :], scores, masked_fill)
    return scores


def attend_forward(queries, key_rows, value_rows, visible_mask):
    scores = masked_scores(queries, key_rows, visible_mask)
    row_top = jnp.max(scores, axis=-1, keepdims=True)
    powers = jnp.exp(scores - row_top)
    row_total = jnp.sum(powers, axis=-1, keepdims=True)
    probability = (powers / row_total).astype(jnp.bfloat16)
    mixture = jnp.einsum(
        "bhqk,bkhd->bqhd", probability, value_rows, preferred_element_type=jnp.float32
    )
    return (mixture.astype(jnp.bfloat16), row_top, row_total)


def attend_backward(grad_mix, queries, key_rows, value_rows, visible_mask, row_top, row_total):
    score_scale = queries.shape[-1] ** (-0.5)
    scores = masked_scores(queries, key_rows, visible_mask)
    probability = jnp.exp(scores - row_top) / row_total
    grad_prob = jnp.einsum(
        "bqhd,bkhd->bhqk", grad_mix, value_rows, preferred_element_type=jnp.float32
    )
    inner_sum = jnp.sum(grad_prob * probability, axis=-1, keepdims=True)
    grad_scores = (probability * (grad_prob - inner_sum)).astype(jnp.bfloat16)
    grad_queries = (
        jnp.einsum("bhqk,bkhd->bqhd", grad_scores, key_rows, preferred_element_type=jnp.float32)
        * score_scale
    )
    grad_keys = (
        jnp.einsum("bhqk,bqhd->bkhd", grad_scores, queries, preferred_element_type=jnp.float32)
        * score_scale
    )
    grad_values = jnp.einsum(
        "bhqk,bqhd->bkhd",
        probability.astype(jnp.bfloat16),
        grad_mix,
        preferred_element_type=jnp.float32,
    )
    return (grad_queries, grad_keys, grad_values)


def vector_slot(vector_float, index, model_width):
    return vector_float[index * model_width : (index + 1) * model_width]


def self_forward(first_sum, self_columns, gain_self, shift_self, images):
    model_width = first_sum.shape[1]
    normed_out, normed, inverse = norm_forward(first_sum, gain_self, shift_self)
    self_low = normed_out.astype(jnp.bfloat16)
    triple = matmul_low(self_low, self_columns[:, : 3 * model_width]).astype(jnp.bfloat16)
    self_queries = to_heads(triple[:, :model_width], images, HEADS)
    self_keys = to_heads(triple[:, model_width : 2 * model_width], images, HEADS)
    self_values = to_heads(triple[:, 2 * model_width :], images, HEADS)
    mixture, row_top, row_total = attend_forward(self_queries, self_keys, self_values, None)
    self_mixed = mixture.reshape(-1, model_width)
    return (
        normed,
        inverse,
        self_low,
        self_queries,
        self_keys,
        self_values,
        self_mixed,
        row_top,
        row_total,
    )


def adam_update(weight, moment, square, grad, rate, decay):
    moment_after = beta_first * moment + (1.0 - beta_first) * grad
    square_after = beta_second * square + (1.0 - beta_second) * grad * grad
    step_count = STEP
    fixed_moment = moment_after / (1.0 - beta_first**step_count)
    fixed_square = square_after / (1.0 - beta_second**step_count)
    weight_after = weight - rate * (
        fixed_moment / (jnp.sqrt(fixed_square) + adam_eps) + decay * weight
    )
    return (weight_after, moment_after, square_after)


MESH = pl.DeviceIdType.MESH
LONG, SHORT = 4, 2
CUT = (LONG, SHORT, SHORT, SHORT)


class Place:
    def __init__(self):
        row, self.y = lax.axis_index("dp"), lax.axis_index("fsdp")
        self.z, self.x, self.core = row // 4, (row // 2) % 2, row % 2
        even = self.core == 0
        x, y = self.x, self.y
        self.near = (jnp.where(even, 1 - x, x), jnp.where(even, y, 1 - y))
        self.far = (jnp.where(even, x, 1 - x), jnp.where(even, 1 - y, y))
        self.first, self.second = jnp.where(even, x, y), jnp.where(even, y, x)

    def device(self, z, x, core, y):
        return (z * 4 + x * 2 + core, y)

    def along(self, step):
        return self.device((self.z + step) % LONG, self.x, self.core, self.y)

    def partners(self):
        return [self.along(step) for step in range(1, LONG)] + [
            self.device(self.z, self.near[0], self.core, self.near[1]),
            self.device(self.z, self.far[0], self.core, self.far[1]),
            self.device(self.z, self.x, 1 - self.core, self.y),
        ]

    def greet(self):
        barrier = pltpu.get_barrier_semaphore()
        for partner in self.partners():
            pl.semaphore_signal(barrier, inc=1, device_id=partner, device_id_type=MESH)
        pl.semaphore_wait(barrier, len(self.partners()))


def remote(source, target, send, receive, device):
    return pltpu.make_async_remote_copy(
        src_ref=source,
        dst_ref=target,
        send_sem=send,
        recv_sem=receive,
        device_id=device,
        device_id_type=MESH,
    )


GATHER_KINDS = LONG - 1 + 1 + 2 + 4


def gather_kernel(widths, *refs):
    count = len(widths)
    shares, wholes = refs[:count], refs[count : 2 * count]
    send, receive, own = refs[2 * count :]
    here = Place()
    z, x, core, y = here.z, here.x, here.core, here.y
    _, _, _, near, far, twin = here.partners()
    chunks = []
    for share, whole, width in zip(shares, wholes, widths):
        for start in range(0, share.shape[1], width):
            chunks.append(
                (share.at[:, pl.ds(start, width)], whole.at[:, :, :, :, :, pl.ds(start, width)])
            )
    keep = [
        pltpu.make_async_copy(share, whole.at[z, x, core, y], own.at[n])
        for n, (share, whole) in enumerate(zip(shares, wholes))
    ]
    for copy in keep:
        copy.start()
    here.greet()
    for copy in keep:
        copy.wait()

    def copy_of(n, kind, back=False):
        share, whole = chunks[n]
        if kind < 3:
            device, source = here.along(kind + 1), share
            target = whole.at[z, x, core, y]
            landing = whole.at[(z - kind - 1) % LONG, x, core, y]
        else:
            sets = ((x, y), here.near, here.far, (1 - x, 1 - y))
            spot = sets[(0, 0, 1, 0, 1, 2, 3)[kind - 3]]
            source = target = whole.at[:, spot[0], core, spot[1]]
            device = (near, far, far, twin, twin, twin, twin)[kind - 3]
            if kind < 6:
                landed = sets[(1, 2, 3)[kind - 3]]
                landing = whole.at[:, landed[0], core, landed[1]]
            else:
                landed = sets[(0, 2, 1, 3)[kind - 6]]
                landing = whole.at[:, landed[0], 1 - core, landed[1]]
        if back:
            source = target = landing
        return remote(source, target, send.at[n, kind], receive.at[n, kind], device)

    def start(n, *kinds):
        for kind in kinds:
            copy_of(n, kind).start()

    def arrived(n, *kinds):
        for kind in kinds:
            copy_of(n, kind, True).wait_recv()

    total = len(chunks)
    for n in range(min(2, total)):
        start(n, 0, 1, 2)
    for tick in range(total + 2):
        if tick + 2 < total:
            start(tick + 2, 0, 1, 2)
        if tick < total:
            arrived(tick, 0, 1, 2)
            start(tick, 3, 4, 6)
        if 0 <= tick - 1 < total:
            arrived(tick - 1, 3)
            start(tick - 1, 5, 7)
        if 0 <= tick - 2 < total:
            arrived(tick - 2, 4, 5)
            start(tick - 2, 8, 9)
    for n in range(total):
        arrived(n, 6, 7, 8, 9)
    for n in range(total):
        for kind in range(GATHER_KINDS):
            copy_of(n, kind).wait_send()


def gather_all(shares, widths):
    chunks = sum(share.shape[1] // width for share, width in zip(shares, widths))
    return pl.pallas_call(
        functools.partial(gather_kernel, tuple(widths)),
        out_shape=[jax.ShapeDtypeStruct(CUT + share.shape, share.dtype) for share in shares],
        in_specs=[pl.BlockSpec(memory_space=pl.ANY)] * len(shares),
        out_specs=[pl.BlockSpec(memory_space=pl.ANY)] * len(shares),
        scratch_shapes=[
            pltpu.SemaphoreType.DMA((chunks, GATHER_KINDS)),
            pltpu.SemaphoreType.DMA((chunks, GATHER_KINDS)),
            pltpu.SemaphoreType.DMA((len(shares),)),
        ],
        compiler_params=pltpu.CompilerParams(collective_id=0, has_side_effects=True),
    )(*shares)


REDUCE_KINDS = 4 + 1 + 1 + 3
LOADS = 3


def reduce_kernel(widths, kinds, *refs):
    count = len(widths)
    grads, shares, squares = refs[:count], refs[count : 2 * count], refs[2 * count]
    scratch = refs[2 * count + 1 :]
    families = max(kinds) + 1
    stores = [scratch[5 * k : 5 * k + 5] for k in range(families)]
    total_ref, meet, send, receive, loaded, meet_send, meet_receive = scratch[5 * families :]
    here = Place()
    z, x, core, y = here.z, here.x, here.core, here.y
    first, second = here.first, here.second
    _, _, _, near, far, twin = here.partners()
    here.greet()
    chunks, used = [], [0] * families
    for grad, share, width, kind in zip(grads, shares, widths, kinds):
        for start_at in range(0, grad.shape[5], width):
            chunks.append((grad, share, start_at, width, stores[kind], used[kind]))
            used[kind] += 1

    def spot(side, one, two):
        return jnp.where(side == 0, one, two), jnp.where(side == 0, two, one)

    def load_copies(n):
        grad, _, start_at, width, store, slot = chunks[n]
        part = grad.at[:, :, :, :, :, pl.ds(start_at, width)]
        copies = []
        for k in range(4):
            to_x, to_y = spot(core, k // 2, k % 2)
            copies.append(
                pltpu.make_async_copy(
                    part.at[:, to_x, core, to_y],
                    store[0].at[slot % LOADS, :, k // 2, k % 2],
                    loaded.at[n, k],
                )
            )
        return copies

    def twin_copies(n):
        grad, _, start_at, width, store, slot = chunks[n]
        part = grad.at[:, :, :, :, :, pl.ds(start_at, width)]
        copies = []
        for k in range(4):
            to_x, to_y = spot(1 - core, k // 2, k % 2)
            copies.append(
                remote(
                    part.at[:, to_x, 1 - core, to_y],
                    store[1].at[slot, :, k // 2, k % 2],
                    send.at[n, k],
                    receive.at[n, k],
                    twin,
                )
            )
        return copies

    def far_copy(n):
        store, slot = chunks[n][4:]
        return remote(
            store[1].at[slot, :, :, 1 - second],
            store[2].at[slot],
            send.at[n, 4],
            receive.at[n, 4],
            far,
        )

    def near_copy(n):
        store, slot = chunks[n][4:]
        return remote(
            store[2].at[slot, :, 1 - first],
            store[3].at[slot],
            send.at[n, 5],
            receive.at[n, 5],
            near,
        )

    def long_copies(n):
        store, slot = chunks[n][4:]
        return [
            remote(
                store[3].at[slot, (z + step) % LONG],
                store[4].at[slot, step - 1],
                send.at[n, 5 + step],
                receive.at[n, 5 + step],
                here.along(step),
            )
            for step in range(1, LONG)
        ]

    def add_up(target, source):
        target[...] = (target[...].astype(jnp.float32) + source[...].astype(jnp.float32)).astype(
            target.dtype
        )

    def begin(n):
        for copy in load_copies(n) + twin_copies(n):
            copy.start()

    def stage_twin(n):
        store, slot = chunks[n][4:]
        for copy in load_copies(n):
            copy.wait()
        for copy in twin_copies(n):
            copy.wait_recv()

        def one(at, carry):
            a, b, c = at // 4, (at // 2) % 2, at % 2
            add_up(store[1].at[slot, a, b, c], store[0].at[slot % LOADS, a, b, c])
            return carry

        lax.fori_loop(0, 16, one, 0)
        far_copy(n).start()

    def stage_far(n):
        store, slot = chunks[n][4:]
        far_copy(n).wait_recv()

        def one(at, carry):
            a, b = at // 2, at % 2
            add_up(store[2].at[slot, a, b], store[1].at[slot, a, b, second])
            return carry

        lax.fori_loop(0, 8, one, 0)
        near_copy(n).start()

    def stage_near(n):
        store, slot = chunks[n][4:]
        near_copy(n).wait_recv()

        def one(at, carry):
            add_up(store[3].at[slot, at], store[2].at[slot, at, first])
            return carry

        lax.fori_loop(0, 4, one, 0)
        for copy in long_copies(n):
            copy.start()

    def stage_long(n):
        _, share, start_at, width, store, slot = chunks[n]
        for copy in long_copies(n):
            copy.wait_recv()
        rows = share.shape[0]
        step_rows = min(rows, 32)

        def one(at, carry):
            lines = pl.ds(pl.multiple_of(at * step_rows, step_rows), step_rows)
            value = store[3][slot, z, lines, :].astype(jnp.float32)
            for step in range(LONG - 1):
                value = value + store[4][slot, step, lines, :].astype(jnp.float32)
            share[lines, pl.ds(start_at, width)] = value
            square = value * value
            gained = total_ref[...]
            for down_at in range(0, step_rows, 8):
                for across in range(0, width, 128):
                    gained = gained + square[down_at : down_at + 8, across : across + 128]
            total_ref[...] = gained
            return carry

        lax.fori_loop(0, rows // step_rows, one, 0)

    total_ref[...] = jnp.zeros_like(total_ref)
    total = len(chunks)
    for n in range(min(2, total)):
        begin(n)
    for tick in range(total + 3):
        if tick + 2 < total:
            begin(tick + 2)
        if tick < total:
            stage_twin(tick)
        if 0 <= tick - 1 < total:
            stage_far(tick - 1)
        if 0 <= tick - 2 < total:
            stage_near(tick - 2)
        if 0 <= tick - 3 < total:
            stage_long(tick - 3)
    for n in range(total):
        for copy in twin_copies(n) + [far_copy(n), near_copy(n)] + long_copies(n):
            copy.wait_send()

    meet[z] = total_ref[...]
    copies = [
        remote(
            total_ref,
            meet.at[z],
            meet_send.at[step - 1],
            meet_receive.at[step - 1],
            here.along(step),
        )
        for step in range(1, LONG)
    ]
    for copy in copies:
        copy.start()
    for copy in copies:
        copy.wait()
    value = meet[0] + meet[1] + meet[2] + meet[3]
    for k, partner in enumerate((near, far, twin)):
        meet[4 + 2 * k] = value
        copy = remote(
            meet.at[4 + 2 * k],
            meet.at[5 + 2 * k],
            meet_send.at[3 + k],
            meet_receive.at[3 + k],
            partner,
        )
        copy.start()
        copy.wait()
        value = value + meet[5 + 2 * k]
    squares[...] = value


def reduce_all(grads, widths, kinds):
    counts = [0] * (max(kinds) + 1)
    shapes = [None] * len(counts)
    for grad, width, kind in zip(grads, widths, kinds):
        counts[kind] += grad.shape[5] // width
        shapes[kind] = ((grad.shape[4], width), grad.dtype)
    scratch = []
    for number, (shape, dtype) in zip(counts, shapes):
        scratch += [
            pltpu.VMEM((LOADS, LONG, SHORT, SHORT) + shape, dtype),
            pltpu.VMEM((number, LONG, SHORT, SHORT) + shape, dtype),
            pltpu.VMEM((number, LONG, SHORT) + shape, dtype),
            pltpu.VMEM((number, LONG) + shape, dtype),
            pltpu.VMEM((number, LONG - 1) + shape, dtype),
        ]
    chunks = sum(counts)
    return pl.pallas_call(
        functools.partial(reduce_kernel, tuple(widths), tuple(kinds)),
        out_shape=[jax.ShapeDtypeStruct(grad.shape[4:], jnp.float32) for grad in grads]
        + [jax.ShapeDtypeStruct((8, 128), jnp.float32)],
        in_specs=[pl.BlockSpec(memory_space=pl.ANY)] * len(grads),
        out_specs=[pl.BlockSpec(memory_space=pltpu.VMEM)] * (len(grads) + 1),
        scratch_shapes=scratch
        + [
            pltpu.VMEM((8, 128), jnp.float32),
            pltpu.VMEM((10, 8, 128), jnp.float32),
            pltpu.SemaphoreType.DMA((chunks, REDUCE_KINDS)),
            pltpu.SemaphoreType.DMA((chunks, REDUCE_KINDS)),
            pltpu.SemaphoreType.DMA((chunks, 4)),
            pltpu.SemaphoreType.DMA((6,)),
            pltpu.SemaphoreType.DMA((6,)),
        ],
        compiler_params=pltpu.CompilerParams(
            collective_id=1, has_side_effects=True, vmem_limit_bytes=60 * 1024 * 1024
        ),
    )(*grads)


VECTOR_TILE = (8, 128)


def packed(rows):
    spare = VECTOR_TILE[0] * VECTOR_TILE[1] - rows.shape[-1]
    return jnp.pad(rows, ((0, 0), (0, spare))).reshape((-1,) + VECTOR_TILE)


def fast_gather(panel, down, vectors):
    model_width = panel.shape[1] // 12
    bf16 = jnp.bfloat16
    panel_low = panel.astype(bf16)
    shares = [packed(vectors[None])[0]]
    shares += [panel_low[:, k * 4 * model_width : (k + 1) * 4 * model_width] for k in range(3)]
    shares += [down.astype(bf16)]
    vector_tiles, *wholes = gather_all(shares, [128] + [model_width] * 3 + [down.shape[1] // 4])
    full_vector = vector_tiles.reshape(-1, VECTOR_TILE[0] * VECTOR_TILE[1])
    full_vector = full_vector[:, : vectors.shape[0]].reshape(-1)
    cross, self_columns, up = [whole.reshape(-1, whole.shape[5]) for whole in wholes[:3]]
    return cross, self_columns, up, wholes[3].reshape(-1, down.shape[1]), full_vector.astype(bf16)


def slow_gather(panel, down, vectors):
    model_width = panel.shape[1] // 12
    bf16 = jnp.bfloat16
    parts = [panel[:, k * 4 * model_width : (k + 1) * 4 * model_width].astype(bf16) for k in range(3)]
    parts += [down.astype(bf16), vectors.astype(bf16)]
    return [lax.all_gather(part, ("dp", "fsdp"), axis=0, tiled=True) for part in parts]


def cut(grad):
    return grad.reshape(CUT + (-1, grad.shape[1]))


def fast_reduce(pieces, down_grad, vector_grad, share_length):
    bf16 = jnp.bfloat16
    model_width = down_grad.shape[1]
    ordered = [pieces[k] for k in (5, 4, 3, 2, 1, 0)]
    grads = [cut(down_grad.astype(bf16))] + [cut(piece.astype(bf16)) for piece in ordered]
    grads.append(packed(vector_grad.reshape(-1, share_length)).reshape(CUT + VECTOR_TILE))
    widths = [model_width // 4] + [model_width] * len(pieces) + [128]
    kinds = [0] + [1] * len(pieces) + [2]
    *shares, squares = reduce_all(grads, widths, kinds)
    panel_share = jnp.concatenate([shares[k] for k in (6, 5, 4, 3, 2, 1)], axis=1)
    return panel_share, shares[0], shares[7].reshape(-1)[:share_length], jnp.sum(squares)


def slow_reduce(pieces, down_grad, vector_grad, share_length):
    shares = [
        lax.psum_scatter(grad, ("dp", "fsdp"), scatter_dimension=0, tiled=True)
        for grad in (jnp.concatenate(pieces, axis=1), down_grad, vector_grad)
    ]
    squares = lax.psum(sum(jnp.sum(share * share) for share in shares), ("dp", "fsdp"))
    return (*shares, squares)


def shards(
    gather,
    reduce,
    latents,
    pixels,
    visible,
    out_grad,
    panel,
    panel_moment,
    panel_square,
    down,
    down_moment,
    down_square,
    vectors,
    vector_moment,
    vector_square,
):
    images, latent_count, model_width = latents.shape
    pixel_count = pixels.shape[1]
    bf16 = jnp.bfloat16
    cross_columns, self_columns, up_columns, full_down, full_vector = gather(panel, down, vectors)
    vector_float = full_vector.astype(jnp.float32)
    gain_pixel = vector_slot(vector_float, 0, model_width)
    shift_pixel = vector_slot(vector_float, 1, model_width)
    gain_cross = vector_slot(vector_float, 2, model_width)
    shift_cross = vector_slot(vector_float, 3, model_width)
    gain_self = vector_slot(vector_float, 4, model_width)
    shift_self = vector_slot(vector_float, 5, model_width)
    gain_feed = vector_slot(vector_float, 6, model_width)
    shift_feed = vector_slot(vector_float, 7, model_width)
    bias_down = vector_slot(vector_float, 8, model_width)
    bias_up = vector_float[9 * model_width :]
    latent_rows = latents.reshape(-1, model_width).astype(jnp.float32)
    pixel_rows = pixels.reshape(-1, model_width).astype(jnp.float32)
    pixel_out, pixel_normed, pixel_inverse = norm_forward(pixel_rows, gain_pixel, shift_pixel)
    pixel_low = pixel_out.astype(bf16)
    cross_out, cross_normed, cross_inverse = norm_forward(latent_rows, gain_cross, shift_cross)
    cross_low = cross_out.astype(bf16)
    cross_queries = matmul_low(cross_low, cross_columns[:, :model_width]).astype(bf16)
    pair_rows = matmul_low(pixel_low, cross_columns[:, model_width : 3 * model_width]).astype(bf16)
    visible_mask = jnp.arange(pixel_count, dtype=jnp.int32)[None, :] < visible[:, None]
    query_heads = to_heads(cross_queries, images, HEADS)
    key_heads = to_heads(pair_rows[:, :model_width], images, HEADS)
    value_heads = to_heads(pair_rows[:, model_width:], images, HEADS)
    cross_mix, cross_top, cross_total = attend_forward(
        query_heads, key_heads, value_heads, visible_mask
    )
    cross_mixed = cross_mix.reshape(-1, model_width)
    first_sum = latent_rows + matmul_low(
        cross_mixed, cross_columns[:, 3 * model_width :]
    )
    forward_saved = self_forward(first_sum, self_columns, gain_self, shift_self, images)
    second_sum = first_sum + matmul_low(forward_saved[6], self_columns[:, 3 * model_width :])
    feed_out, feed_normed, feed_inverse = norm_forward(second_sum, gain_feed, shift_feed)
    feed_low = feed_out.astype(bf16)
    upper_in = matmul_low(feed_low, up_columns) + bias_up
    hidden_float, gelu_back = jax.vjp(gelu_exact, upper_in)
    hidden = hidden_float.astype(bf16)
    result = second_sum + (matmul_low(hidden, full_down) + bias_down)
    latents_out = result.astype(bf16).reshape(latents.shape)
    grad_three = out_grad.reshape(-1, model_width).astype(jnp.float32)
    grad_branch = grad_three.astype(bf16)
    grad_down = rows_inner(hidden, grad_branch)
    grad_bias_down = jnp.sum(grad_branch.astype(jnp.float32), axis=0)
    grad_upper = gelu_back(times_transposed(grad_branch, full_down))[0].astype(bf16)
    grad_up = rows_inner(feed_low, grad_upper)
    grad_bias_up = jnp.sum(grad_upper.astype(jnp.float32), axis=0)
    grad_feed, grad_gain_feed, grad_shift_feed = norm_backward(
        times_transposed(grad_upper, up_columns),
        feed_normed,
        feed_inverse,
        gain_feed,
    )
    grad_two = grad_three + grad_feed
    (
        self_normed,
        self_inverse,
        self_low,
        self_queries,
        self_keys,
        self_values,
        self_mixed,
        self_top,
        self_total,
    ) = forward_saved
    grad_self_branch = grad_two.astype(bf16)
    grad_self_out = rows_inner(self_mixed, grad_self_branch)
    grad_self_mix = times_transposed(grad_self_branch, self_columns[:, 3 * model_width :]).astype(
        bf16
    )
    grad_query_heads, grad_key_heads, grad_value_heads = attend_backward(
        to_heads(grad_self_mix, images, HEADS),
        self_queries,
        self_keys,
        self_values,
        None,
        self_top,
        self_total,
    )
    grad_triple = jnp.concatenate(
        [
            grad_query_heads.reshape(-1, model_width),
            grad_key_heads.reshape(-1, model_width),
            grad_value_heads.reshape(-1, model_width),
        ],
        axis=1,
    ).astype(bf16)
    grad_self_in = rows_inner(self_low, grad_triple)
    grad_first, grad_gain_self, grad_shift_self = norm_backward(
        times_transposed(grad_triple, self_columns[:, : 3 * model_width]),
        self_normed,
        self_inverse,
        gain_self,
    )
    grad_one = grad_two + grad_first
    grad_cross_branch = grad_one.astype(bf16)
    grad_cross_out = rows_inner(cross_mixed, grad_cross_branch)
    grad_cross_mix = times_transposed(
        grad_cross_branch, cross_columns[:, 3 * model_width :]
    ).astype(bf16)
    cross_query_grad, cross_key_grad, cross_value_grad = attend_backward(
        to_heads(grad_cross_mix, images, HEADS),
        query_heads,
        key_heads,
        value_heads,
        visible_mask,
        cross_top,
        cross_total,
    )
    grad_queries = cross_query_grad.reshape(-1, model_width).astype(bf16)
    grad_pair = jnp.concatenate(
        [cross_key_grad.reshape(-1, model_width), cross_value_grad.reshape(-1, model_width)], axis=1
    ).astype(bf16)
    grad_cross_query = rows_inner(cross_low, grad_queries)
    grad_cross_pair = rows_inner(pixel_low, grad_pair)
    grad_input_norm, grad_gain_cross, grad_shift_cross = norm_backward(
        times_transposed(grad_queries, cross_columns[:, :model_width]),
        cross_normed,
        cross_inverse,
        gain_cross,
    )
    pixel_unused, grad_gain_pixel, grad_shift_pixel = norm_backward(
        times_transposed(grad_pair, cross_columns[:, model_width : 3 * model_width]),
        pixel_normed,
        pixel_inverse,
        gain_pixel,
    )
    latents_grad = (grad_one + grad_input_norm).reshape(latents.shape)
    vector_grad = jnp.concatenate(
        [
            grad_gain_pixel,
            grad_shift_pixel,
            grad_gain_cross,
            grad_shift_cross,
            grad_gain_self,
            grad_shift_self,
            grad_gain_feed,
            grad_shift_feed,
            grad_bias_down,
            grad_bias_up,
        ]
    )
    pieces = [
        grad_cross_query,
        grad_cross_pair,
        grad_cross_out,
        grad_self_in,
        grad_self_out,
        grad_up,
    ]
    panel_share, down_share, vector_share, squares = reduce(
        pieces, grad_down, vector_grad, vectors.shape[0]
    )
    grad_norm = jnp.sqrt(squares)
    device_total = lax.axis_size(("dp", "fsdp"))
    token_total = images * latent_count * device_total
    param_total = (
        model_width * panel.shape[1] + full_down.shape[0] * model_width + full_vector.shape[0]
    )
    threshold = clip_coeff * (token_total * param_total) ** 0.5
    factor = threshold / jnp.maximum(grad_norm, threshold)
    panel_after, panel_moment_after, panel_square_after = adam_update(
        panel, panel_moment, panel_square, panel_share * factor, rate_matrix, weight_decay
    )
    down_after, down_moment_after, down_square_after = adam_update(
        down, down_moment, down_square, down_share * factor, rate_matrix, weight_decay
    )
    vectors_after, vector_moment_after, vector_square_after = adam_update(
        vectors, vector_moment, vector_square, vector_share * factor, rate_vector, 0.0
    )
    return (
        latents_out,
        latents_grad,
        grad_norm,
        panel_after,
        panel_moment_after,
        panel_square_after,
        down_after,
        down_moment_after,
        down_square_after,
        vectors_after,
        vector_moment_after,
        vector_square_after,
    )


def solution(mesh):
    placed = (
        P(("dp", "fsdp"), None, None),
        P(("dp", "fsdp"), None, None),
        P(("dp", "fsdp")),
        P(("dp", "fsdp"), None, None),
        P(("dp", "fsdp"), None),
        P(("dp", "fsdp"), None),
        P(("dp", "fsdp"), None),
        P(("dp", "fsdp"), None),
        P(("dp", "fsdp"), None),
        P(("dp", "fsdp"), None),
        P(("dp", "fsdp")),
        P(("dp", "fsdp")),
        P(("dp", "fsdp")),
    )
    fast = (mesh.shape["dp"], mesh.shape["fsdp"]) == (LONG * SHORT * SHORT, SHORT)
    step = functools.partial(
        shards, fast_gather if fast else slow_gather, fast_reduce if fast else slow_reduce
    )
    return jax.shard_map(
        step,
        mesh=mesh,
        in_specs=placed,
        out_specs=(
            P(("dp", "fsdp"), None, None),
            P(("dp", "fsdp"), None, None),
            P(),
            P(("dp", "fsdp"), None),
            P(("dp", "fsdp"), None),
            P(("dp", "fsdp"), None),
            P(("dp", "fsdp"), None),
            P(("dp", "fsdp"), None),
            P(("dp", "fsdp"), None),
            P(("dp", "fsdp")),
            P(("dp", "fsdp")),
            P(("dp", "fsdp")),
        ),
        check_vma=False,
    )
```

```python
import functools

import jax
import jax.numpy as jnp
from jax import lax
from jax.experimental import pallas as pl
from jax.experimental.pallas import tpu as pltpu
from jax.sharding import PartitionSpec as P

HEADS = 8
STEP = 10


norm_eps = 1e-05
beta_first = 0.9
beta_second = 0.999
adam_eps = 1e-08
rate_matrix = 0.05
rate_vector = 0.5
weight_decay = 0.1
clip_coeff = 0.01
masked_fill = -1e30


def matmul_low(left, right):
    return jnp.dot(left, right, preferred_element_type=jnp.float32)


def rows_inner(left, right):
    return lax.dot_general(
        left, right, (((0,), (0,)), ((), ())), preferred_element_type=jnp.float32
    )


def times_transposed(left, right):
    return lax.dot_general(
        left, right, (((1,), (1,)), ((), ())), preferred_element_type=jnp.float32
    )


def gelu_exact(values):
    return jax.nn.gelu(values, approximate=False)


def norm_forward(values, gain_row, shift_row):
    centre = values - jnp.mean(values, axis=-1, keepdims=True)
    inverse = lax.rsqrt(jnp.mean(centre * centre, axis=-1, keepdims=True) + norm_eps)
    normed = centre * inverse
    return (normed * gain_row + shift_row, normed, inverse)


def norm_backward(grad_out, normed, inverse, gain_row):
    grad_normed = grad_out * gain_row
    grad_values = inverse * (
        grad_normed
        - jnp.mean(grad_normed, axis=-1, keepdims=True)
        - normed * jnp.mean(grad_normed * normed, axis=-1, keepdims=True)
    )
    return (grad_values, jnp.sum(grad_out * normed, axis=0), jnp.sum(grad_out, axis=0))


def to_heads(rows, images, head_count):
    return rows.reshape(images, -1, head_count, rows.shape[1] // head_count)


def masked_scores(queries, key_rows, visible_mask):
    score_scale = queries.shape[-1] ** (-0.5)
    scores = (
        jnp.einsum("bqhd,bkhd->bhqk", queries, key_rows, preferred_element_type=jnp.float32)
        * score_scale
    )
    if visible_mask is not None:
        scores = jnp.where(visible_mask[:, None, None, :], scores, masked_fill)
    return scores


def attend_forward(queries, key_rows, value_rows, visible_mask):
    scores = masked_scores(queries, key_rows, visible_mask)
    row_top = jnp.max(scores, axis=-1, keepdims=True)
    powers = jnp.exp(scores - row_top)
    row_total = jnp.sum(powers, axis=-1, keepdims=True)
    probability = (powers / row_total).astype(jnp.bfloat16)
    mixture = jnp.einsum(
        "bhqk,bkhd->bqhd", probability, value_rows, preferred_element_type=jnp.float32
    )
    return (mixture.astype(jnp.bfloat16), row_top, row_total)


def attend_backward(grad_mix, queries, key_rows, value_rows, visible_mask, row_top, row_total):
    score_scale = queries.shape[-1] ** (-0.5)
    scores = masked_scores(queries, key_rows, visible_mask)
    probability = jnp.exp(scores - row_top) / row_total
    grad_prob = jnp.einsum(
        "bqhd,bkhd->bhqk", grad_mix, value_rows, preferred_element_type=jnp.float32
    )
    inner_sum = jnp.sum(grad_prob * probability, axis=-1, keepdims=True)
    grad_scores = (probability * (grad_prob - inner_sum)).astype(jnp.bfloat16)
    grad_queries = (
        jnp.einsum("bhqk,bkhd->bqhd", grad_scores, key_rows, preferred_element_type=jnp.float32)
        * score_scale
    )
    grad_keys = (
        jnp.einsum("bhqk,bqhd->bkhd", grad_scores, queries, preferred_element_type=jnp.float32)
        * score_scale
    )
    grad_values = jnp.einsum(
        "bhqk,bqhd->bkhd",
        probability.astype(jnp.bfloat16),
        grad_mix,
        preferred_element_type=jnp.float32,
    )
    return (grad_queries, grad_keys, grad_values)


def vector_slot(vector_float, index, model_width):
    return vector_float[index * model_width : (index + 1) * model_width]


def self_forward(first_sum, self_columns, gain_self, shift_self, images):
    model_width = first_sum.shape[1]
    normed_out, normed, inverse = norm_forward(first_sum, gain_self, shift_self)
    self_low = normed_out.astype(jnp.bfloat16)
    triple = matmul_low(self_low, self_columns[:, : 3 * model_width]).astype(jnp.bfloat16)
    self_queries = to_heads(triple[:, :model_width], images, HEADS)
    self_keys = to_heads(triple[:, model_width : 2 * model_width], images, HEADS)
    self_values = to_heads(triple[:, 2 * model_width :], images, HEADS)
    mixture, row_top, row_total = attend_forward(self_queries, self_keys, self_values, None)
    self_mixed = mixture.reshape(-1, model_width)
    return (
        normed,
        inverse,
        self_low,
        self_queries,
        self_keys,
        self_values,
        self_mixed,
        row_top,
        row_total,
    )


def adam_update(weight, moment, square, grad, rate, decay):
    moment_after = beta_first * moment + (1.0 - beta_first) * grad
    square_after = beta_second * square + (1.0 - beta_second) * grad * grad
    step_count = STEP
    fixed_moment = moment_after / (1.0 - beta_first**step_count)
    fixed_square = square_after / (1.0 - beta_second**step_count)
    weight_after = weight - rate * (
        fixed_moment / (jnp.sqrt(fixed_square) + adam_eps) + decay * weight
    )
    return (weight_after, moment_after, square_after)


MESH = pl.DeviceIdType.MESH
LONG, SHORT = 4, 2
CUT = (LONG, SHORT, SHORT, SHORT)
VMEM_LIMIT = 60 * 1024 * 1024


class Place:
    def __init__(self):
        row, self.y = lax.axis_index("dp"), lax.axis_index("fsdp")
        self.z, self.x, self.core = row // 4, (row // 2) % 2, row % 2
        even = self.core == 0
        x, y = self.x, self.y
        self.near = (jnp.where(even, 1 - x, x), jnp.where(even, y, 1 - y))
        self.far = (jnp.where(even, x, 1 - x), jnp.where(even, 1 - y, y))
        self.first, self.second = jnp.where(even, x, y), jnp.where(even, y, x)
        self.near_device = self.device(self.z, self.near[0], self.core, self.near[1])
        self.far_device = self.device(self.z, self.far[0], self.core, self.far[1])
        self.twin_device = self.device(self.z, x, 1 - self.core, y)
        self.up_device = self.device(self.z + 1, x, self.core, y)
        self.down_device = self.device(self.z - 1, x, self.core, y)

    def device(self, z, x, core, y):
        return (z * 4 + x * 2 + core, y)

    def along(self, step):
        return self.device((self.z + step) % LONG, self.x, self.core, self.y)

    def greet(self, everyone_along=False):
        barrier = pltpu.get_barrier_semaphore()

        def signal(partner):
            pl.semaphore_signal(barrier, inc=1, device_id=partner, device_id_type=MESH)

        for partner in (self.near_device, self.far_device, self.twin_device):
            signal(partner)
        if everyone_along:
            for step in range(1, LONG):
                signal(self.along(step))
            pl.semaphore_wait(barrier, 3 + LONG - 1)
            return
        pl.when(self.z < LONG - 1)(lambda: signal(self.up_device))
        pl.when(self.z > 0)(lambda: signal(self.down_device))
        at_end = jnp.logical_or(self.z == 0, self.z == LONG - 1)
        pl.semaphore_wait(barrier, 3 + jnp.where(at_end, 1, 2))


def remote(source, target, send, receive, device):
    return pltpu.make_async_remote_copy(
        src_ref=source,
        dst_ref=target,
        send_sem=send,
        recv_sem=receive,
        device_id=device,
        device_id_type=MESH,
    )


GATHER_KINDS = 4 * (LONG - 1) + 4 + 1 + 2
GATHER_STAGES = 6


class Gather:
    def __init__(self, here, chunks, send, receive):
        self.here, self.chunks, self.send, self.receive = here, chunks, send, receive
        self.count = len(chunks)
        self.sets = ((here.x, here.y), here.near, here.far, (1 - here.x, 1 - here.y))

    def line_first(self, n):
        return n % 3 == 0

    def block(self, n, which, z=slice(None)):
        x, y = self.sets[which]
        return self.chunks[n].at[z, x, self.here.core, y]

    def copy(self, n, kind, block, device):
        return remote(block, block, self.send.at[n, kind], self.receive.at[n, kind], device)

    def hop(self, n, step, action):
        here, z = self.here, self.here.z
        for piece in (0,) if self.line_first(n) else (0, 1):
            kind = 6 * piece + 2 * (step - 1)

            def upward(origin, device):
                return self.copy(n, kind, self.block(n, piece, origin), device)

            def downward(origin, device):
                return self.copy(n, kind + 1, self.block(n, piece, origin), device)

            if action == "receive":

                @pl.when(z - step >= 0)
                def _():
                    upward(z - step, here.down_device).wait_recv()

                @pl.when(z + step <= LONG - 1)
                def _():
                    downward(z + step, here.up_device).wait_recv()

            else:

                @pl.when(jnp.logical_and(z - step + 1 >= 0, z < LONG - 1))
                def _():
                    copy = upward(z - step + 1, here.up_device)
                    copy.start() if action == "start" else copy.wait_send()

                @pl.when(jnp.logical_and(z + step - 1 <= LONG - 1, z > 0))
                def _():
                    copy = downward(z + step - 1, here.down_device)
                    copy.start() if action == "start" else copy.wait_send()

    def twin(self, n, which):
        return self.copy(n, 12 + which, self.block(n, which), self.here.twin_device)

    def twin_back(self, n, which):
        x, y = self.sets[(0, 2, 1, 3)[which]]
        block = self.chunks[n].at[:, x, 1 - self.here.core, y]
        return self.copy(n, 12 + which, block, self.here.twin_device)

    def near(self, n, which):
        z = slice(None) if self.line_first(n) else self.here.z
        return self.copy(n, 16, self.block(n, which, z), self.here.near_device)

    def far(self, n, which, back=False):
        return self.copy(
            n, 17 + which, self.block(n, which + 2 * back), self.here.far_device
        )

    def stage(self, n, step):
        if not 0 <= n < self.count:
            return
        if step == 5:
            for which in range(2):
                self.far(n, which, True).wait_recv()
                self.twin(n, 2 + which).start()
        elif self.line_first(n):
            if step in (1, 2, 3):
                self.hop(n, step, "receive")
            if step < 3:
                self.hop(n, step + 1, "start")
            elif step == 3:
                self.near(n, 0).start()
                self.far(n, 0).start()
                self.twin(n, 0).start()
            else:
                self.near(n, 1).wait_recv()
                self.far(n, 1).start()
                self.twin(n, 1).start()
        elif step == 0:
            self.near(n, 0).start()
        else:
            if step == 1:
                self.near(n, 1).wait_recv()
            else:
                self.hop(n, step - 1, "receive")
            if step < 4:
                self.hop(n, step, "start")
            else:
                for which in range(2):
                    self.far(n, which).start()
                    self.twin(n, which).start()

    def whole(self, n):
        for which in range(4):
            self.twin_back(n, which).wait_recv()

    def finish(self):
        for n in range(self.count):
            for step in range(1, LONG):
                self.hop(n, step, "sent")
            self.near(n, 0).wait_send()
            for which in range(2):
                self.far(n, which).wait_send()
            for which in range(4):
                self.twin(n, which).wait_send()


def gather_kernel(widths, *refs):
    count = len(widths)
    shares, wholes = refs[:count], refs[count : 2 * count]
    send, receive, own, *lows = refs[2 * count :]
    here = Place()
    chunks, keep = [], []
    for n, (share, whole, low, width) in enumerate(zip(shares, wholes, lows, widths)):
        low[...] = share[...].astype(low.dtype)
        keep.append(pltpu.make_async_copy(low, whole.at[here.z, here.x, here.core, here.y], own.at[n]))
        keep[-1].start()
        for start in range(0, share.shape[1], width):
            chunks.append(whole.at[:, :, :, :, :, pl.ds(start, width)])
    gather = Gather(here, chunks, send, receive)
    here.greet()
    for copy in keep:
        copy.wait()
    for tick in range(len(chunks) + GATHER_STAGES - 1):
        for step in range(GATHER_STAGES):
            gather.stage(tick - step, step)
    for n in range(len(chunks)):
        gather.whole(n)
    gather.finish()


def gather_all(shares, widths, types):
    chunks = sum(share.shape[1] // width for share, width in zip(shares, widths))
    return pl.pallas_call(
        functools.partial(gather_kernel, tuple(widths)),
        out_shape=[
            jax.ShapeDtypeStruct(CUT + share.shape, dtype) for share, dtype in zip(shares, types)
        ],
        in_specs=[pl.BlockSpec(memory_space=pltpu.VMEM)] * len(shares),
        out_specs=[pl.BlockSpec(memory_space=pl.ANY)] * len(shares),
        scratch_shapes=[
            pltpu.SemaphoreType.DMA((chunks, GATHER_KINDS)),
            pltpu.SemaphoreType.DMA((chunks, GATHER_KINDS)),
            pltpu.SemaphoreType.DMA((len(shares),)),
        ]
        + [pltpu.VMEM(share.shape, dtype) for share, dtype in zip(shares, types)],
        compiler_params=pltpu.CompilerParams(
            collective_id=0, has_side_effects=True, vmem_limit_bytes=VMEM_LIMIT
        ),
    )(*shares)


REDUCE_KINDS = 4 + 1 + 1 + 3
LOADS = 3


def reduce_kernel(widths, kinds, *refs):
    count = len(widths)
    grads, shares, squares = refs[:count], refs[count : 2 * count], refs[2 * count]
    scratch = refs[2 * count + 1 :]
    families = max(kinds) + 1
    stores = [scratch[5 * k : 5 * k + 5] for k in range(families)]
    total_ref, meet, send, receive, loaded, meet_send, meet_receive = scratch[5 * families :]
    here = Place()
    z, x, core, y = here.z, here.x, here.core, here.y
    first, second = here.first, here.second
    near, far, twin = here.near_device, here.far_device, here.twin_device
    here.greet(True)
    chunks, used = [], [0] * families
    for grad, share, width, kind in zip(grads, shares, widths, kinds):
        for start_at in range(0, grad.shape[5], width):
            chunks.append((grad, share, start_at, width, stores[kind], used[kind]))
            used[kind] += 1

    def spot(side, one, two):
        return jnp.where(side == 0, one, two), jnp.where(side == 0, two, one)

    def load_copies(n):
        grad, _, start_at, width, store, slot = chunks[n]
        part = grad.at[:, :, :, :, :, pl.ds(start_at, width)]
        copies = []
        for k in range(4):
            to_x, to_y = spot(core, k // 2, k % 2)
            copies.append(
                pltpu.make_async_copy(
                    part.at[:, to_x, core, to_y],
                    store[0].at[slot % LOADS, :, k // 2, k % 2],
                    loaded.at[n, k],
                )
            )
        return copies

    def twin_copies(n):
        grad, _, start_at, width, store, slot = chunks[n]
        part = grad.at[:, :, :, :, :, pl.ds(start_at, width)]
        copies = []
        for k in range(4):
            to_x, to_y = spot(1 - core, k // 2, k % 2)
            copies.append(
                remote(
                    part.at[:, to_x, 1 - core, to_y],
                    store[1].at[slot, :, k // 2, k % 2],
                    send.at[n, k],
                    receive.at[n, k],
                    twin,
                )
            )
        return copies

    def far_copy(n):
        store, slot = chunks[n][4:]
        return remote(
            store[1].at[slot, :, :, 1 - second],
            store[2].at[slot],
            send.at[n, 4],
            receive.at[n, 4],
            far,
        )

    def near_copy(n):
        store, slot = chunks[n][4:]
        return remote(
            store[2].at[slot, :, 1 - first],
            store[3].at[slot],
            send.at[n, 5],
            receive.at[n, 5],
            near,
        )

    def long_copies(n):
        store, slot = chunks[n][4:]
        return [
            remote(
                store[3].at[slot, (z + step) % LONG],
                store[4].at[slot, step - 1],
                send.at[n, 5 + step],
                receive.at[n, 5 + step],
                here.along(step),
            )
            for step in range(1, LONG)
        ]

    def add_up(target, source):
        target[...] = (target[...].astype(jnp.float32) + source[...].astype(jnp.float32)).astype(
            target.dtype
        )

    def begin(n):
        for copy in load_copies(n) + twin_copies(n):
            copy.start()

    def stage_twin(n):
        store, slot = chunks[n][4:]
        for copy in load_copies(n):
            copy.wait()
        for copy in twin_copies(n):
            copy.wait_recv()

        def one(at, carry):
            a, b, c = at // 4, (at // 2) % 2, at % 2
            add_up(store[1].at[slot, a, b, c], store[0].at[slot % LOADS, a, b, c])
            return carry

        lax.fori_loop(0, 16, one, 0)
        far_copy(n).start()

    def stage_far(n):
        store, slot = chunks[n][4:]
        far_copy(n).wait_recv()

        def one(at, carry):
            a, b = at // 2, at % 2
            add_up(store[2].at[slot, a, b], store[1].at[slot, a, b, second])
            return carry

        lax.fori_loop(0, 8, one, 0)
        near_copy(n).start()

    def stage_near(n):
        store, slot = chunks[n][4:]
        near_copy(n).wait_recv()

        def one(at, carry):
            add_up(store[3].at[slot, at], store[2].at[slot, at, first])
            return carry

        lax.fori_loop(0, 4, one, 0)
        for copy in long_copies(n):
            copy.start()

    def stage_long(n):
        _, share, start_at, width, store, slot = chunks[n]
        for copy in long_copies(n):
            copy.wait_recv()
        rows = share.shape[0]
        step_rows = min(rows, 32)

        def one(at, carry):
            lines = pl.ds(pl.multiple_of(at * step_rows, step_rows), step_rows)
            value = store[3][slot, z, lines, :].astype(jnp.float32)
            for step in range(LONG - 1):
                value = value + store[4][slot, step, lines, :].astype(jnp.float32)
            share[lines, pl.ds(start_at, width)] = value
            square = value * value
            gained = total_ref[...]
            for down_at in range(0, step_rows, 8):
                for across in range(0, width, 128):
                    gained = gained + square[down_at : down_at + 8, across : across + 128]
            total_ref[...] = gained
            return carry

        lax.fori_loop(0, rows // step_rows, one, 0)

    total_ref[...] = jnp.zeros_like(total_ref)
    total = len(chunks)
    for n in range(min(2, total)):
        begin(n)
    for tick in range(total + 3):
        if tick + 2 < total:
            begin(tick + 2)
        if tick < total:
            stage_twin(tick)
        if 0 <= tick - 1 < total:
            stage_far(tick - 1)
        if 0 <= tick - 2 < total:
            stage_near(tick - 2)
        if 0 <= tick - 3 < total:
            stage_long(tick - 3)
    for n in range(total):
        for copy in twin_copies(n) + [far_copy(n), near_copy(n)] + long_copies(n):
            copy.wait_send()

    meet[z] = total_ref[...]
    copies = [
        remote(
            total_ref,
            meet.at[z],
            meet_send.at[step - 1],
            meet_receive.at[step - 1],
            here.along(step),
        )
        for step in range(1, LONG)
    ]
    for copy in copies:
        copy.start()
    for copy in copies:
        copy.wait()
    value = meet[0] + meet[1] + meet[2] + meet[3]
    for k, partner in enumerate((near, far, twin)):
        meet[4 + 2 * k] = value
        copy = remote(
            meet.at[4 + 2 * k],
            meet.at[5 + 2 * k],
            meet_send.at[3 + k],
            meet_receive.at[3 + k],
            partner,
        )
        copy.start()
        copy.wait()
        value = value + meet[5 + 2 * k]
    squares[...] = value


def reduce_all(grads, widths, kinds):
    counts = [0] * (max(kinds) + 1)
    shapes = [None] * len(counts)
    for grad, width, kind in zip(grads, widths, kinds):
        counts[kind] += grad.shape[5] // width
        shapes[kind] = ((grad.shape[4], width), grad.dtype)
    scratch = []
    for number, (shape, dtype) in zip(counts, shapes):
        scratch += [
            pltpu.VMEM((LOADS, LONG, SHORT, SHORT) + shape, dtype),
            pltpu.VMEM((number, LONG, SHORT, SHORT) + shape, dtype),
            pltpu.VMEM((number, LONG, SHORT) + shape, dtype),
            pltpu.VMEM((number, LONG) + shape, dtype),
            pltpu.VMEM((number, LONG - 1) + shape, dtype),
        ]
    chunks = sum(counts)
    return pl.pallas_call(
        functools.partial(reduce_kernel, tuple(widths), tuple(kinds)),
        out_shape=[jax.ShapeDtypeStruct(grad.shape[4:], jnp.float32) for grad in grads]
        + [jax.ShapeDtypeStruct((8, 128), jnp.float32)],
        in_specs=[pl.BlockSpec(memory_space=pl.ANY)] * len(grads),
        out_specs=[pl.BlockSpec(memory_space=pltpu.VMEM)] * (len(grads) + 1),
        scratch_shapes=scratch
        + [
            pltpu.VMEM((8, 128), jnp.float32),
            pltpu.VMEM((10, 8, 128), jnp.float32),
            pltpu.SemaphoreType.DMA((chunks, REDUCE_KINDS)),
            pltpu.SemaphoreType.DMA((chunks, REDUCE_KINDS)),
            pltpu.SemaphoreType.DMA((chunks, 4)),
            pltpu.SemaphoreType.DMA((6,)),
            pltpu.SemaphoreType.DMA((6,)),
        ],
        compiler_params=pltpu.CompilerParams(
            collective_id=1, has_side_effects=True, vmem_limit_bytes=VMEM_LIMIT
        ),
    )(*grads)


VECTOR_TILE = (8, 128)


def packed(rows):
    spare = VECTOR_TILE[0] * VECTOR_TILE[1] - rows.shape[-1]
    return jnp.pad(rows, ((0, 0), (0, spare))).reshape((-1,) + VECTOR_TILE)


def fast_gather(panel, down, vectors):
    model_width = panel.shape[1] // 12
    bf16 = jnp.bfloat16
    shares = [packed(vectors[None])[0]]
    shares += [panel[:, k * 4 * model_width : (k + 1) * 4 * model_width] for k in range(3)]
    shares += [down]
    vector_tiles, *wholes = gather_all(
        shares,
        [128] + [model_width] * 3 + [down.shape[1] // 4],
        [jnp.float32] + [bf16] * 4,
    )
    full_vector = vector_tiles.reshape(-1, VECTOR_TILE[0] * VECTOR_TILE[1])
    full_vector = full_vector[:, : vectors.shape[0]].reshape(-1)
    cross, self_columns, up = [whole.reshape(-1, whole.shape[5]) for whole in wholes[:3]]
    return cross, self_columns, up, wholes[3].reshape(-1, down.shape[1]), full_vector.astype(bf16)


def slow_gather(panel, down, vectors):
    model_width = panel.shape[1] // 12
    bf16 = jnp.bfloat16
    parts = [panel[:, k * 4 * model_width : (k + 1) * 4 * model_width].astype(bf16) for k in range(3)]
    parts += [down.astype(bf16), vectors.astype(bf16)]
    return [lax.all_gather(part, ("dp", "fsdp"), axis=0, tiled=True) for part in parts]


def cut(grad):
    return grad.reshape(CUT + (-1, grad.shape[1]))


def fast_reduce(pieces, down_grad, vector_grad, share_length):
    bf16 = jnp.bfloat16
    model_width = down_grad.shape[1]
    ordered = [pieces[k] for k in (5, 4, 3, 2, 1, 0)]
    grads = [cut(down_grad.astype(bf16))] + [cut(piece.astype(bf16)) for piece in ordered]
    grads.append(packed(vector_grad.reshape(-1, share_length)).reshape(CUT + VECTOR_TILE))
    widths = [model_width // 4] + [model_width] * len(pieces) + [128]
    kinds = [0] + [1] * len(pieces) + [2]
    *shares, squares = reduce_all(grads, widths, kinds)
    panel_share = jnp.concatenate([shares[k] for k in (6, 5, 4, 3, 2, 1)], axis=1)
    return panel_share, shares[0], shares[7].reshape(-1)[:share_length], jnp.sum(squares)


def slow_reduce(pieces, down_grad, vector_grad, share_length):
    shares = [
        lax.psum_scatter(grad, ("dp", "fsdp"), scatter_dimension=0, tiled=True)
        for grad in (jnp.concatenate(pieces, axis=1), down_grad, vector_grad)
    ]
    squares = lax.psum(sum(jnp.sum(share * share) for share in shares), ("dp", "fsdp"))
    return (*shares, squares)


def shards(
    gather,
    reduce,
    latents,
    pixels,
    visible,
    out_grad,
    panel,
    panel_moment,
    panel_square,
    down,
    down_moment,
    down_square,
    vectors,
    vector_moment,
    vector_square,
):
    images, latent_count, model_width = latents.shape
    pixel_count = pixels.shape[1]
    bf16 = jnp.bfloat16
    cross_columns, self_columns, up_columns, full_down, full_vector = gather(panel, down, vectors)
    vector_float = full_vector.astype(jnp.float32)
    gain_pixel = vector_slot(vector_float, 0, model_width)
    shift_pixel = vector_slot(vector_float, 1, model_width)
    gain_cross = vector_slot(vector_float, 2, model_width)
    shift_cross = vector_slot(vector_float, 3, model_width)
    gain_self = vector_slot(vector_float, 4, model_width)
    shift_self = vector_slot(vector_float, 5, model_width)
    gain_feed = vector_slot(vector_float, 6, model_width)
    shift_feed = vector_slot(vector_float, 7, model_width)
    bias_down = vector_slot(vector_float, 8, model_width)
    bias_up = vector_float[9 * model_width :]
    latent_rows = latents.reshape(-1, model_width).astype(jnp.float32)
    pixel_rows = pixels.reshape(-1, model_width).astype(jnp.float32)
    pixel_out, pixel_normed, pixel_inverse = norm_forward(pixel_rows, gain_pixel, shift_pixel)
    pixel_low = pixel_out.astype(bf16)
    cross_out, cross_normed, cross_inverse = norm_forward(latent_rows, gain_cross, shift_cross)
    cross_low = cross_out.astype(bf16)
    cross_queries = matmul_low(cross_low, cross_columns[:, :model_width]).astype(bf16)
    pair_rows = matmul_low(pixel_low, cross_columns[:, model_width : 3 * model_width]).astype(bf16)
    visible_mask = jnp.arange(pixel_count, dtype=jnp.int32)[None, :] < visible[:, None]
    query_heads = to_heads(cross_queries, images, HEADS)
    key_heads = to_heads(pair_rows[:, :model_width], images, HEADS)
    value_heads = to_heads(pair_rows[:, model_width:], images, HEADS)
    cross_mix, cross_top, cross_total = attend_forward(
        query_heads, key_heads, value_heads, visible_mask
    )
    cross_mixed = cross_mix.reshape(-1, model_width)
    first_sum = latent_rows + matmul_low(
        cross_mixed, cross_columns[:, 3 * model_width :]
    )
    forward_saved = self_forward(first_sum, self_columns, gain_self, shift_self, images)
    second_sum = first_sum + matmul_low(forward_saved[6], self_columns[:, 3 * model_width :])
    feed_out, feed_normed, feed_inverse = norm_forward(second_sum, gain_feed, shift_feed)
    feed_low = feed_out.astype(bf16)
    upper_in = matmul_low(feed_low, up_columns) + bias_up
    hidden_float, gelu_back = jax.vjp(gelu_exact, upper_in)
    hidden = hidden_float.astype(bf16)
    result = second_sum + (matmul_low(hidden, full_down) + bias_down)
    latents_out = result.astype(bf16).reshape(latents.shape)
    grad_three = out_grad.reshape(-1, model_width).astype(jnp.float32)
    grad_branch = grad_three.astype(bf16)
    grad_down = rows_inner(hidden, grad_branch)
    grad_bias_down = jnp.sum(grad_branch.astype(jnp.float32), axis=0)
    grad_upper = gelu_back(times_transposed(grad_branch, full_down))[0].astype(bf16)
    grad_up = rows_inner(feed_low, grad_upper)
    grad_bias_up = jnp.sum(grad_upper.astype(jnp.float32), axis=0)
    grad_feed, grad_gain_feed, grad_shift_feed = norm_backward(
        times_transposed(grad_upper, up_columns),
        feed_normed,
        feed_inverse,
        gain_feed,
    )
    grad_two = grad_three + grad_feed
    (
        self_normed,
        self_inverse,
        self_low,
        self_queries,
        self_keys,
        self_values,
        self_mixed,
        self_top,
        self_total,
    ) = forward_saved
    grad_self_branch = grad_two.astype(bf16)
    grad_self_out = rows_inner(self_mixed, grad_self_branch)
    grad_self_mix = times_transposed(grad_self_branch, self_columns[:, 3 * model_width :]).astype(
        bf16
    )
    grad_query_heads, grad_key_heads, grad_value_heads = attend_backward(
        to_heads(grad_self_mix, images, HEADS),
        self_queries,
        self_keys,
        self_values,
        None,
        self_top,
        self_total,
    )
    grad_triple = jnp.concatenate(
        [
            grad_query_heads.reshape(-1, model_width),
            grad_key_heads.reshape(-1, model_width),
            grad_value_heads.reshape(-1, model_width),
        ],
        axis=1,
    ).astype(bf16)
    grad_self_in = rows_inner(self_low, grad_triple)
    grad_first, grad_gain_self, grad_shift_self = norm_backward(
        times_transposed(grad_triple, self_columns[:, : 3 * model_width]),
        self_normed,
        self_inverse,
        gain_self,
    )
    grad_one = grad_two + grad_first
    grad_cross_branch = grad_one.astype(bf16)
    grad_cross_out = rows_inner(cross_mixed, grad_cross_branch)
    grad_cross_mix = times_transposed(
        grad_cross_branch, cross_columns[:, 3 * model_width :]
    ).astype(bf16)
    cross_query_grad, cross_key_grad, cross_value_grad = attend_backward(
        to_heads(grad_cross_mix, images, HEADS),
        query_heads,
        key_heads,
        value_heads,
        visible_mask,
        cross_top,
        cross_total,
    )
    grad_queries = cross_query_grad.reshape(-1, model_width).astype(bf16)
    grad_pair = jnp.concatenate(
        [cross_key_grad.reshape(-1, model_width), cross_value_grad.reshape(-1, model_width)], axis=1
    ).astype(bf16)
    grad_cross_query = rows_inner(cross_low, grad_queries)
    grad_cross_pair = rows_inner(pixel_low, grad_pair)
    grad_input_norm, grad_gain_cross, grad_shift_cross = norm_backward(
        times_transposed(grad_queries, cross_columns[:, :model_width]),
        cross_normed,
        cross_inverse,
        gain_cross,
    )
    pixel_unused, grad_gain_pixel, grad_shift_pixel = norm_backward(
        times_transposed(grad_pair, cross_columns[:, model_width : 3 * model_width]),
        pixel_normed,
        pixel_inverse,
        gain_pixel,
    )
    latents_grad = (grad_one + grad_input_norm).reshape(latents.shape)
    vector_grad = jnp.concatenate(
        [
            grad_gain_pixel,
            grad_shift_pixel,
            grad_gain_cross,
            grad_shift_cross,
            grad_gain_self,
            grad_shift_self,
            grad_gain_feed,
            grad_shift_feed,
            grad_bias_down,
            grad_bias_up,
        ]
    )
    pieces = [
        grad_cross_query,
        grad_cross_pair,
        grad_cross_out,
        grad_self_in,
        grad_self_out,
        grad_up,
    ]
    panel_share, down_share, vector_share, squares = reduce(
        pieces, grad_down, vector_grad, vectors.shape[0]
    )
    grad_norm = jnp.sqrt(squares)
    device_total = lax.axis_size(("dp", "fsdp"))
    token_total = images * latent_count * device_total
    param_total = (
        model_width * panel.shape[1] + full_down.shape[0] * model_width + full_vector.shape[0]
    )
    threshold = clip_coeff * (token_total * param_total) ** 0.5
    factor = threshold / jnp.maximum(grad_norm, threshold)
    panel_after, panel_moment_after, panel_square_after = adam_update(
        panel, panel_moment, panel_square, panel_share * factor, rate_matrix, weight_decay
    )
    down_after, down_moment_after, down_square_after = adam_update(
        down, down_moment, down_square, down_share * factor, rate_matrix, weight_decay
    )
    vectors_after, vector_moment_after, vector_square_after = adam_update(
        vectors, vector_moment, vector_square, vector_share * factor, rate_vector, 0.0
    )
    return (
        latents_out,
        latents_grad,
        grad_norm,
        panel_after,
        panel_moment_after,
        panel_square_after,
        down_after,
        down_moment_after,
        down_square_after,
        vectors_after,
        vector_moment_after,
        vector_square_after,
    )


def solution(mesh):
    placed = (
        P(("dp", "fsdp"), None, None),
        P(("dp", "fsdp"), None, None),
        P(("dp", "fsdp")),
        P(("dp", "fsdp"), None, None),
        P(("dp", "fsdp"), None),
        P(("dp", "fsdp"), None),
        P(("dp", "fsdp"), None),
        P(("dp", "fsdp"), None),
        P(("dp", "fsdp"), None),
        P(("dp", "fsdp"), None),
        P(("dp", "fsdp")),
        P(("dp", "fsdp")),
        P(("dp", "fsdp")),
    )
    fast = (mesh.shape["dp"], mesh.shape["fsdp"]) == (LONG * SHORT * SHORT, SHORT)
    step = functools.partial(
        shards, fast_gather if fast else slow_gather, fast_reduce if fast else slow_reduce
    )
    return jax.shard_map(
        step,
        mesh=mesh,
        in_specs=placed,
        out_specs=(
            P(("dp", "fsdp"), None, None),
            P(("dp", "fsdp"), None, None),
            P(),
            P(("dp", "fsdp"), None),
            P(("dp", "fsdp"), None),
            P(("dp", "fsdp"), None),
            P(("dp", "fsdp"), None),
            P(("dp", "fsdp"), None),
            P(("dp", "fsdp"), None),
            P(("dp", "fsdp")),
            P(("dp", "fsdp")),
            P(("dp", "fsdp")),
        ),
        check_vma=False,
    )
```

```python
import functools
import math
import types

import jax
import jax.numpy as jnp
from jax import lax
from jax.experimental import pallas as pl
from jax.experimental.pallas import tpu as pltpu
from jax.sharding import PartitionSpec as P

HEADS = 8
STEP = 10


norm_eps = 1e-05
beta_first = 0.9
beta_second = 0.999
adam_eps = 1e-08
rate_matrix = 0.05
rate_vector = 0.5
weight_decay = 0.1
clip_coeff = 0.01
masked_fill = -1e30


def matmul_low(left, right):
    return jnp.dot(left, right, preferred_element_type=jnp.float32)


def rows_inner(left, right):
    return lax.dot_general(
        left, right, (((0,), (0,)), ((), ())), preferred_element_type=jnp.float32
    )


def times_transposed(left, right):
    return lax.dot_general(
        left, right, (((1,), (1,)), ((), ())), preferred_element_type=jnp.float32
    )


def gelu_exact(values):
    return jax.nn.gelu(values, approximate=False)


def norm_forward(values, gain_row, shift_row):
    centre = values - jnp.mean(values, axis=-1, keepdims=True)
    inverse = lax.rsqrt(jnp.mean(centre * centre, axis=-1, keepdims=True) + norm_eps)
    normed = centre * inverse
    return (normed * gain_row + shift_row, normed, inverse)


def norm_backward(grad_out, normed, inverse, gain_row):
    grad_normed = grad_out * gain_row
    grad_values = inverse * (
        grad_normed
        - jnp.mean(grad_normed, axis=-1, keepdims=True)
        - normed * jnp.mean(grad_normed * normed, axis=-1, keepdims=True)
    )
    return (grad_values, jnp.sum(grad_out * normed, axis=0), jnp.sum(grad_out, axis=0))


def to_heads(rows, images, head_count):
    return rows.reshape(images, -1, head_count, rows.shape[1] // head_count)


def masked_scores(queries, key_rows, visible_mask):
    score_scale = queries.shape[-1] ** (-0.5)
    scores = (
        jnp.einsum("bqhd,bkhd->bhqk", queries, key_rows, preferred_element_type=jnp.float32)
        * score_scale
    )
    if visible_mask is not None:
        scores = jnp.where(visible_mask[:, None, None, :], scores, masked_fill)
    return scores


def attend_forward(queries, key_rows, value_rows, visible_mask):
    scores = masked_scores(queries, key_rows, visible_mask)
    row_top = jnp.max(scores, axis=-1, keepdims=True)
    powers = jnp.exp(scores - row_top)
    row_total = jnp.sum(powers, axis=-1, keepdims=True)
    probability = (powers / row_total).astype(jnp.bfloat16)
    mixture = jnp.einsum(
        "bhqk,bkhd->bqhd", probability, value_rows, preferred_element_type=jnp.float32
    )
    return (mixture.astype(jnp.bfloat16), row_top, row_total)


def attend_backward(grad_mix, queries, key_rows, value_rows, visible_mask, row_top, row_total):
    score_scale = queries.shape[-1] ** (-0.5)
    scores = masked_scores(queries, key_rows, visible_mask)
    probability = jnp.exp(scores - row_top) / row_total
    grad_prob = jnp.einsum(
        "bqhd,bkhd->bhqk", grad_mix, value_rows, preferred_element_type=jnp.float32
    )
    inner_sum = jnp.sum(grad_prob * probability, axis=-1, keepdims=True)
    grad_scores = (probability * (grad_prob - inner_sum)).astype(jnp.bfloat16)
    grad_queries = (
        jnp.einsum("bhqk,bkhd->bqhd", grad_scores, key_rows, preferred_element_type=jnp.float32)
        * score_scale
    )
    grad_keys = (
        jnp.einsum("bhqk,bqhd->bkhd", grad_scores, queries, preferred_element_type=jnp.float32)
        * score_scale
    )
    grad_values = jnp.einsum(
        "bhqk,bqhd->bkhd",
        probability.astype(jnp.bfloat16),
        grad_mix,
        preferred_element_type=jnp.float32,
    )
    return (grad_queries, grad_keys, grad_values)


def vector_slot(vector_float, index, model_width):
    return vector_float[index * model_width : (index + 1) * model_width]


def self_forward(first_sum, self_columns, gain_self, shift_self, images):
    model_width = first_sum.shape[1]
    normed_out, normed, inverse = norm_forward(first_sum, gain_self, shift_self)
    self_low = normed_out.astype(jnp.bfloat16)
    triple = matmul_low(self_low, self_columns[:, : 3 * model_width]).astype(jnp.bfloat16)
    self_queries = to_heads(triple[:, :model_width], images, HEADS)
    self_keys = to_heads(triple[:, model_width : 2 * model_width], images, HEADS)
    self_values = to_heads(triple[:, 2 * model_width :], images, HEADS)
    mixture, row_top, row_total = attend_forward(self_queries, self_keys, self_values, None)
    self_mixed = mixture.reshape(-1, model_width)
    return (
        normed,
        inverse,
        self_low,
        self_queries,
        self_keys,
        self_values,
        self_mixed,
        row_top,
        row_total,
    )


def adam_update(weight, moment, square, grad, rate, decay):
    moment_after = beta_first * moment + (1.0 - beta_first) * grad
    square_after = beta_second * square + (1.0 - beta_second) * grad * grad
    step_count = STEP
    fixed_moment = moment_after / (1.0 - beta_first**step_count)
    fixed_square = square_after / (1.0 - beta_second**step_count)
    weight_after = weight - rate * (
        fixed_moment / (jnp.sqrt(fixed_square) + adam_eps) + decay * weight
    )
    return (weight_after, moment_after, square_after)


MESH = pl.DeviceIdType.MESH
LONG, SHORT = 4, 2
CUT = (LONG, SHORT, SHORT, SHORT)
VMEM_LIMIT = 60 * 1024 * 1024


class Place:
    def __init__(self):
        row, self.y = lax.axis_index("dp"), lax.axis_index("fsdp")
        self.z, self.x, self.core = row // 4, (row // 2) % 2, row % 2
        even = self.core == 0
        x, y = self.x, self.y
        self.near = (jnp.where(even, 1 - x, x), jnp.where(even, y, 1 - y))
        self.far = (jnp.where(even, x, 1 - x), jnp.where(even, 1 - y, y))
        self.first, self.second = jnp.where(even, x, y), jnp.where(even, y, x)
        self.near_device = self.device(self.z, self.near[0], self.core, self.near[1])
        self.far_device = self.device(self.z, self.far[0], self.core, self.far[1])
        self.twin_device = self.device(self.z, x, 1 - self.core, y)
        self.up_device = self.device(self.z + 1, x, self.core, y)
        self.down_device = self.device(self.z - 1, x, self.core, y)

    def device(self, z, x, core, y):
        return (z * 4 + x * 2 + core, y)

    def along(self, step):
        return self.device((self.z + step) % LONG, self.x, self.core, self.y)

    def greet(self, everyone_along=False):
        barrier = pltpu.get_barrier_semaphore()

        def signal(partner):
            pl.semaphore_signal(barrier, inc=1, device_id=partner, device_id_type=MESH)

        for partner in (self.near_device, self.far_device, self.twin_device):
            signal(partner)
        if everyone_along:
            for step in range(1, LONG):
                signal(self.along(step))
            pl.semaphore_wait(barrier, 3 + LONG - 1)
            return
        pl.when(self.z < LONG - 1)(lambda: signal(self.up_device))
        pl.when(self.z > 0)(lambda: signal(self.down_device))
        at_end = jnp.logical_or(self.z == 0, self.z == LONG - 1)
        pl.semaphore_wait(barrier, 3 + jnp.where(at_end, 1, 2))


def remote(source, target, send, receive, device):
    return pltpu.make_async_remote_copy(
        src_ref=source,
        dst_ref=target,
        send_sem=send,
        recv_sem=receive,
        device_id=device,
        device_id_type=MESH,
    )


GATHER_KINDS = 4 * (LONG - 1) + 4 + 1 + 2
GATHER_STAGES = 6
START, RECEIVE, SENT = range(3)


class Gather:
    def __init__(self, here, chunks, send, receive):
        self.here, self.chunks, self.send, self.receive = here, chunks, send, receive
        self.count = len(chunks)
        self.sets = ((here.x, here.y), here.near, here.far, (1 - here.x, 1 - here.y))

    def line_first(self, n):
        return n % 3 == 0

    def block(self, n, which, z=slice(None)):
        x, y = self.sets[which]
        return self.chunks[n].at[z, x, self.here.core, y]

    def copy(self, n, kind, block, device):
        return remote(block, block, self.send.at[n, kind], self.receive.at[n, kind], device)

    def hop(self, n, step, action):
        here, z = self.here, self.here.z
        for piece in (0,) if self.line_first(n) else (0, 1):
            kind = 6 * piece + 2 * (step - 1)

            def upward(origin, device):
                return self.copy(n, kind, self.block(n, piece, origin), device)

            def downward(origin, device):
                return self.copy(n, kind + 1, self.block(n, piece, origin), device)

            if action == RECEIVE:

                @pl.when(z - step >= 0)
                def _():
                    upward(z - step, here.down_device).wait_recv()

                @pl.when(z + step <= LONG - 1)
                def _():
                    downward(z + step, here.up_device).wait_recv()

            else:

                @pl.when(jnp.logical_and(z - step + 1 >= 0, z < LONG - 1))
                def _():
                    copy = upward(z - step + 1, here.up_device)
                    copy.start() if action == START else copy.wait_send()

                @pl.when(jnp.logical_and(z + step - 1 <= LONG - 1, z > 0))
                def _():
                    copy = downward(z + step - 1, here.down_device)
                    copy.start() if action == START else copy.wait_send()

    def twin(self, n, which):
        return self.copy(n, 12 + which, self.block(n, which), self.here.twin_device)

    def twin_back(self, n, which):
        x, y = self.sets[(0, 2, 1, 3)[which]]
        block = self.chunks[n].at[:, x, 1 - self.here.core, y]
        return self.copy(n, 12 + which, block, self.here.twin_device)

    def near(self, n, which):
        z = slice(None) if self.line_first(n) else self.here.z
        return self.copy(n, 16, self.block(n, which, z), self.here.near_device)

    def far(self, n, which, back=False):
        return self.copy(
            n, 17 + which, self.block(n, which + 2 * back), self.here.far_device
        )

    def stage(self, n, step):
        if not 0 <= n < self.count:
            return
        if step == 5:
            for which in range(2):
                self.far(n, which, True).wait_recv()
                self.twin(n, 2 + which).start()
        elif self.line_first(n):
            if step in (1, 2, 3):
                self.hop(n, step, RECEIVE)
            if step < 3:
                self.hop(n, step + 1, START)
            elif step == 3:
                self.near(n, 0).start()
                self.far(n, 0).start()
                self.twin(n, 0).start()
            else:
                self.near(n, 1).wait_recv()
                self.far(n, 1).start()
                self.twin(n, 1).start()
        elif step == 0:
            self.near(n, 0).start()
        else:
            if step == 1:
                self.near(n, 1).wait_recv()
            else:
                self.hop(n, step - 1, RECEIVE)
            if step < 4:
                self.hop(n, step, START)
            else:
                for which in range(2):
                    self.far(n, which).start()
                    self.twin(n, which).start()

    def whole(self, n):
        for which in range(4):
            self.twin_back(n, which).wait_recv()

    def finish(self):
        for n in range(self.count):
            for step in range(1, LONG):
                self.hop(n, step, SENT)
            self.near(n, 0).wait_send()
            for which in range(2):
                self.far(n, which).wait_send()
            for which in range(4):
                self.twin(n, which).wait_send()


REDUCE_KINDS = 1 + 1 + 2 * (LONG - 1)
REDUCE_STAGES = 6
RING = 9
STAGED = 3


class Reduce:
    def __init__(self, here, r, count, put):
        self.here, self.r, self.count, self.put = here, r, count, put

    def line_last(self, n):
        return n % 3 == 0

    def at(self, n):
        slot = n % RING
        return slot, slot // 3 if self.line_last(n) else slot // 3 * 2 + slot % 3 - 1

    def copy(self, n, kind, source, target, device):
        r = self.r
        return remote(source, target, r.reduce_send.at[n, kind], r.reduce_receive.at[n, kind], device)

    def far(self, n):
        r, here = self.r, self.here
        source = r.staged.at[n % STAGED, :, :, 1 - here.second]
        return self.copy(n, 0, source, r.from_far.at[n % RING], here.far_device)

    def near(self, n):
        r, here = self.r, self.here
        slot, index = self.at(n)
        if self.line_last(n):
            source, target = r.from_far.at[slot, :, 1 - here.first], r.from_near_line.at[index]
        else:
            source, target = r.from_far.at[slot, here.z, 1 - here.first], r.from_near.at[index]
        return self.copy(n, 1, source, target, here.near_device)

    def line(self, n, place):
        r = self.r
        slot, index = self.at(n)
        return r.from_near_line.at[index, place] if self.line_last(n) else r.from_far.at[slot, place]

    def landing(self, n, kind):
        r = self.r
        index = self.at(n)[1]
        return r.from_line_short.at[index, kind] if self.line_last(n) else r.from_line.at[index, kind]

    def hop(self, n, step, action):
        here, z, away = self.here, self.here.z, LONG - step
        kind = 2 * (step - 1)

        @pl.when(z - away >= 0)
        def _():
            copy = self.copy(
                n, 2 + kind, self.line(n, z - away), self.landing(n, kind), here.down_device
            )
            copy.start() if action == START else copy.wait_send()

        @pl.when(z + away <= LONG - 1)
        def _():
            copy = self.copy(
                n, 3 + kind, self.line(n, z + away), self.landing(n, kind + 1), here.up_device
            )
            copy.start() if action == START else copy.wait_send()

    def hop_in(self, n, step):
        here, z, away = self.here, self.here.z, LONG - step
        kind = 2 * (step - 1)
        for side, place, there, device in (
            (0, z - away + 1, jnp.logical_and(z < LONG - 1, z - away + 1 >= 0), here.up_device),
            (1, z + away - 1, jnp.logical_and(z > 0, z + away - 1 <= LONG - 1), here.down_device),
        ):

            @pl.when(there)
            def _():
                landed = self.landing(n, kind + side)
                self.copy(n, 2 + kind + side, landed, landed, device).wait_recv()
                total = self.line(n, place)
                if self.line_last(n):
                    add_up(total, landed)
                else:
                    for part in range(SHORT):
                        add_up(total.at[part], landed.at[part])

    def credit(self, n, kind, condition=None):
        if n < RING:
            return

        def take():
            pl.semaphore_wait(self.r.credit.at[n - RING, kind], 1)

        take() if condition is None else pl.when(condition)(take)

    def give(self, n):
        if n + RING >= self.count:
            return
        here, r = self.here, self.r

        def signal(kind, device):
            pl.semaphore_signal(r.credit.at[n, kind], inc=1, device_id=device, device_id_type=MESH)

        self.near(n).wait_send()
        for step in range(1, LONG):
            self.hop(n, step, SENT)
        signal(0, here.far_device)
        signal(1, here.near_device)
        pl.when(here.z < LONG - 1)(lambda: signal(2, here.up_device))
        pl.when(here.z > 0)(lambda: signal(3, here.down_device))

    def first_hop(self, n):
        self.credit(n, 3, self.here.z < LONG - 1)
        self.credit(n, 2, self.here.z > 0)
        self.hop(n, 1, START)

    def free(self, n):
        if n >= STAGED:
            self.far(n - STAGED).wait_send()

    def stage(self, n, step):
        if not 0 <= n < self.count:
            return
        r, here = self.r, self.here
        slot, index = self.at(n)
        if step == 0:
            self.credit(n, 0)
            self.far(n).start()
            return
        if step == 1:
            self.far(n).wait_recv()

            def one(at, carry):
                add_up(
                    r.from_far.at[slot, at // 2, at % 2],
                    r.staged.at[n % STAGED, at // 2, at % 2, here.second],
                )
                return carry

            lax.fori_loop(0, LONG * SHORT, one, 0)
            if self.line_last(n):
                self.credit(n, 1)
                self.near(n).start()
            else:
                self.first_hop(n)
        elif self.line_last(n):
            if step == 2:
                self.near(n).wait_recv()

                def one(at, carry):
                    add_up(r.from_near_line.at[index, at], r.from_far.at[slot, at, here.first])
                    return carry

                lax.fori_loop(0, LONG, one, 0)
                self.first_hop(n)
            else:
                self.hop_in(n, step - 2)
                if step < 5:
                    self.hop(n, step - 1, START)
                else:
                    self.put(n, r.from_near_line[index, here.z].astype(jnp.float32))
                    self.give(n)
        elif step < 5:
            self.hop_in(n, step - 1)
            if step < 4:
                self.hop(n, step, START)
            else:
                self.credit(n, 1)
                self.near(n).start()
        else:
            self.near(n).wait_recv()
            own = r.from_far[slot, here.z, here.first].astype(jnp.float32)
            self.put(n, own + r.from_near[index].astype(jnp.float32))
            self.give(n)

    def tick(self, n):
        for step in range(REDUCE_STAGES):
            self.stage(n - step, step)

    def finish(self):
        for n in range(max(0, self.count - STAGED), self.count):
            self.far(n).wait_send()
        for n in range(max(0, self.count - RING), self.count):
            self.near(n).wait_send()
            for step in range(1, LONG):
                self.hop(n, step, SENT)


def add_up(target, source):
    total = target[...].astype(jnp.float32) + source[...].astype(jnp.float32)
    target[...] = total.astype(target.dtype)


class Meeting:
    def __init__(self, here, value, line, pairs, send, receive):
        self.here, self.value, self.line, self.pairs = here, value, line, pairs
        self.send, self.receive = send, receive

    def along(self, step, back=False):
        here = self.here
        place = (here.z - step) % LONG if back else here.z
        return remote(
            self.line.at[place] if back else self.value,
            self.line.at[place],
            self.send.at[step - 1],
            self.receive.at[step - 1],
            here.along(step),
        )

    def pair(self, k):
        here = self.here
        device = (here.near_device, here.far_device, here.twin_device)[k]
        return remote(
            self.pairs.at[2 * k],
            self.pairs.at[2 * k + 1],
            self.send.at[LONG - 1 + k],
            self.receive.at[LONG - 1 + k],
            device,
        )

    def step(self, k):
        if k == 0:
            self.line[self.here.z] = self.value[...]
            for away in range(1, LONG):
                self.along(away).start()
            return None
        if k == 1:
            for away in range(1, LONG):
                self.along(away).wait_send()
                self.along(away, True).wait_recv()
            total = self.line[0]
            for place in range(1, LONG):
                total = total + self.line[place]
        else:
            self.pair(k - 2).wait()
            total = self.pairs[2 * k - 4] + self.pairs[2 * k - 3]
        if k < 4:
            self.pairs[2 * k - 2] = total
            self.pair(k - 1).start()
        return total


TILE = 256
LANES = 128
BAND = 32
CROSS_Q, CROSS_K, CROSS_V, CROSS_O, SELF_Q, SELF_K, SELF_V, SELF_O, UP = range(9)


def tile(start, size):
    return pl.ds(pl.multiple_of(start, size), size)


def bands(rows, body, carry=0):
    return lax.fori_loop(0, rows // BAND, lambda k, c: body(tile(k * BAND, BAND), c), carry)


def normalised(values):
    centre = values - jnp.mean(values, axis=-1, keepdims=True)
    inverse = lax.rsqrt(jnp.mean(centre * centre, axis=-1, keepdims=True) + norm_eps)
    return centre * inverse, inverse


def block_kernel(names, sizes, *refs):
    r = types.SimpleNamespace(**dict(zip(names, refs, strict=True)))
    width, lat, pix, hidden_parts = sizes
    f32, bf16 = jnp.float32, jnp.bfloat16
    here = Place()
    core = here.core
    scale = (width // HEADS) ** (-0.5)
    panel_blocks = UP + hidden_parts
    gather_order = [CROSS_K, CROSS_V, CROSS_Q, CROSS_O, SELF_Q, SELF_K, SELF_V, SELF_O]
    gather_order += list(range(UP, panel_blocks))
    share_rows = r.panel.shape[0]

    meet_in = Meeting(here, r.vectors, r.meet_line, r.meet_pairs, r.meet_send, r.meet_receive)
    meet_out = Meeting(here, r.vector_grad, r.sum_line, r.sum_pairs, r.sum_send, r.sum_receive)
    meet_last = Meeting(here, r.squares, r.last_line, r.last_pairs, r.last_send, r.last_receive)

    chunks, keep = [], []
    for block in gather_order:
        columns = pl.ds(block * width, width)
        r.low_panel[:, columns] = r.panel[:, columns].astype(bf16)
        whole = r.whole_panel.at[:, :, :, :, :, columns]
        chunks.append(whole)
        own = whole.at[here.z, here.x, core, here.y]
        keep.append(pltpu.make_async_copy(r.low_panel.at[:, columns], own, r.own.at[len(keep)]))
        keep[-1].start()
    for part in range(hidden_parts):
        rows = pl.ds(part * share_rows, share_rows)
        r.low_down[rows, :] = r.down[rows, :].astype(bf16)
        whole = r.whole_down.at[:, :, :, :, rows]
        chunks.append(whole)
        own = whole.at[here.z, here.x, core, here.y]
        keep.append(pltpu.make_async_copy(r.low_down.at[rows], own, r.own.at[len(keep)]))
        keep[-1].start()
    gather = Gather(here, chunks, r.gather_send, r.gather_receive)
    here.greet(True)

    def gather_tick(tick):
        if tick < len(keep):
            keep[tick].wait()
        for step in range(GATHER_STAGES):
            gather.stage(tick - step, step)

    twins = {}

    def to_twin(source, target):
        number = len(twins)
        copy = remote(
            source, target, r.twin_send.at[number], r.twin_receive.at[number], here.twin_device
        )
        copy.start()
        twins[number] = copy
        return number

    def from_twin(number):
        twins[number].wait_recv()

    flat_panel = r.whole_panel.reshape(-1, panel_blocks * width)
    flat_down = r.whole_down.reshape(-1, width)
    loads = []

    def fetch(part):
        if isinstance(part, tuple):
            source = flat_down.at[pl.ds(part[1] * width, width)]
        else:
            source = flat_panel.at[:, pl.ds(part * width, width)]
        slot = len(loads) % 2
        copy = pltpu.make_async_copy(source, r.weights.at[slot], r.load.at[slot])
        copy.start()
        loads.append(copy)
        return len(loads) - 1

    def fetched(number):
        loads[number].wait()
        return number % 2

    def put(n, value):
        if n < hidden_parts:
            r.down_share[n * share_rows : (n + 1) * share_rows, :] = value
        else:
            block = reduce_order[n]
            r.panel_share[:, block * width : (block + 1) * width] = value
        square = value * value
        gained = r.squares[...]
        for across in range(0, width, LANES):
            for at in range(0, share_rows, 8):
                gained = gained + square[at : at + 8, across : across + LANES]
        r.squares[...] = gained

    reduce_order = [None] * hidden_parts + list(range(UP, panel_blocks))
    reduce_order += [SELF_O, SELF_Q, SELF_K, SELF_V, CROSS_O, CROSS_Q, CROSS_K, CROSS_V]
    reduce = Reduce(here, r, len(reduce_order), put)

    def vector(k):
        return r.rows[k : k + 1, :]

    def times(left, slot, emit):
        def one(k, carry):
            columns = tile(k * TILE, TILE)
            emit(columns, jnp.dot(left[...], r.weights[slot, :, columns], preferred_element_type=f32))
            return carry

        lax.fori_loop(0, width // TILE, one, 0)

    def times_back(left, slot, emit):
        def one(k, carry):
            columns = tile(k * TILE, TILE)
            emit(columns, times_transposed(left[...], r.weights[slot, columns, :]))
            return carry

        lax.fori_loop(0, width // TILE, one, 0)

    def norm_rows(read, count, gain, shift, target):
        def one(rows, carry):
            normed, _ = normalised(read(rows))
            target[rows, :] = (normed * vector(gain) + vector(shift)).astype(bf16)
            return carry

        bands(count, one)

    def keep_vector(k, value):
        for at in range(width // LANES):
            row = k * (width // LANES) + at
            r.vector_grad[row : row + 1, :] = value[:, at * LANES : (at + 1) * LANES]

    def folded(value):
        total = value[0:8]
        for at in range(8, BAND, 8):
            total = total + value[at : at + 8]
        return total

    def norm_back(read, grad, count, gain, shift, emit):
        def one(rows, carry):
            gain_sum, shift_sum = carry
            normed, inverse = normalised(read(rows))
            out = grad[rows, :]
            if emit is not None:
                inner = out * vector(gain)
                emit(
                    rows,
                    inverse
                    * (
                        inner
                        - jnp.mean(inner, axis=-1, keepdims=True)
                        - normed * jnp.mean(inner * normed, axis=-1, keepdims=True)
                    ),
                )
            return gain_sum + folded(out * normed), shift_sum + folded(out)

        empty = jnp.zeros((8, width), f32)
        gain_sum, shift_sum = bands(count, one, (empty, empty))
        keep_vector(gain, jnp.sum(gain_sum, axis=0, keepdims=True))
        keep_vector(shift, jnp.sum(shift_sum, axis=0, keepdims=True))

    head = width // HEADS

    def probabilities(queries, keys, masked):
        scores = times_transposed(queries, keys) * scale
        if masked:
            scores = jnp.where(r.mask[0:1, :] > 0.5, scores, masked_fill)
        powers = jnp.exp(scores - jnp.max(scores, axis=-1, keepdims=True))
        return powers / jnp.sum(powers, axis=-1, keepdims=True)

    def attend(queries, keys, key_start, values, value_start, masked, target):
        def one(k, carry):
            columns = tile(k * head, head)
            probability = probabilities(
                queries[:, columns], keys[:, tile(key_start + k * head, head)], masked
            )
            value_rows = values[:, tile(value_start + k * head, head)]
            target[:, columns] = matmul_low(probability.astype(bf16), value_rows).astype(bf16)
            return carry

        lax.fori_loop(0, HEADS, one, 0)

    def attend_back(grad, queries, keys, key_start, values, value_start, masked, targets):
        query_grad, key_grad, key_at, value_grad, value_at = targets

        def one(k, carry):
            columns = tile(k * head, head)
            key_columns = tile(key_start + k * head, head)
            value_columns = tile(value_start + k * head, head)
            query_rows, key_rows = queries[:, columns], keys[:, key_columns]
            probability = probabilities(query_rows, key_rows, masked)
            grad_mix = grad[:, columns]
            grad_prob = times_transposed(grad_mix, values[:, value_columns])
            inner = jnp.sum(grad_prob * probability, axis=-1, keepdims=True)
            grad_scores = (probability * (grad_prob - inner)).astype(bf16)
            query_grad[:, columns] = (matmul_low(grad_scores, key_rows) * scale).astype(bf16)
            key_grad[:, tile(key_at + k * head, head)] = (
                rows_inner(grad_scores, query_rows) * scale
            ).astype(bf16)
            value_grad[:, tile(value_at + k * head, head)] = rows_inner(
                probability.astype(bf16), grad_mix
            ).astype(bf16)
            return carry

        lax.fori_loop(0, HEADS, one, 0)

    row_id = lax.broadcasted_iota(jnp.int32, (LANES, LANES), 0)
    unit = (row_id == lax.broadcasted_iota(jnp.int32, (LANES, LANES), 1)).astype(bf16)

    def turn(source, target, landing):
        def one(k, carry):
            turned = times_transposed(unit, source[:, tile(k * LANES, LANES)]).astype(bf16)
            for side in range(2):
                target[side, k] = turned[side * LANES // 2 : (side + 1) * LANES // 2]
            return carry

        lax.fori_loop(0, width // LANES, one, 0)
        return to_twin(target.at[1 - core], landing)

    def weight_grad(n, own, other, grad, grad_other, start):
        reduce.free(n)
        slot = n % STAGED

        def one(k, carry):
            columns = tile(start + k * TILE, TILE)
            total = matmul_low(own(), grad[:, columns]) + matmul_low(other(), grad_other[:, columns])
            total = total.astype(bf16).reshape(LONG, SHORT, SHORT, share_rows, TILE)
            into = tile(k * TILE, TILE)
            for to_x in range(SHORT):
                for to_y in range(SHORT):
                    first = jnp.where(core == 0, to_x, to_y)
                    second = jnp.where(core == 0, to_y, to_x)
                    r.staged[slot, :, first, second, :, into] = total[:, to_x, to_y]
            return carry

        lax.fori_loop(0, width // TILE, one, 0)

    def turned_pair(target, landing):
        rows = target.shape[3]
        return (
            lambda: target[core].reshape(-1, rows),
            lambda: landing[...].reshape(-1, rows),
        )

    dz_sent = None
    marks = types.SimpleNamespace()

    def after_vectors(total):
        per = width // LANES
        for row in range(r.rows.shape[0]):
            for at in range(per):
                line = total[row * per + at : row * per + at + 1, :]
                r.rows[row : row + 1, at * LANES : (at + 1) * LANES] = line.astype(bf16).astype(f32)
        norm_rows(lambda rows: r.pixels[rows, :].astype(f32), pix, 0, 1, r.pixel_low)
        norm_rows(lambda rows: r.latents[rows, :].astype(f32), lat, 2, 3, r.left)
        marks.pixel = turn(r.pixel_low, r.turned_pixel, r.landed_pixel)
        marks.cross = turn(r.left, r.turned_cross, r.landed_cross)

    def to_columns(target, start=0):
        def emit(columns, value):
            where = pl.ds(pl.multiple_of(columns.start + start, TILE), TILE)
            target[:, where] = value.astype(bf16)

        return emit

    def add_columns(target, base):
        def emit(columns, value):
            target[:, columns] = base[:, columns].astype(f32) + value

        return emit

    def forward(block, slot):
        if block == CROSS_K:
            times(r.pixel_low, slot, to_columns(r.pair))
        elif block == CROSS_V:
            times(r.pixel_low, slot, to_columns(r.pair, width))
        elif block == CROSS_Q:
            times(r.left, slot, to_columns(r.cross_query))
            attend(r.cross_query, r.pair, 0, r.pair, width, True, r.mixed)
            marks.cross_mix = turn(r.mixed, r.turned_cross_mix, r.landed_cross_mix)
        elif block == CROSS_O:
            times(r.mixed, slot, add_columns(r.first, r.latents))
            norm_rows(lambda rows: r.first[rows, :], lat, 4, 5, r.left)
            marks.self = turn(r.left, r.turned_self, r.landed_self)
        elif block in (SELF_Q, SELF_K, SELF_V):
            times(r.left, slot, to_columns(r.triple, (block - SELF_Q) * width))
            if block == SELF_V:
                attend(r.triple, r.triple, width, r.triple, 2 * width, False, r.mixed)
                marks.self_mix = turn(r.mixed, r.turned_self_mix, r.landed_self_mix)
        elif block == SELF_O:
            times(r.mixed, slot, add_columns(r.second, r.first))
            norm_rows(lambda rows: r.second[rows, :], lat, 6, 7, r.left)
            marks.feed = turn(r.left, r.turned_feed, r.landed_feed)
        else:
            part = block - UP

            def emit(columns, value):
                upper = value + r.rows[9 + part : 10 + part, columns]
                below = 0.5 + 0.5 * lax.erf(upper * (0.5**0.5))
                where = pl.ds(pl.multiple_of(columns.start + part * width, TILE), TILE)
                r.hidden[:, where] = (upper * below).astype(bf16)
                density = jnp.exp(-0.5 * upper * upper) * ((2.0 * math.pi) ** -0.5)
                r.slope[:, where] = below + upper * density

            times(r.left, slot, emit)

            def one(k, carry):
                block_at = part * (width // LANES) + k
                turned = times_transposed(unit, r.hidden[:, tile(block_at * LANES, LANES)])
                turned = turned.astype(bf16).reshape(hidden_parts, share_rows, lat)
                side = (k // 2) % 2
                r.turned_hidden[side, block_at // 4 * 2 + k % 2] = turned
                return carry

            lax.fori_loop(0, width // LANES, one, 0)

    ticks = len(chunks) + GATHER_STAGES - 1
    lead = GATHER_STAGES + 1
    forward_blocks = len(gather_order)
    for tick in range(forward_blocks + lead):
        gather_tick(tick)
        if tick < 5:
            total = meet_in.step(tick)
            if tick == 4:
                after_vectors(total)
        elif tick == 5:
            marks.dz = to_twin(r.out_grad, r.landed_dz)
        if 0 <= tick - lead + 1 < forward_blocks:
            gather.whole(tick - lead + 1)
            fetch(gather_order[tick - lead + 1])
        if tick - lead >= 0:
            forward(gather_order[tick - lead], fetched(tick - lead))
    marks.hidden = to_twin(r.turned_hidden.at[1 - core], r.landed_hidden)

    r.squares[...] = jnp.zeros_like(r.squares)
    for tick in range(forward_blocks + lead, ticks):
        gather_tick(tick)
    from_twin(marks.dz)
    from_twin(marks.hidden)

    def hidden_grad(part):
        weight_grad(
            part,
            lambda: r.turned_hidden[core, :, part].reshape(-1, lat),
            lambda: r.landed_hidden[:, part].reshape(-1, lat),
            r.out_grad,
            r.landed_dz,
            0,
        )
        reduce.tick(part)

    hidden_grad(0)
    for n in range(forward_blocks, len(chunks)):
        gather.whole(n)
    number = fetch(("down", 0))
    hidden_grad(1)

    def start_out(rows, carry):
        r.total[rows, :] = r.second[rows, :] + vector(8)
        return carry + folded(r.out_grad[rows, :].astype(f32))

    shift_sum = bands(lat, start_out, jnp.zeros((8, width), f32))
    keep_vector(8, jnp.sum(shift_sum, axis=0, keepdims=True))
    du_marks = []

    def out_and_du(part, slot):
        hidden_part = r.hidden.at[:, pl.ds(part * width, width)]

        def emit(columns, value):
            r.total[:, columns] += value

        times(hidden_part, slot, emit)

        def emit_du(columns, value):
            where = pl.ds(pl.multiple_of(columns.start + part * width, TILE), TILE)
            low = (value * r.slope[:, where]).astype(bf16)
            r.hidden[:, where] = low
            column_sum = jnp.sum(low.astype(f32), axis=0, keepdims=True)
            at = 9 * (width // LANES) + part * (width // LANES) + lax.div(columns.start, LANES)
            for k in range(TILE // LANES):
                r.vector_grad[pl.ds(at + k, 1), :] = column_sum[:, k * LANES : (k + 1) * LANES]

        times_back(r.out_grad, slot, emit_du)
        du_marks.append(to_twin(hidden_part, r.landed_du.at[:, pl.ds(part * width, width)]))

    for part in range(hidden_parts):
        slot = fetched(number)
        number = fetch(("down", part + 1) if part + 1 < hidden_parts else UP)
        out_and_du(part, slot)
        if part + 2 < hidden_parts:
            hidden_grad(part + 2)

    def finish_out(rows, carry):
        r.latents_out[rows, :] = r.total[rows, :].astype(bf16)
        r.total[rows, :] = jnp.zeros((BAND, width), f32)
        return carry

    bands(lat, finish_out)

    def add_total(columns, value):
        r.total[:, columns] += value

    from_twin(marks.feed)
    own, other = turned_pair(r.turned_feed, r.landed_feed)
    for part in range(hidden_parts):
        slot = fetched(number)
        number = fetch(UP + part + 1 if part + 1 < hidden_parts else SELF_O)
        times_back(r.hidden.at[:, pl.ds(part * width, width)], slot, add_total)
        from_twin(du_marks[part])
        n = hidden_parts + part
        weight_grad(n, own, other, r.hidden, r.landed_du, part * width)
        if part + 1 == hidden_parts:

            def into_second(rows, value):
                value = value + r.out_grad[rows, :].astype(f32)
                r.second[rows, :] = value
                r.grad_low[rows, :] = value.astype(bf16)

            norm_back(lambda rows: r.second[rows, :], r.total, lat, 6, 7, into_second)
            marks.ds = to_twin(r.grad_low, r.landed_ds)
        reduce.tick(n)

    def branch_out(n, slot, grad_low, landed, mark, turned, landed_turned, turned_mark):
        times_back(grad_low, slot, to_columns(r.mixed))
        from_twin(mark)
        from_twin(turned_mark)
        weight_grad(n, *turned_pair(turned, landed_turned), grad_low, landed, 0)

    n = 2 * hidden_parts
    slot = fetched(number)
    number = fetch(SELF_Q)
    branch_out(
        n, slot, r.grad_low, r.landed_ds, marks.ds, r.turned_self_mix, r.landed_self_mix, marks.self_mix
    )
    reduce.stage(n, 0)
    attend_back(
        r.mixed,
        r.triple,
        r.triple,
        width,
        r.triple,
        2 * width,
        False,
        (r.triple_grad, r.triple_grad, width, r.triple_grad, 2 * width),
    )
    triple_marks = []
    for part in range(3):
        columns = pl.ds(part * width, width)
        triple_marks.append(to_twin(r.triple_grad.at[:, columns], r.landed_triple.at[:, columns]))
    for step in range(1, REDUCE_STAGES):
        reduce.stage(n - step, step)

    def clear(rows, carry):
        r.total[rows, :] = jnp.zeros((BAND, width), f32)
        return carry

    bands(lat, clear)
    from_twin(marks.self)
    own, other = turned_pair(r.turned_self, r.landed_self)
    for part in range(3):
        slot = fetched(number)
        number = fetch((SELF_K, SELF_V, CROSS_O)[part])
        times_back(r.triple_grad.at[:, pl.ds(part * width, width)], slot, add_total)
        from_twin(triple_marks[part])
        n += 1
        weight_grad(n, own, other, r.triple_grad, r.landed_triple, part * width)
        if part == 2:

            def into_first(rows, value):
                value = value + r.second[rows, :]
                r.second[rows, :] = value
                r.cross_low[rows, :] = value.astype(bf16)

            norm_back(lambda rows: r.first[rows, :], r.total, lat, 4, 5, into_first)
            marks.dc = to_twin(r.cross_low, r.landed_dc)
        reduce.tick(n)

    n += 1
    slot = fetched(number)
    number = fetch(CROSS_Q)
    branch_out(
        n, slot, r.cross_low, r.landed_dc, marks.dc, r.turned_cross_mix, r.landed_cross_mix, marks.cross_mix
    )
    reduce.stage(n, 0)
    attend_back(
        r.mixed,
        r.cross_query,
        r.pair,
        0,
        r.pair,
        width,
        True,
        (r.query_grad, r.pair_grad, 0, r.pair_grad, width),
    )
    query_mark = to_twin(r.query_grad, r.landed_query)
    pair_marks = []
    for part in range(2):
        columns = pl.ds(part * width, width)
        pair_marks.append(to_twin(r.pair_grad.at[:, columns], r.landed_pair.at[:, columns]))
    for step in range(1, REDUCE_STAGES):
        reduce.stage(n - step, step)

    slot = fetched(number)
    number = fetch(CROSS_K)

    def set_total(columns, value):
        r.total[:, columns] = value

    times_back(r.query_grad, slot, set_total)
    from_twin(query_mark)
    from_twin(marks.cross)
    n += 1
    weight_grad(n, *turned_pair(r.turned_cross, r.landed_cross), r.query_grad, r.landed_query, 0)
    reduce.stage(n, 0)

    def into_latents(rows, value):
        r.latents_grad[rows, :] = value + r.second[rows, :]

    norm_back(lambda rows: r.latents[rows, :].astype(f32), r.total, lat, 2, 3, into_latents)
    for step in range(1, REDUCE_STAGES):
        reduce.stage(n - step, step)
    from_twin(marks.pixel)
    own, other = turned_pair(r.turned_pixel, r.landed_pixel)
    pixel_total = r.total.at[pl.ds(0, pix)]

    for part in range(2):
        slot = fetched(number)
        if part == 0:
            number = fetch(CROSS_V)

        def emit_pixel(columns, value):
            if part == 0:
                pixel_total[:, columns] = value
            else:
                pixel_total[:, columns] += value

        times_back(r.pair_grad.at[:, pl.ds(part * width, width)], slot, emit_pixel)
        from_twin(pair_marks[part])
        n += 1
        weight_grad(n, own, other, r.pair_grad, r.landed_pair, part * width)
        reduce.stage(n, 0)
        if part == 1:
            norm_back(lambda rows: r.pixels[rows, :].astype(f32), pixel_total, pix, 0, 1, None)
            meet_out.step(0)
        for step in range(1, REDUCE_STAGES):
            reduce.stage(n - step, step)
    for k in range(1, REDUCE_STAGES):
        if k < 5:
            total = meet_out.step(k)
            if k == 4:
                r.vector_share[...] = total
        reduce.tick(n + k)
    for k in range(5):
        total = meet_last.step(k)
    r.square_sum[...] = total
    reduce.finish()
    gather.finish()
    for copy in twins.values():
        copy.wait_send()


def run_block(latents, pixels, mask, out_grad, panel, down, vectors):
    f32, bf16 = jnp.float32, jnp.bfloat16
    lat, width = latents.shape
    pix = pixels.shape[0]
    share_rows = panel.shape[0]
    hidden_parts = down.shape[0] // share_rows
    wide = hidden_parts * width
    half = LANES // 2
    blocks = panel.shape[1] // width
    chunks = blocks + hidden_parts
    unit = (share_rows, width)
    vmem = pltpu.VMEM
    dma, any_space = pltpu.SemaphoreType.DMA, pl.BlockSpec(memory_space=pl.ANY)
    in_vmem = pl.BlockSpec(memory_space=pltpu.VMEM)
    inputs = dict(
        latents=latents,
        pixels=pixels,
        mask=mask,
        out_grad=out_grad,
        panel=panel,
        down=down,
        vectors=vectors,
    )
    outputs = dict(
        latents_out=((lat, width), bf16),
        latents_grad=((lat, width), f32),
        panel_share=(panel.shape, f32),
        down_share=(down.shape, f32),
        vector_share=(vectors.shape, f32),
        square_sum=((8, LANES), f32),
        whole_panel=(CUT + panel.shape, bf16),
        whole_down=(CUT + down.shape, bf16),
    )
    groups = width // LANES
    lines = -(-RING // 3)
    scratch = dict(
        low_panel=vmem(panel.shape, bf16),
        low_down=vmem(down.shape, bf16),
        weights=vmem((2, width, width), bf16),
        rows=vmem((vectors.shape[0] // groups, width), f32),
        pixel_low=vmem((pix, width), bf16),
        left=vmem((lat, width), bf16),
        mixed=vmem((lat, width), bf16),
        cross_query=vmem((lat, width), bf16),
        pair=vmem((pix, 2 * width), bf16),
        first=vmem((lat, width), f32),
        triple=vmem((lat, 3 * width), bf16),
        second=vmem((lat, width), f32),
        hidden=vmem((lat, wide), bf16),
        slope=vmem((lat, wide), f32),
        total=vmem((lat, width), f32),
        grad_low=vmem((lat, width), bf16),
        cross_low=vmem((lat, width), bf16),
        triple_grad=vmem((lat, 3 * width), bf16),
        query_grad=vmem((lat, width), bf16),
        pair_grad=vmem((pix, 2 * width), bf16),
        vector_grad=vmem(vectors.shape, f32),
        squares=vmem((8, LANES), f32),
        turned_pixel=vmem((2, groups, half, pix), bf16),
        landed_pixel=vmem((groups, half, pix), bf16),
        turned_hidden=vmem((2, wide // LANES // 2, hidden_parts, share_rows, lat), bf16),
        landed_hidden=vmem((wide // LANES // 2, hidden_parts, share_rows, lat), bf16),
        landed_dz=vmem((lat, width), bf16),
        landed_du=vmem((lat, wide), bf16),
        landed_ds=vmem((lat, width), bf16),
        landed_triple=vmem((lat, 3 * width), bf16),
        landed_dc=vmem((lat, width), bf16),
        landed_query=vmem((lat, width), bf16),
        landed_pair=vmem((pix, 2 * width), bf16),
        staged=vmem((STAGED, LONG, SHORT, SHORT) + unit, bf16),
        from_far=vmem((RING, LONG, SHORT) + unit, bf16),
        from_near_line=vmem((lines, LONG) + unit, bf16),
        from_near=vmem((RING - lines,) + unit, bf16),
        from_line_short=vmem((lines, 2 * (LONG - 1)) + unit, bf16),
        from_line=vmem((RING - lines, 2 * (LONG - 1), SHORT) + unit, bf16),
        own=dma((chunks,)),
        load=dma((2,)),
        gather_send=dma((chunks, GATHER_KINDS)),
        gather_receive=dma((chunks, GATHER_KINDS)),
        reduce_send=dma((chunks, REDUCE_KINDS)),
        reduce_receive=dma((chunks, REDUCE_KINDS)),
        twin_send=dma((16 + hidden_parts,)),
        twin_receive=dma((16 + hidden_parts,)),
        credit=pltpu.SemaphoreType.REGULAR((chunks - RING, 4)),
    )
    for name in ("cross", "cross_mix", "self", "self_mix", "feed"):
        scratch["turned_" + name] = vmem((2, groups, half, lat), bf16)
        scratch["landed_" + name] = vmem((groups, half, lat), bf16)
    for name, shape in (("meet", vectors.shape), ("sum", vectors.shape), ("last", (8, LANES))):
        scratch[name + "_line"] = vmem((LONG,) + shape, f32)
        scratch[name + "_pairs"] = vmem((6,) + shape, f32)
        scratch[name + "_send"] = dma((LONG + 2,))
        scratch[name + "_receive"] = dma((LONG + 2,))
    names = tuple(inputs) + tuple(outputs) + tuple(scratch)
    sizes = (width, lat, pix, hidden_parts)
    results = pl.pallas_call(
        functools.partial(block_kernel, names, sizes),
        out_shape=[jax.ShapeDtypeStruct(*spec) for spec in outputs.values()],
        in_specs=[in_vmem] * len(inputs),
        out_specs=[in_vmem] * 6 + [any_space] * 2,
        scratch_shapes=list(scratch.values()),
        compiler_params=pltpu.CompilerParams(
            collective_id=0, has_side_effects=True, vmem_limit_bytes=VMEM_LIMIT
        ),
    )(*inputs.values())
    return results[:6]


def fast_step(
    latents,
    pixels,
    visible,
    out_grad,
    panel,
    panel_moment,
    panel_square,
    down,
    down_moment,
    down_square,
    vectors,
    vector_moment,
    vector_square,
):
    latent_count, model_width = latents.shape[1:]
    pixel_count = pixels.shape[1]
    device_total = lax.axis_size(("dp", "fsdp"))
    own_start = lax.axis_index(("dp", "fsdp")) * vectors.shape[0]
    vector_total = vectors.shape[0] * device_total
    own_vectors = lax.dynamic_update_slice(
        jnp.zeros((vector_total,), jnp.float32), vectors, (own_start,)
    )
    mask = jnp.arange(pixel_count, dtype=jnp.int32)[None, :] < visible[:, None]
    mask = jnp.broadcast_to(mask.astype(jnp.float32), (8, pixel_count))
    latents_out, latents_grad, panel_share, down_share, vector_sum, squares = run_block(
        latents.reshape(-1, model_width),
        pixels.reshape(-1, model_width),
        mask,
        out_grad.reshape(-1, model_width),
        panel,
        down,
        own_vectors.reshape(-1, LANES),
    )
    grad_norm = jnp.sqrt(jnp.sum(squares) + jnp.sum(vector_sum * vector_sum))
    vector_share = lax.dynamic_slice(vector_sum.reshape(-1), (own_start,), vectors.shape)
    token_total = latents.shape[0] * latent_count * device_total
    param_total = device_total * (panel.size + down.size + vectors.size)
    threshold = clip_coeff * (token_total * param_total) ** 0.5
    factor = threshold / jnp.maximum(grad_norm, threshold)
    return (
        latents_out.reshape(latents.shape),
        latents_grad.reshape(latents.shape),
        grad_norm,
        *adam_update(
            panel, panel_moment, panel_square, panel_share * factor, rate_matrix, weight_decay
        ),
        *adam_update(down, down_moment, down_square, down_share * factor, rate_matrix, weight_decay),
        *adam_update(vectors, vector_moment, vector_square, vector_share * factor, rate_vector, 0.0),
    )


def slow_gather(panel, down, vectors):
    model_width = panel.shape[1] // 12
    bf16 = jnp.bfloat16
    parts = [panel[:, k * 4 * model_width : (k + 1) * 4 * model_width].astype(bf16) for k in range(3)]
    parts += [down.astype(bf16), vectors.astype(bf16)]
    return [lax.all_gather(part, ("dp", "fsdp"), axis=0, tiled=True) for part in parts]


def slow_reduce(pieces, down_grad, vector_grad, share_length):
    shares = [
        lax.psum_scatter(grad, ("dp", "fsdp"), scatter_dimension=0, tiled=True)
        for grad in (jnp.concatenate(pieces, axis=1), down_grad, vector_grad)
    ]
    squares = lax.psum(sum(jnp.sum(share * share) for share in shares), ("dp", "fsdp"))
    return (*shares, squares)


def shards(
    gather,
    reduce,
    latents,
    pixels,
    visible,
    out_grad,
    panel,
    panel_moment,
    panel_square,
    down,
    down_moment,
    down_square,
    vectors,
    vector_moment,
    vector_square,
):
    images, latent_count, model_width = latents.shape
    pixel_count = pixels.shape[1]
    bf16 = jnp.bfloat16
    cross_columns, self_columns, up_columns, full_down, full_vector = gather(panel, down, vectors)
    vector_float = full_vector.astype(jnp.float32)
    gain_pixel = vector_slot(vector_float, 0, model_width)
    shift_pixel = vector_slot(vector_float, 1, model_width)
    gain_cross = vector_slot(vector_float, 2, model_width)
    shift_cross = vector_slot(vector_float, 3, model_width)
    gain_self = vector_slot(vector_float, 4, model_width)
    shift_self = vector_slot(vector_float, 5, model_width)
    gain_feed = vector_slot(vector_float, 6, model_width)
    shift_feed = vector_slot(vector_float, 7, model_width)
    bias_down = vector_slot(vector_float, 8, model_width)
    bias_up = vector_float[9 * model_width :]
    latent_rows = latents.reshape(-1, model_width).astype(jnp.float32)
    pixel_rows = pixels.reshape(-1, model_width).astype(jnp.float32)
    pixel_out, pixel_normed, pixel_inverse = norm_forward(pixel_rows, gain_pixel, shift_pixel)
    pixel_low = pixel_out.astype(bf16)
    cross_out, cross_normed, cross_inverse = norm_forward(latent_rows, gain_cross, shift_cross)
    cross_low = cross_out.astype(bf16)
    cross_queries = matmul_low(cross_low, cross_columns[:, :model_width]).astype(bf16)
    pair_rows = matmul_low(pixel_low, cross_columns[:, model_width : 3 * model_width]).astype(bf16)
    visible_mask = jnp.arange(pixel_count, dtype=jnp.int32)[None, :] < visible[:, None]
    query_heads = to_heads(cross_queries, images, HEADS)
    key_heads = to_heads(pair_rows[:, :model_width], images, HEADS)
    value_heads = to_heads(pair_rows[:, model_width:], images, HEADS)
    cross_mix, cross_top, cross_total = attend_forward(
        query_heads, key_heads, value_heads, visible_mask
    )
    cross_mixed = cross_mix.reshape(-1, model_width)
    first_sum = latent_rows + matmul_low(
        cross_mixed, cross_columns[:, 3 * model_width :]
    )
    forward_saved = self_forward(first_sum, self_columns, gain_self, shift_self, images)
    second_sum = first_sum + matmul_low(forward_saved[6], self_columns[:, 3 * model_width :])
    feed_out, feed_normed, feed_inverse = norm_forward(second_sum, gain_feed, shift_feed)
    feed_low = feed_out.astype(bf16)
    upper_in = matmul_low(feed_low, up_columns) + bias_up
    hidden_float, gelu_back = jax.vjp(gelu_exact, upper_in)
    hidden = hidden_float.astype(bf16)
    result = second_sum + (matmul_low(hidden, full_down) + bias_down)
    latents_out = result.astype(bf16).reshape(latents.shape)
    grad_three = out_grad.reshape(-1, model_width).astype(jnp.float32)
    grad_branch = grad_three.astype(bf16)
    grad_down = rows_inner(hidden, grad_branch)
    grad_bias_down = jnp.sum(grad_branch.astype(jnp.float32), axis=0)
    grad_upper = gelu_back(times_transposed(grad_branch, full_down))[0].astype(bf16)
    grad_up = rows_inner(feed_low, grad_upper)
    grad_bias_up = jnp.sum(grad_upper.astype(jnp.float32), axis=0)
    grad_feed, grad_gain_feed, grad_shift_feed = norm_backward(
        times_transposed(grad_upper, up_columns),
        feed_normed,
        feed_inverse,
        gain_feed,
    )
    grad_two = grad_three + grad_feed
    (
        self_normed,
        self_inverse,
        self_low,
        self_queries,
        self_keys,
        self_values,
        self_mixed,
        self_top,
        self_total,
    ) = forward_saved
    grad_self_branch = grad_two.astype(bf16)
    grad_self_out = rows_inner(self_mixed, grad_self_branch)
    grad_self_mix = times_transposed(grad_self_branch, self_columns[:, 3 * model_width :]).astype(
        bf16
    )
    grad_query_heads, grad_key_heads, grad_value_heads = attend_backward(
        to_heads(grad_self_mix, images, HEADS),
        self_queries,
        self_keys,
        self_values,
        None,
        self_top,
        self_total,
    )
    grad_triple = jnp.concatenate(
        [
            grad_query_heads.reshape(-1, model_width),
            grad_key_heads.reshape(-1, model_width),
            grad_value_heads.reshape(-1, model_width),
        ],
        axis=1,
    ).astype(bf16)
    grad_self_in = rows_inner(self_low, grad_triple)
    grad_first, grad_gain_self, grad_shift_self = norm_backward(
        times_transposed(grad_triple, self_columns[:, : 3 * model_width]),
        self_normed,
        self_inverse,
        gain_self,
    )
    grad_one = grad_two + grad_first
    grad_cross_branch = grad_one.astype(bf16)
    grad_cross_out = rows_inner(cross_mixed, grad_cross_branch)
    grad_cross_mix = times_transposed(
        grad_cross_branch, cross_columns[:, 3 * model_width :]
    ).astype(bf16)
    cross_query_grad, cross_key_grad, cross_value_grad = attend_backward(
        to_heads(grad_cross_mix, images, HEADS),
        query_heads,
        key_heads,
        value_heads,
        visible_mask,
        cross_top,
        cross_total,
    )
    grad_queries = cross_query_grad.reshape(-1, model_width).astype(bf16)
    grad_pair = jnp.concatenate(
        [cross_key_grad.reshape(-1, model_width), cross_value_grad.reshape(-1, model_width)], axis=1
    ).astype(bf16)
    grad_cross_query = rows_inner(cross_low, grad_queries)
    grad_cross_pair = rows_inner(pixel_low, grad_pair)
    grad_input_norm, grad_gain_cross, grad_shift_cross = norm_backward(
        times_transposed(grad_queries, cross_columns[:, :model_width]),
        cross_normed,
        cross_inverse,
        gain_cross,
    )
    pixel_unused, grad_gain_pixel, grad_shift_pixel = norm_backward(
        times_transposed(grad_pair, cross_columns[:, model_width : 3 * model_width]),
        pixel_normed,
        pixel_inverse,
        gain_pixel,
    )
    latents_grad = (grad_one + grad_input_norm).reshape(latents.shape)
    vector_grad = jnp.concatenate(
        [
            grad_gain_pixel,
            grad_shift_pixel,
            grad_gain_cross,
            grad_shift_cross,
            grad_gain_self,
            grad_shift_self,
            grad_gain_feed,
            grad_shift_feed,
            grad_bias_down,
            grad_bias_up,
        ]
    )
    pieces = [
        grad_cross_query,
        grad_cross_pair,
        grad_cross_out,
        grad_self_in,
        grad_self_out,
        grad_up,
    ]
    panel_share, down_share, vector_share, squares = reduce(
        pieces, grad_down, vector_grad, vectors.shape[0]
    )
    grad_norm = jnp.sqrt(squares)
    device_total = lax.axis_size(("dp", "fsdp"))
    token_total = images * latent_count * device_total
    param_total = (
        model_width * panel.shape[1] + full_down.shape[0] * model_width + full_vector.shape[0]
    )
    threshold = clip_coeff * (token_total * param_total) ** 0.5
    factor = threshold / jnp.maximum(grad_norm, threshold)
    panel_after, panel_moment_after, panel_square_after = adam_update(
        panel, panel_moment, panel_square, panel_share * factor, rate_matrix, weight_decay
    )
    down_after, down_moment_after, down_square_after = adam_update(
        down, down_moment, down_square, down_share * factor, rate_matrix, weight_decay
    )
    vectors_after, vector_moment_after, vector_square_after = adam_update(
        vectors, vector_moment, vector_square, vector_share * factor, rate_vector, 0.0
    )
    return (
        latents_out,
        latents_grad,
        grad_norm,
        panel_after,
        panel_moment_after,
        panel_square_after,
        down_after,
        down_moment_after,
        down_square_after,
        vectors_after,
        vector_moment_after,
        vector_square_after,
    )


def solution(mesh):
    placed = (
        P(("dp", "fsdp"), None, None),
        P(("dp", "fsdp"), None, None),
        P(("dp", "fsdp")),
        P(("dp", "fsdp"), None, None),
        P(("dp", "fsdp"), None),
        P(("dp", "fsdp"), None),
        P(("dp", "fsdp"), None),
        P(("dp", "fsdp"), None),
        P(("dp", "fsdp"), None),
        P(("dp", "fsdp"), None),
        P(("dp", "fsdp")),
        P(("dp", "fsdp")),
        P(("dp", "fsdp")),
    )
    fast = (mesh.shape["dp"], mesh.shape["fsdp"]) == (LONG * SHORT * SHORT, SHORT)
    step = fast_step if fast else functools.partial(shards, slow_gather, slow_reduce)
    return jax.shard_map(
        step,
        mesh=mesh,
        in_specs=placed,
        out_specs=(
            P(("dp", "fsdp"), None, None),
            P(("dp", "fsdp"), None, None),
            P(),
            P(("dp", "fsdp"), None),
            P(("dp", "fsdp"), None),
            P(("dp", "fsdp"), None),
            P(("dp", "fsdp"), None),
            P(("dp", "fsdp"), None),
            P(("dp", "fsdp"), None),
            P(("dp", "fsdp")),
            P(("dp", "fsdp")),
            P(("dp", "fsdp")),
        ),
        check_vma=False,
    )
```

```python
import functools
import math
import types

import jax
import jax.numpy as jnp
from jax import lax
from jax.experimental import pallas as pl
from jax.experimental.pallas import tpu as pltpu
from jax.sharding import PartitionSpec as P

HEADS = 8
STEP = 10


norm_eps = 1e-05
beta_first = 0.9
beta_second = 0.999
adam_eps = 1e-08
rate_matrix = 0.05
rate_vector = 0.5
weight_decay = 0.1
clip_coeff = 0.01
masked_fill = -1e30


def matmul_low(left, right):
    return jnp.dot(left, right, preferred_element_type=jnp.float32)


def rows_inner(left, right):
    return lax.dot_general(
        left, right, (((0,), (0,)), ((), ())), preferred_element_type=jnp.float32
    )


def times_transposed(left, right):
    return lax.dot_general(
        left, right, (((1,), (1,)), ((), ())), preferred_element_type=jnp.float32
    )


def gelu_exact(values):
    return jax.nn.gelu(values, approximate=False)


def norm_forward(values, gain_row, shift_row):
    centre = values - jnp.mean(values, axis=-1, keepdims=True)
    inverse = lax.rsqrt(jnp.mean(centre * centre, axis=-1, keepdims=True) + norm_eps)
    normed = centre * inverse
    return (normed * gain_row + shift_row, normed, inverse)


def norm_backward(grad_out, normed, inverse, gain_row):
    grad_normed = grad_out * gain_row
    grad_values = inverse * (
        grad_normed
        - jnp.mean(grad_normed, axis=-1, keepdims=True)
        - normed * jnp.mean(grad_normed * normed, axis=-1, keepdims=True)
    )
    return (grad_values, jnp.sum(grad_out * normed, axis=0), jnp.sum(grad_out, axis=0))


def to_heads(rows, images, head_count):
    return rows.reshape(images, -1, head_count, rows.shape[1] // head_count)


def masked_scores(queries, key_rows, visible_mask):
    score_scale = queries.shape[-1] ** (-0.5)
    scores = (
        jnp.einsum("bqhd,bkhd->bhqk", queries, key_rows, preferred_element_type=jnp.float32)
        * score_scale
    )
    if visible_mask is not None:
        scores = jnp.where(visible_mask[:, None, None, :], scores, masked_fill)
    return scores


def attend_forward(queries, key_rows, value_rows, visible_mask):
    scores = masked_scores(queries, key_rows, visible_mask)
    row_top = jnp.max(scores, axis=-1, keepdims=True)
    powers = jnp.exp(scores - row_top)
    row_total = jnp.sum(powers, axis=-1, keepdims=True)
    probability = (powers / row_total).astype(jnp.bfloat16)
    mixture = jnp.einsum(
        "bhqk,bkhd->bqhd", probability, value_rows, preferred_element_type=jnp.float32
    )
    return (mixture.astype(jnp.bfloat16), row_top, row_total)


def attend_backward(grad_mix, queries, key_rows, value_rows, visible_mask, row_top, row_total):
    score_scale = queries.shape[-1] ** (-0.5)
    scores = masked_scores(queries, key_rows, visible_mask)
    probability = jnp.exp(scores - row_top) / row_total
    grad_prob = jnp.einsum(
        "bqhd,bkhd->bhqk", grad_mix, value_rows, preferred_element_type=jnp.float32
    )
    inner_sum = jnp.sum(grad_prob * probability, axis=-1, keepdims=True)
    grad_scores = (probability * (grad_prob - inner_sum)).astype(jnp.bfloat16)
    grad_queries = (
        jnp.einsum("bhqk,bkhd->bqhd", grad_scores, key_rows, preferred_element_type=jnp.float32)
        * score_scale
    )
    grad_keys = (
        jnp.einsum("bhqk,bqhd->bkhd", grad_scores, queries, preferred_element_type=jnp.float32)
        * score_scale
    )
    grad_values = jnp.einsum(
        "bhqk,bqhd->bkhd",
        probability.astype(jnp.bfloat16),
        grad_mix,
        preferred_element_type=jnp.float32,
    )
    return (grad_queries, grad_keys, grad_values)


def vector_slot(vector_float, index, model_width):
    return vector_float[index * model_width : (index + 1) * model_width]


def self_forward(first_sum, self_columns, gain_self, shift_self, images):
    model_width = first_sum.shape[1]
    normed_out, normed, inverse = norm_forward(first_sum, gain_self, shift_self)
    self_low = normed_out.astype(jnp.bfloat16)
    triple = matmul_low(self_low, self_columns[:, : 3 * model_width]).astype(jnp.bfloat16)
    self_queries = to_heads(triple[:, :model_width], images, HEADS)
    self_keys = to_heads(triple[:, model_width : 2 * model_width], images, HEADS)
    self_values = to_heads(triple[:, 2 * model_width :], images, HEADS)
    mixture, row_top, row_total = attend_forward(self_queries, self_keys, self_values, None)
    self_mixed = mixture.reshape(-1, model_width)
    return (
        normed,
        inverse,
        self_low,
        self_queries,
        self_keys,
        self_values,
        self_mixed,
        row_top,
        row_total,
    )


def adam_update(weight, moment, square, grad, rate, decay):
    moment_after = beta_first * moment + (1.0 - beta_first) * grad
    square_after = beta_second * square + (1.0 - beta_second) * grad * grad
    step_count = STEP
    fixed_moment = moment_after / (1.0 - beta_first**step_count)
    fixed_square = square_after / (1.0 - beta_second**step_count)
    weight_after = weight - rate * (
        fixed_moment / (jnp.sqrt(fixed_square) + adam_eps) + decay * weight
    )
    return (weight_after, moment_after, square_after)


MESH = pl.DeviceIdType.MESH
LONG, SHORT = 4, 2
CUT = (LONG, SHORT, SHORT, SHORT)
PLANE = SHORT * SHORT * SHORT
VMEM_LIMIT = 60 * 1024 * 1024


class Place:
    def __init__(self):
        row, self.y = lax.axis_index("dp"), lax.axis_index("fsdp")
        self.z, self.x, self.core = row // 4, (row // 2) % 2, row % 2
        even = self.core == 0
        x, y = self.x, self.y
        self.near = (jnp.where(even, 1 - x, x), jnp.where(even, y, 1 - y))
        self.far = (jnp.where(even, x, 1 - x), jnp.where(even, 1 - y, y))
        self.first, self.second = jnp.where(even, x, y), jnp.where(even, y, x)
        self.near_device = self.device(self.z, self.near[0], self.core, self.near[1])
        self.far_device = self.device(self.z, self.far[0], self.core, self.far[1])
        self.twin_device = self.device(self.z, x, 1 - self.core, y)
        self.up_device = self.device(self.z + 1, x, self.core, y)
        self.down_device = self.device(self.z - 1, x, self.core, y)

    def device(self, z, x, core, y):
        return (z * 4 + x * 2 + core, y)

    def along(self, step):
        return self.device((self.z + step) % LONG, self.x, self.core, self.y)

    def across(self, away):
        flip_x, flip_core, flip_y = away // 4, away // 2 % 2, away % 2
        return self.device(
            self.z,
            1 - self.x if flip_x else self.x,
            1 - self.core if flip_core else self.core,
            1 - self.y if flip_y else self.y,
        )

    def greet(self):
        barrier = pltpu.get_barrier_semaphore()
        partners = [self.along(step) for step in range(1, LONG)]
        partners += [self.across(away) for away in range(1, PLANE)]
        for partner in partners:
            pl.semaphore_signal(barrier, inc=1, device_id=partner, device_id_type=MESH)
        pl.semaphore_wait(barrier, len(partners))


def remote(source, target, send, receive, device):
    return pltpu.make_async_remote_copy(
        src_ref=source,
        dst_ref=target,
        send_sem=send,
        recv_sem=receive,
        device_id=device,
        device_id_type=MESH,
    )


GATHER_KINDS = 4 * (LONG - 1) + 4 + 1 + 2
GATHER_STAGES = 6
SPLIT = 2
SPREAD = 2
START, RECEIVE, SENT = range(3)


class Gather:
    def __init__(self, here, chunks, send, receive):
        self.here, self.chunks, self.send, self.receive = here, chunks, send, receive
        self.count = len(chunks)
        self.sets = ((here.x, here.y), here.near, here.far, (1 - here.x, 1 - here.y))

    def line_first(self, n):
        return n % 3 == 0

    def block(self, n, which, z=slice(None)):
        x, y = self.sets[which]
        return self.chunks[n].at[z, x, self.here.core, y]

    def copy(self, n, kind, block, device):
        return remote(block, block, self.send.at[n, kind], self.receive.at[n, kind], device)

    def hop(self, n, step, action):
        here, z = self.here, self.here.z
        for piece in (0,) if self.line_first(n) else (0, 1):
            kind = 6 * piece + 2 * (step - 1)

            def upward(origin, device):
                return self.copy(n, kind, self.block(n, piece, origin), device)

            def downward(origin, device):
                return self.copy(n, kind + 1, self.block(n, piece, origin), device)

            if action == RECEIVE:

                @pl.when(z - step >= 0)
                def _():
                    upward(z - step, here.down_device).wait_recv()

                @pl.when(z + step <= LONG - 1)
                def _():
                    downward(z + step, here.up_device).wait_recv()

            else:

                @pl.when(jnp.logical_and(z - step + 1 >= 0, z < LONG - 1))
                def _():
                    copy = upward(z - step + 1, here.up_device)
                    copy.start() if action == START else copy.wait_send()

                @pl.when(jnp.logical_and(z + step - 1 <= LONG - 1, z > 0))
                def _():
                    copy = downward(z + step - 1, here.down_device)
                    copy.start() if action == START else copy.wait_send()

    def twin(self, n, which):
        return self.copy(n, 12 + which, self.block(n, which), self.here.twin_device)

    def twin_back(self, n, which):
        x, y = self.sets[(0, 2, 1, 3)[which]]
        block = self.chunks[n].at[:, x, 1 - self.here.core, y]
        return self.copy(n, 12 + which, block, self.here.twin_device)

    def near(self, n, which):
        z = slice(None) if self.line_first(n) else self.here.z
        return self.copy(n, 16, self.block(n, which, z), self.here.near_device)

    def far(self, n, which, back=False):
        return self.copy(
            n, 17 + which, self.block(n, which + 2 * back), self.here.far_device
        )

    def stage(self, n, step):
        if not 0 <= n < self.count:
            return
        if step == 5:
            for which in range(2):
                self.far(n, which, True).wait_recv()
                self.twin(n, 2 + which).start()
        elif self.line_first(n):
            if step in (1, 2, 3):
                self.hop(n, step, RECEIVE)
            if step < 3:
                self.hop(n, step + 1, START)
            elif step == 3:
                self.near(n, 0).start()
                self.far(n, 0).start()
                self.twin(n, 0).start()
            else:
                self.near(n, 1).wait_recv()
                self.far(n, 1).start()
                self.twin(n, 1).start()
        elif step == 0:
            self.near(n, 0).start()
        else:
            if step == 1:
                self.near(n, 1).wait_recv()
            else:
                self.hop(n, step - 1, RECEIVE)
            if step < 4:
                self.hop(n, step, START)
            else:
                for which in range(2):
                    self.far(n, which).start()
                    self.twin(n, which).start()

    def whole(self, n):
        for which in range(4):
            self.twin_back(n, which).wait_recv()

    def finish(self):
        for n in range(self.count):
            for step in range(1, LONG):
                self.hop(n, step, SENT)
            self.near(n, 0).wait_send()
            for which in range(2):
                self.far(n, which).wait_send()
            for which in range(4):
                self.twin(n, which).wait_send()


REDUCE_KINDS = 1 + 1 + 2 * (LONG - 1)
REDUCE_STAGES = 6
RING = 9
STAGED = 3


class Reduce:
    def __init__(self, here, r, count, put):
        self.here, self.r, self.count, self.put = here, r, count, put

    def line_last(self, n):
        return n % 3 == 0

    def at(self, n):
        slot = n % RING
        return slot, slot // 3 if self.line_last(n) else slot // 3 * 2 + slot % 3 - 1

    def copy(self, n, kind, source, target, device):
        r = self.r
        return remote(source, target, r.reduce_send.at[n, kind], r.reduce_receive.at[n, kind], device)

    def far(self, n):
        r, here = self.r, self.here
        source = r.staged.at[n % STAGED, :, :, 1 - here.second]
        return self.copy(n, 0, source, r.from_far.at[n % RING], here.far_device)

    def near(self, n):
        r, here = self.r, self.here
        slot, index = self.at(n)
        if self.line_last(n):
            source, target = r.from_far.at[slot, :, 1 - here.first], r.from_near_line.at[index]
        else:
            source, target = r.from_far.at[slot, here.z, 1 - here.first], r.from_near.at[index]
        return self.copy(n, 1, source, target, here.near_device)

    def line(self, n, place):
        r = self.r
        slot, index = self.at(n)
        return r.from_near_line.at[index, place] if self.line_last(n) else r.from_far.at[slot, place]

    def landing(self, n, kind):
        r = self.r
        index = self.at(n)[1]
        return r.from_line_short.at[index, kind] if self.line_last(n) else r.from_line.at[index, kind]

    def hop(self, n, step, action):
        here, z, away = self.here, self.here.z, LONG - step
        kind = 2 * (step - 1)

        @pl.when(z - away >= 0)
        def _():
            copy = self.copy(
                n, 2 + kind, self.line(n, z - away), self.landing(n, kind), here.down_device
            )
            copy.start() if action == START else copy.wait_send()

        @pl.when(z + away <= LONG - 1)
        def _():
            copy = self.copy(
                n, 3 + kind, self.line(n, z + away), self.landing(n, kind + 1), here.up_device
            )
            copy.start() if action == START else copy.wait_send()

    def hop_in(self, n, step):
        here, z, away = self.here, self.here.z, LONG - step
        kind = 2 * (step - 1)
        for side, place, there, device in (
            (0, z - away + 1, jnp.logical_and(z < LONG - 1, z - away + 1 >= 0), here.up_device),
            (1, z + away - 1, jnp.logical_and(z > 0, z + away - 1 <= LONG - 1), here.down_device),
        ):

            @pl.when(there)
            def _():
                landed = self.landing(n, kind + side)
                self.copy(n, 2 + kind + side, landed, landed, device).wait_recv()
                total = self.line(n, place)
                if self.line_last(n):
                    add_up(total, landed)
                else:
                    for part in range(SHORT):
                        add_up(total.at[part], landed.at[part])

    def credit(self, n, kind, condition=None):
        if n < RING:
            return

        def take():
            pl.semaphore_wait(self.r.credit.at[n - RING, kind], 1)

        take() if condition is None else pl.when(condition)(take)

    def give(self, n):
        if n + RING >= self.count:
            return
        here, r = self.here, self.r

        def signal(kind, device):
            pl.semaphore_signal(r.credit.at[n, kind], inc=1, device_id=device, device_id_type=MESH)

        self.near(n).wait_send()
        for step in range(1, LONG):
            self.hop(n, step, SENT)
        signal(0, here.far_device)
        signal(1, here.near_device)
        pl.when(here.z < LONG - 1)(lambda: signal(2, here.up_device))
        pl.when(here.z > 0)(lambda: signal(3, here.down_device))

    def first_hop(self, n):
        self.credit(n, 3, self.here.z < LONG - 1)
        self.credit(n, 2, self.here.z > 0)
        self.hop(n, 1, START)

    def free(self, n):
        if n >= STAGED:
            self.far(n - STAGED).wait_send()

    def stage(self, n, step):
        if not 0 <= n < self.count:
            return
        r, here = self.r, self.here
        slot, index = self.at(n)
        if step == 0:
            self.credit(n, 0)
            self.far(n).start()
            return
        if step == 1:
            self.far(n).wait_recv()

            def one(at, carry):
                add_up(
                    r.from_far.at[slot, at // 2, at % 2],
                    r.staged.at[n % STAGED, at // 2, at % 2, here.second],
                )
                return carry

            lax.fori_loop(0, LONG * SHORT, one, 0)
            if self.line_last(n):
                self.credit(n, 1)
                self.near(n).start()
            else:
                self.first_hop(n)
        elif self.line_last(n):
            if step == 2:
                self.near(n).wait_recv()

                def one(at, carry):
                    add_up(r.from_near_line.at[index, at], r.from_far.at[slot, at, here.first])
                    return carry

                lax.fori_loop(0, LONG, one, 0)
                self.first_hop(n)
            else:
                self.hop_in(n, step - 2)
                if step < 5:
                    self.hop(n, step - 1, START)
                else:
                    self.put(n, r.from_near_line[index, here.z].astype(jnp.float32))
                    self.give(n)
        elif step < 5:
            self.hop_in(n, step - 1)
            if step < 4:
                self.hop(n, step, START)
            else:
                self.credit(n, 1)
                self.near(n).start()
        else:
            self.near(n).wait_recv()
            own = r.from_far[slot, here.z, here.first].astype(jnp.float32)
            self.put(n, own + r.from_near[index].astype(jnp.float32))
            self.give(n)

    def tick(self, n):
        for step in range(REDUCE_STAGES):
            self.stage(n - step, step)

    def finish(self):
        for n in range(max(0, self.count - STAGED), self.count):
            self.far(n).wait_send()
        for n in range(max(0, self.count - RING), self.count):
            self.near(n).wait_send()
            for step in range(1, LONG):
                self.hop(n, step, SENT)


def add_up(target, source):
    total = target[...].astype(jnp.float32) + source[...].astype(jnp.float32)
    target[...] = total.astype(target.dtype)


class Meeting:
    def __init__(self, here, value, line, plane, send, receive):
        self.here, self.value, self.line, self.plane = here, value, line, plane
        self.send, self.receive = send, receive
        self.place = here.x * 4 + here.core * 2 + here.y

    def along(self, step, back=False):
        here = self.here
        place = (here.z - step) % LONG if back else here.z
        return remote(
            self.line.at[place] if back else self.value,
            self.line.at[place],
            self.send.at[step - 1],
            self.receive.at[step - 1],
            here.along(step),
        )

    def across(self, away, back=False):
        here = self.here
        place = self.place
        if back:
            x = 1 - here.x if away // 4 else here.x
            core = 1 - here.core if away // 2 % 2 else here.core
            y = 1 - here.y if away % 2 else here.y
            place = x * 4 + core * 2 + y
        block = self.plane.at[place]
        number = LONG - 2 + away
        return remote(
            block, block, self.send.at[number], self.receive.at[number], here.across(away)
        )

    def step(self, k):
        if k == 0:
            self.line[self.here.z] = self.value[...]
            for away in range(1, LONG):
                self.along(away).start()
            return None
        if k == 1:
            for away in range(1, LONG):
                self.along(away).wait_send()
                self.along(away, True).wait_recv()
            total = self.line[0]
            for place in range(1, LONG):
                total = total + self.line[place]
            self.plane[self.place] = total
            for away in range(1, PLANE):
                self.across(away).start()
            return None
        for away in range(1, PLANE):
            self.across(away).wait_send()
            self.across(away, True).wait_recv()
        total = self.plane[0]
        for place in range(1, PLANE):
            total = total + self.plane[place]
        return total


TILE = 256
LANES = 128
FORWARD_BUDGET = 1.5
VECTOR_TICKS = (0, 7, 9)
TURNED, LANDED = "turned_", "landed_"
BAND = 32
CROSS_Q, CROSS_K, CROSS_V, CROSS_O, SELF_Q, SELF_K, SELF_V, SELF_O, UP = range(9)


def tile(start, size):
    return pl.ds(pl.multiple_of(start, size), size)


def bands(rows, body, carry=0):
    return lax.fori_loop(0, rows // BAND, lambda k, c: body(tile(k * BAND, BAND), c), carry, unroll=4)


def normalised(values):
    centre = values - jnp.mean(values, axis=-1, keepdims=True)
    inverse = lax.rsqrt(jnp.mean(centre * centre, axis=-1, keepdims=True) + norm_eps)
    return centre * inverse, inverse


def block_kernel(names, sizes, *refs):
    r = types.SimpleNamespace(**dict(zip(names, refs, strict=True)))
    width, lat, pix, hidden_parts, threshold = sizes
    f32, bf16 = jnp.float32, jnp.bfloat16
    here = Place()
    core = here.core
    scale = (width // HEADS) ** (-0.5)
    panel_blocks = UP + hidden_parts
    gather_order = [CROSS_K, CROSS_V, CROSS_Q, CROSS_O, SELF_Q, SELF_K, SELF_V, SELF_O]
    gather_order += list(range(UP, panel_blocks))
    share_rows = r.panel.shape[0]

    meet_in = Meeting(here, r.vectors, r.meet_line, r.meet_plane, r.meet_send, r.meet_receive)
    meet_out = Meeting(here, r.vector_grad, r.sum_line, r.sum_plane, r.sum_send, r.sum_receive)
    meet_last = Meeting(here, r.squares, r.last_line, r.last_plane, r.last_send, r.last_receive)

    chunks, keep = [], []

    def keep_own(low, whole):
        own = whole.at[here.z, here.x, core, here.y]
        keep.append(pltpu.make_async_copy(low, own, r.own.at[len(keep)]))
        keep[-1].start()

    for block in gather_order:
        columns = pl.ds(block * width, width)
        r.low_panel[:, columns] = r.panel[:, columns].astype(bf16)
        keep_own(r.low_panel.at[:, columns], r.whole_panel.at[:, :, :, :, :, columns])
        for part in range(SPLIT):
            columns = pl.ds(block * width + part * width // SPLIT, width // SPLIT)
            chunks.append(r.whole_panel.at[:, :, :, :, :, columns])
    for block in range(hidden_parts):
        rows = pl.ds(block * share_rows, share_rows)
        r.low_down[rows, :] = r.down[rows, :].astype(bf16)
        keep_own(r.low_down.at[rows], r.whole_down.at[:, :, :, :, rows])
        for part in range(SPLIT):
            rows = pl.ds(block * share_rows + part * share_rows // SPLIT, share_rows // SPLIT)
            chunks.append(r.whole_down.at[:, :, :, :, rows])
    gather = Gather(here, chunks, r.gather_send, r.gather_receive)
    here.greet()

    def gather_tick(tick):
        if tick % SPLIT == 0 and tick < len(chunks):
            keep[tick // SPLIT].wait()
        for step in range(GATHER_STAGES):
            gather.stage(tick - SPREAD * step, step)

    twins = {}

    def to_twin(source, target):
        number = len(twins)
        copy = remote(
            source, target, r.twin_send.at[number], r.twin_receive.at[number], here.twin_device
        )
        copy.start()
        twins[number] = copy
        return number

    def from_twin(number):
        twins[number].wait_recv()

    flat_panel = r.whole_panel.reshape(-1, panel_blocks * width)
    flat_down = r.whole_down.reshape(-1, width)
    loads = []

    def fetch(part):
        if isinstance(part, tuple):
            source = flat_down.at[pl.ds(part[1] * width, width)]
        else:
            source = flat_panel.at[:, pl.ds(part * width, width)]
        slot = len(loads) % 2
        copy = pltpu.make_async_copy(source, r.weights.at[slot], r.load.at[slot])
        copy.start()
        loads.append(copy)
        return len(loads) - 1

    def fetched(number):
        loads[number].wait()
        return number % 2

    def put(n, value):
        if n < hidden_parts:
            r.down_share[n * share_rows : (n + 1) * share_rows, :] = value
        else:
            block = reduce_order[n]
            r.panel_share[:, block * width : (block + 1) * width] = value
        square = value * value
        gained = r.squares[...]
        for across in range(0, width, LANES):
            for at in range(0, share_rows, 8):
                gained = gained + square[at : at + 8, across : across + LANES]
        r.squares[...] = gained

    reduce_order = [None] * hidden_parts + list(range(UP, panel_blocks))
    reduce_order += [SELF_O, SELF_Q, SELF_K, SELF_V, CROSS_O, CROSS_Q, CROSS_K, CROSS_V]
    reduce = Reduce(here, r, len(reduce_order), put)

    def vector(k):
        return r.rows[k : k + 1, :]

    def times(left, slot, emit):
        def one(k, carry):
            columns = tile(k * TILE, TILE)
            emit(columns, jnp.dot(left[...], r.weights[slot, :, columns], preferred_element_type=f32))
            return carry

        lax.fori_loop(0, width // TILE, one, 0, unroll=4)

    def times_back(left, slot, emit):
        def one(k, carry):
            columns = tile(k * TILE, TILE)
            emit(columns, times_transposed(left[...], r.weights[slot, columns, :]))
            return carry

        lax.fori_loop(0, width // TILE, one, 0, unroll=4)

    def norm_rows(read, count, gain, shift, target):
        def one(rows, carry):
            normed, _ = normalised(read(rows))
            target[rows, :] = (normed * vector(gain) + vector(shift)).astype(bf16)
            return carry

        bands(count, one)

    def keep_vector(k, value):
        for at in range(width // LANES):
            row = k * (width // LANES) + at
            r.vector_grad[row : row + 1, :] = value[:, at * LANES : (at + 1) * LANES]

    def folded(value):
        total = value[0:8]
        for at in range(8, BAND, 8):
            total = total + value[at : at + 8]
        return total

    def norm_back(read, grad, count, gain, shift, emit):
        def one(rows, carry):
            gain_sum, shift_sum = carry
            normed, inverse = normalised(read(rows))
            out = grad[rows, :]
            if emit is not None:
                inner = out * vector(gain)
                emit(
                    rows,
                    inverse
                    * (
                        inner
                        - jnp.mean(inner, axis=-1, keepdims=True)
                        - normed * jnp.mean(inner * normed, axis=-1, keepdims=True)
                    ),
                )
            return gain_sum + folded(out * normed), shift_sum + folded(out)

        empty = jnp.zeros((8, width), f32)
        gain_sum, shift_sum = bands(count, one, (empty, empty))
        keep_vector(gain, jnp.sum(gain_sum, axis=0, keepdims=True))
        keep_vector(shift, jnp.sum(shift_sum, axis=0, keepdims=True))

    head = width // HEADS

    def probabilities(queries, keys, masked):
        scores = times_transposed(queries, keys) * scale
        if masked:
            scores = jnp.where(r.mask[0:1, :] > 0.5, scores, masked_fill)
        powers = jnp.exp(scores - jnp.max(scores, axis=-1, keepdims=True))
        return powers / jnp.sum(powers, axis=-1, keepdims=True)

    def attend(heads, queries, keys, key_start, values, value_start, masked, target):
        def one(k, carry):
            columns = tile(k * head, head)
            probability = probabilities(
                queries[:, columns], keys[:, tile(key_start + k * head, head)], masked
            )
            value_rows = values[:, tile(value_start + k * head, head)]
            target[:, columns] = matmul_low(probability.astype(bf16), value_rows).astype(bf16)
            return carry

        lax.fori_loop(*heads, one, 0, unroll=HEADS // 2)

    def attend_back(grad, queries, keys, key_start, values, value_start, masked, targets):
        query_grad, key_grad, key_at, value_grad, value_at = targets

        def one(k, carry):
            columns = tile(k * head, head)
            key_columns = tile(key_start + k * head, head)
            value_columns = tile(value_start + k * head, head)
            query_rows, key_rows = queries[:, columns], keys[:, key_columns]
            probability = probabilities(query_rows, key_rows, masked)
            grad_mix = grad[:, columns]
            grad_prob = times_transposed(grad_mix, values[:, value_columns])
            inner = jnp.sum(grad_prob * probability, axis=-1, keepdims=True)
            grad_scores = (probability * (grad_prob - inner)).astype(bf16)
            query_grad[:, columns] = (matmul_low(grad_scores, key_rows) * scale).astype(bf16)
            key_grad[:, tile(key_at + k * head, head)] = (
                rows_inner(grad_scores, query_rows) * scale
            ).astype(bf16)
            value_grad[:, tile(value_at + k * head, head)] = rows_inner(
                probability.astype(bf16), grad_mix
            ).astype(bf16)
            return carry

        lax.fori_loop(0, HEADS, one, 0, unroll=4)

    row_id = lax.broadcasted_iota(jnp.int32, (LANES, LANES), 0)
    unit = (row_id == lax.broadcasted_iota(jnp.int32, (LANES, LANES), 1)).astype(bf16)

    def turn(source, target, landing):
        def one(k, carry):
            turned = times_transposed(unit, source[:, tile(k * LANES, LANES)]).astype(bf16)
            for side in range(2):
                target[side, k] = turned[side * LANES // 2 : (side + 1) * LANES // 2]
            return carry

        lax.fori_loop(0, width // LANES, one, 0, unroll=8)
        return to_twin(target.at[1 - core], landing)

    def weight_grad(n, own, other, grad, grad_other, start):
        reduce.free(n)
        slot = n % STAGED

        def one(k, carry):
            columns = tile(start + k * TILE, TILE)
            total = matmul_low(own(), grad[:, columns]) + matmul_low(other(), grad_other[:, columns])
            total = total.astype(bf16).reshape(LONG, SHORT, SHORT, share_rows, TILE)
            into = tile(k * TILE, TILE)
            for to_x in range(SHORT):
                for to_y in range(SHORT):
                    first = jnp.where(core == 0, to_x, to_y)
                    second = jnp.where(core == 0, to_y, to_x)
                    r.staged[slot, :, first, second, :, into] = total[:, to_x, to_y]
            return carry

        lax.fori_loop(0, width // TILE, one, 0, unroll=4)

    def turned_pair(target, landing):
        rows = target.shape[3]
        return (
            lambda: target[core].reshape(-1, rows),
            lambda: landing[...].reshape(-1, rows),
        )

    marks = types.SimpleNamespace()

    def set_rows(total):
        per = width // LANES
        for row in range(r.rows.shape[0]):
            for at in range(per):
                line = total[row * per + at : row * per + at + 1, :]
                r.rows[row : row + 1, at * LANES : (at + 1) * LANES] = line.astype(bf16).astype(f32)

    def after_vectors():
        yield 0.5, lambda: norm_rows(
            lambda rows: r.pixels[rows, :].astype(f32), pix, 0, 1, r.pixel_low
        )
        yield 0.9, lambda: norm_rows(
            lambda rows: r.latents[rows, :].astype(f32), lat, 2, 3, r.left
        )
        yield 0.4, lambda: mark_turn("pixel", r.pixel_low)
        yield 0.5, lambda: mark_turn("cross", r.left)

    def to_columns(target, start=0):
        def emit(columns, value):
            where = pl.ds(pl.multiple_of(columns.start + start, TILE), TILE)
            target[:, where] = value.astype(bf16)

        return emit

    def add_columns(target, base):
        def emit(columns, value):
            target[:, columns] = base[:, columns].astype(f32) + value

        return emit

    def mark_turn(name, source):
        landing = getattr(r, LANDED + name)
        setattr(marks, name, turn(source, getattr(r, TURNED + name), landing))

    halves = ((0, HEADS // 2), (HEADS // 2, HEADS))

    def forward(block, number):
        if block in (CROSS_K, CROSS_V):
            emit = to_columns(r.pair, (block - CROSS_K) * width)
            yield 0.6, lambda: times(r.pixel_low, fetched(number), emit)
        elif block == CROSS_Q:
            yield 0.8, lambda: times(r.left, fetched(number), to_columns(r.cross_query))
            for heads in halves:
                yield 1.0, functools.partial(
                    attend, heads, r.cross_query, r.pair, 0, r.pair, width, True, r.mixed
                )
            yield 0.5, lambda: mark_turn("cross_mix", r.mixed)
        elif block == CROSS_O:
            yield 0.8, lambda: times(r.mixed, fetched(number), add_columns(r.first, r.latents))
            yield 0.8, lambda: norm_rows(lambda rows: r.first[rows, :], lat, 4, 5, r.left)
            yield 0.5, lambda: mark_turn("self", r.left)
        elif block in (SELF_Q, SELF_K, SELF_V):
            emit = to_columns(r.triple, (block - SELF_Q) * width)
            yield 0.8, lambda: times(r.left, fetched(number), emit)
            if block == SELF_V:
                for heads in halves:
                    yield 1.5, functools.partial(
                        attend, heads, r.triple, r.triple, width, r.triple, 2 * width, False, r.mixed
                    )
                yield 0.5, lambda: mark_turn("self_mix", r.mixed)
        elif block == SELF_O:
            yield 0.8, lambda: times(r.mixed, fetched(number), add_columns(r.second, r.first))
            yield 0.8, lambda: norm_rows(lambda rows: r.second[rows, :], lat, 6, 7, r.left)
            yield 0.5, lambda: mark_turn("feed", r.left)
        else:
            part = block - UP

            def emit(columns, value):
                upper = value + r.rows[9 + part : 10 + part, columns]
                below = 0.5 + 0.5 * lax.erf(upper * (0.5**0.5))
                where = pl.ds(pl.multiple_of(columns.start + part * width, TILE), TILE)
                r.hidden[:, where] = (upper * below).astype(bf16)
                density = jnp.exp(-0.5 * upper * upper) * ((2.0 * math.pi) ** -0.5)
                r.slope[:, where] = below + upper * density

            def one(k, carry):
                block_at = part * (width // LANES) + k
                turned = times_transposed(unit, r.hidden[:, tile(block_at * LANES, LANES)])
                turned = turned.astype(bf16).reshape(hidden_parts, share_rows, lat)
                side = (k // 2) % 2
                r.turned_hidden[side, block_at // 4 * 2 + k % 2] = turned
                return carry

            yield 1.5, lambda: times(r.left, fetched(number), emit)
            yield 0.6, lambda: lax.fori_loop(0, width // LANES, one, 0, unroll=8)

    forward_blocks = len(gather_order)
    ticks = len(chunks) + SPREAD * (GATHER_STAGES - 1)
    arrival = SPLIT - 1 + SPREAD * (GATHER_STAGES - 1) + 1
    todo, taken = [], 0

    def work(budget, until=None):
        nonlocal taken
        spent = 0.0
        while taken < len(todo) and (spent < budget or (until is not None and taken < until)):
            cost, step = todo[taken]
            taken += 1
            step()
            spent += cost

    tick, fetch_next, ends = 0, 0, []
    while fetch_next < forward_blocks:
        gather_tick(tick)
        if tick in VECTOR_TICKS:
            total = meet_in.step(VECTOR_TICKS.index(tick))
            if tick == VECTOR_TICKS[2]:
                set_rows(total)
                todo.extend(after_vectors())
        elif tick == VECTOR_TICKS[2] + 1:
            marks.dz = to_twin(r.out_grad, r.landed_dz)
        if tick >= SPLIT * fetch_next + arrival:
            if len(ends) > 1:
                work(0.0, ends[-2])
            for n in range(SPLIT * fetch_next, SPLIT * fetch_next + SPLIT):
                gather.whole(n)
            number = fetch(gather_order[fetch_next])
            work(FORWARD_BUDGET)
            todo.extend(forward(gather_order[fetch_next], number))
            ends.append(len(todo))
            fetch_next += 1
        else:
            work(FORWARD_BUDGET)
        tick += 1
    work(1e9)
    marks.hidden = to_twin(r.turned_hidden.at[1 - core], r.landed_hidden)

    r.squares[...] = jnp.zeros_like(r.squares)
    gather_tick(tick)
    tick += 1
    from_twin(marks.dz)
    from_twin(marks.hidden)

    def hidden_grad(part):
        weight_grad(
            part,
            lambda: r.turned_hidden[core, :, part].reshape(-1, lat),
            lambda: r.landed_hidden[:, part].reshape(-1, lat),
            r.out_grad,
            r.landed_dz,
            0,
        )
        reduce.tick(part)

    part = 0
    while tick < ticks:
        if part < 3:
            hidden_grad(part)
            part += 1
        for _ in range(2):
            if tick < ticks:
                gather_tick(tick)
                tick += 1
    hidden_next = part
    for n in range(SPLIT * forward_blocks, len(chunks)):
        gather.whole(n)
    number = fetch(("down", 0))

    def start_out(rows, carry):
        r.total[rows, :] = r.second[rows, :] + vector(8)
        return carry + folded(r.out_grad[rows, :].astype(f32))

    shift_sum = bands(lat, start_out, jnp.zeros((8, width), f32))
    keep_vector(8, jnp.sum(shift_sum, axis=0, keepdims=True))
    du_marks = []

    def out_and_du(part, slot):
        hidden_part = r.hidden.at[:, pl.ds(part * width, width)]

        def emit(columns, value):
            r.total[:, columns] += value

        times(hidden_part, slot, emit)

        def emit_du(columns, value):
            where = pl.ds(pl.multiple_of(columns.start + part * width, TILE), TILE)
            low = (value * r.slope[:, where]).astype(bf16)
            r.hidden[:, where] = low
            column_sum = jnp.sum(low.astype(f32), axis=0, keepdims=True)
            at = 9 * (width // LANES) + part * (width // LANES) + lax.div(columns.start, LANES)
            for k in range(TILE // LANES):
                r.vector_grad[pl.ds(at + k, 1), :] = column_sum[:, k * LANES : (k + 1) * LANES]

        times_back(r.out_grad, slot, emit_du)
        du_marks.append(to_twin(hidden_part, r.landed_du.at[:, pl.ds(part * width, width)]))

    for part in range(hidden_parts):
        slot = fetched(number)
        number = fetch(("down", part + 1) if part + 1 < hidden_parts else UP)
        out_and_du(part, slot)
        if hidden_next + part < hidden_parts:
            hidden_grad(hidden_next + part)

    def finish_out(rows, carry):
        r.latents_out[rows, :] = r.total[rows, :].astype(bf16)
        r.total[rows, :] = jnp.zeros((BAND, width), f32)
        return carry

    bands(lat, finish_out)

    def add_total(columns, value):
        r.total[:, columns] += value

    from_twin(marks.feed)
    own, other = turned_pair(r.turned_feed, r.landed_feed)
    for part in range(hidden_parts):
        slot = fetched(number)
        number = fetch(UP + part + 1 if part + 1 < hidden_parts else SELF_O)
        times_back(r.hidden.at[:, pl.ds(part * width, width)], slot, add_total)
        from_twin(du_marks[part])
        n = hidden_parts + part
        weight_grad(n, own, other, r.hidden, r.landed_du, part * width)
        if part + 1 == hidden_parts:

            def into_second(rows, value):
                value = value + r.out_grad[rows, :].astype(f32)
                r.second[rows, :] = value
                r.grad_low[rows, :] = value.astype(bf16)

            norm_back(lambda rows: r.second[rows, :], r.total, lat, 6, 7, into_second)
            marks.ds = to_twin(r.grad_low, r.landed_ds)
        reduce.tick(n)

    def branch_out(n, slot, grad_low, landed, mark, turned, landed_turned, turned_mark):
        times_back(grad_low, slot, to_columns(r.mixed))
        from_twin(mark)
        from_twin(turned_mark)
        weight_grad(n, *turned_pair(turned, landed_turned), grad_low, landed, 0)

    n = 2 * hidden_parts
    slot = fetched(number)
    number = fetch(SELF_Q)
    branch_out(
        n, slot, r.grad_low, r.landed_ds, marks.ds, r.turned_self_mix, r.landed_self_mix, marks.self_mix
    )
    reduce.stage(n, 0)
    attend_back(
        r.mixed,
        r.triple,
        r.triple,
        width,
        r.triple,
        2 * width,
        False,
        (r.triple_grad, r.triple_grad, width, r.triple_grad, 2 * width),
    )
    triple_marks = []
    for part in range(3):
        columns = pl.ds(part * width, width)
        triple_marks.append(to_twin(r.triple_grad.at[:, columns], r.landed_triple.at[:, columns]))
    for step in range(1, REDUCE_STAGES):
        reduce.stage(n - step, step)

    def clear(rows, carry):
        r.total[rows, :] = jnp.zeros((BAND, width), f32)
        return carry

    bands(lat, clear)
    from_twin(marks.self)
    own, other = turned_pair(r.turned_self, r.landed_self)
    for part in range(3):
        slot = fetched(number)
        number = fetch((SELF_K, SELF_V, CROSS_O)[part])
        times_back(r.triple_grad.at[:, pl.ds(part * width, width)], slot, add_total)
        from_twin(triple_marks[part])
        n += 1
        weight_grad(n, own, other, r.triple_grad, r.landed_triple, part * width)
        if part == 2:

            def into_first(rows, value):
                value = value + r.second[rows, :]
                r.second[rows, :] = value
                r.cross_low[rows, :] = value.astype(bf16)

            norm_back(lambda rows: r.first[rows, :], r.total, lat, 4, 5, into_first)
            marks.dc = to_twin(r.cross_low, r.landed_dc)
        reduce.tick(n)

    n += 1
    slot = fetched(number)
    number = fetch(CROSS_Q)
    branch_out(
        n, slot, r.cross_low, r.landed_dc, marks.dc, r.turned_cross_mix, r.landed_cross_mix, marks.cross_mix
    )
    reduce.stage(n, 0)
    attend_back(
        r.mixed,
        r.cross_query,
        r.pair,
        0,
        r.pair,
        width,
        True,
        (r.query_grad, r.pair_grad, 0, r.pair_grad, width),
    )
    query_mark = to_twin(r.query_grad, r.landed_query)
    pair_marks = []
    for part in range(2):
        columns = pl.ds(part * width, width)
        pair_marks.append(to_twin(r.pair_grad.at[:, columns], r.landed_pair.at[:, columns]))
    for step in range(1, REDUCE_STAGES):
        reduce.stage(n - step, step)

    slot = fetched(number)
    number = fetch(CROSS_K)

    def set_total(columns, value):
        r.total[:, columns] = value

    times_back(r.query_grad, slot, set_total)
    from_twin(query_mark)
    from_twin(marks.cross)
    n += 1
    weight_grad(n, *turned_pair(r.turned_cross, r.landed_cross), r.query_grad, r.landed_query, 0)
    reduce.stage(n, 0)

    def into_latents(rows, value):
        r.latents_grad[rows, :] = value + r.second[rows, :]

    norm_back(lambda rows: r.latents[rows, :].astype(f32), r.total, lat, 2, 3, into_latents)
    for step in range(1, REDUCE_STAGES):
        reduce.stage(n - step, step)
    from_twin(marks.pixel)
    own, other = turned_pair(r.turned_pixel, r.landed_pixel)
    pixel_total = r.total.at[pl.ds(0, pix)]

    for part in range(2):
        slot = fetched(number)
        if part == 0:
            number = fetch(CROSS_V)

        def emit_pixel(columns, value):
            if part == 0:
                pixel_total[:, columns] = value
            else:
                pixel_total[:, columns] += value

        times_back(r.pair_grad.at[:, pl.ds(part * width, width)], slot, emit_pixel)
        from_twin(pair_marks[part])
        n += 1
        weight_grad(n, own, other, r.pair_grad, r.landed_pair, part * width)
        reduce.stage(n, 0)
        if part == 1:
            norm_back(lambda rows: r.pixels[rows, :].astype(f32), pixel_total, pix, 0, 1, None)
            meet_out.step(0)
        for step in range(1, REDUCE_STAGES):
            reduce.stage(n - step, step)
    for k in range(1, REDUCE_STAGES):
        if k == 1:
            meet_out.step(1)
        elif k == 3:
            total = meet_out.step(2)
            r.vector_share[...] = total
            vector_squares = jnp.sum(total * total)
        reduce.tick(n + k)
    for k in range(3):
        total = meet_last.step(k)
    norm = jnp.sqrt(jnp.zeros((8, LANES), f32) + (jnp.sum(total) + vector_squares))
    r.norms[0] = norm
    r.norms[1] = threshold / jnp.maximum(norm, threshold)
    reduce.finish()
    gather.finish()
    for copy in twins.values():
        copy.wait_send()


def run_block(latents, pixels, mask, out_grad, panel, down, vectors, threshold):
    f32, bf16 = jnp.float32, jnp.bfloat16
    lat, width = latents.shape
    pix = pixels.shape[0]
    share_rows = panel.shape[0]
    hidden_parts = down.shape[0] // share_rows
    wide = hidden_parts * width
    half = LANES // 2
    blocks = panel.shape[1] // width
    chunks = blocks + hidden_parts
    unit = (share_rows, width)
    vmem = pltpu.VMEM
    dma, any_space = pltpu.SemaphoreType.DMA, pl.BlockSpec(memory_space=pl.ANY)
    in_vmem = pl.BlockSpec(memory_space=pltpu.VMEM)
    inputs = dict(
        latents=latents,
        pixels=pixels,
        mask=mask,
        out_grad=out_grad,
        panel=panel,
        down=down,
        vectors=vectors,
    )
    outputs = dict(
        latents_out=((lat, width), bf16),
        latents_grad=((lat, width), f32),
        panel_share=(panel.shape, f32),
        down_share=(down.shape, f32),
        vector_share=(vectors.shape, f32),
        norms=((2, 8, LANES), f32),
        whole_panel=(CUT + panel.shape, bf16),
        whole_down=(CUT + down.shape, bf16),
    )
    groups = width // LANES
    lines = -(-RING // 3)
    scratch = dict(
        low_panel=vmem(panel.shape, bf16),
        low_down=vmem(down.shape, bf16),
        weights=vmem((2, width, width), bf16),
        rows=vmem((vectors.shape[0] // groups, width), f32),
        pixel_low=vmem((pix, width), bf16),
        left=vmem((lat, width), bf16),
        mixed=vmem((lat, width), bf16),
        cross_query=vmem((lat, width), bf16),
        pair=vmem((pix, 2 * width), bf16),
        first=vmem((lat, width), f32),
        triple=vmem((lat, 3 * width), bf16),
        second=vmem((lat, width), f32),
        hidden=vmem((lat, wide), bf16),
        slope=vmem((lat, wide), f32),
        total=vmem((lat, width), f32),
        grad_low=vmem((lat, width), bf16),
        cross_low=vmem((lat, width), bf16),
        triple_grad=vmem((lat, 3 * width), bf16),
        query_grad=vmem((lat, width), bf16),
        pair_grad=vmem((pix, 2 * width), bf16),
        vector_grad=vmem(vectors.shape, f32),
        squares=vmem((8, LANES), f32),
        turned_pixel=vmem((2, groups, half, pix), bf16),
        landed_pixel=vmem((groups, half, pix), bf16),
        turned_hidden=vmem((2, wide // LANES // 2, hidden_parts, share_rows, lat), bf16),
        landed_hidden=vmem((wide // LANES // 2, hidden_parts, share_rows, lat), bf16),
        landed_dz=vmem((lat, width), bf16),
        landed_du=vmem((lat, wide), bf16),
        landed_ds=vmem((lat, width), bf16),
        landed_triple=vmem((lat, 3 * width), bf16),
        landed_dc=vmem((lat, width), bf16),
        landed_query=vmem((lat, width), bf16),
        landed_pair=vmem((pix, 2 * width), bf16),
        staged=vmem((STAGED, LONG, SHORT, SHORT) + unit, bf16),
        from_far=vmem((RING, LONG, SHORT) + unit, bf16),
        from_near_line=vmem((lines, LONG) + unit, bf16),
        from_near=vmem((RING - lines,) + unit, bf16),
        from_line_short=vmem((lines, 2 * (LONG - 1)) + unit, bf16),
        from_line=vmem((RING - lines, 2 * (LONG - 1), SHORT) + unit, bf16),
        own=dma((chunks,)),
        load=dma((2,)),
        gather_send=dma((chunks * SPLIT, GATHER_KINDS)),
        gather_receive=dma((chunks * SPLIT, GATHER_KINDS)),
        reduce_send=dma((chunks, REDUCE_KINDS)),
        reduce_receive=dma((chunks, REDUCE_KINDS)),
        twin_send=dma((16 + hidden_parts,)),
        twin_receive=dma((16 + hidden_parts,)),
        credit=pltpu.SemaphoreType.REGULAR((chunks - RING, 4)),
    )
    for name in ("cross", "cross_mix", "self", "self_mix", "feed"):
        scratch[TURNED + name] = vmem((2, groups, half, lat), bf16)
        scratch[LANDED + name] = vmem((groups, half, lat), bf16)
    for name, shape in (("meet", vectors.shape), ("sum", vectors.shape), ("last", (8, LANES))):
        scratch[name + "_line"] = vmem((LONG,) + shape, f32)
        scratch[name + "_plane"] = vmem((PLANE,) + shape, f32)
        scratch[name + "_send"] = dma((LONG + PLANE - 2,))
        scratch[name + "_receive"] = dma((LONG + PLANE - 2,))
    names = tuple(inputs) + tuple(outputs) + tuple(scratch)
    sizes = (width, lat, pix, hidden_parts, threshold)
    results = pl.pallas_call(
        functools.partial(block_kernel, names, sizes),
        out_shape=[jax.ShapeDtypeStruct(*spec) for spec in outputs.values()],
        in_specs=[in_vmem] * len(inputs),
        out_specs=[in_vmem] * 6 + [any_space] * 2,
        scratch_shapes=list(scratch.values()),
        compiler_params=pltpu.CompilerParams(
            collective_id=0, has_side_effects=True, vmem_limit_bytes=VMEM_LIMIT
        ),
    )(*inputs.values())
    return results[:6]


ADAM_STEPS = 4


def adam_kernel(norms, *refs):
    factor = norms[1, 0:1, 0:1]
    ins, outs = refs[:10], refs[10:]
    for at in range(2):
        grad, weight, moment, square = ins[4 * at : 4 * at + 4]
        after = adam_update(
            weight[...], moment[...], square[...], grad[...] * factor, rate_matrix, weight_decay
        )
        for out, value in zip(outs[3 * at : 3 * at + 3], after):
            out[...] = value
    for out, value in zip(outs[6:], ins[8:]):
        out[...] = value[...]


def adam_all(norms, panels, downs, passed):
    columns = panels[0].shape[1] // ADAM_STEPS
    in_columns = pl.BlockSpec((panels[0].shape[0], columns), lambda k: (0, k))

    def in_rows(array):
        return pl.BlockSpec((array.shape[0] // ADAM_STEPS, array.shape[1]), lambda k: (k, 0))

    arrays = panels + downs + passed
    specs = [in_columns] * 4 + [in_rows(array) for array in downs + passed]
    keep = [1, 2, 3, 5, 6, 7, 8, 9]
    return pl.pallas_call(
        adam_kernel,
        grid=(ADAM_STEPS,),
        out_shape=[jax.ShapeDtypeStruct(arrays[k].shape, arrays[k].dtype) for k in keep],
        in_specs=[pl.BlockSpec(norms.shape, lambda k: (0, 0, 0))] + specs,
        out_specs=[specs[k] for k in keep],
    )(norms, *arrays)


def fast_step(
    latents,
    pixels,
    visible,
    out_grad,
    panel,
    panel_moment,
    panel_square,
    down,
    down_moment,
    down_square,
    vectors,
    vector_moment,
    vector_square,
):
    latent_count, model_width = latents.shape[1:]
    pixel_count = pixels.shape[1]
    device_total = lax.axis_size(("dp", "fsdp"))
    own_start = lax.axis_index(("dp", "fsdp")) * vectors.shape[0]
    vector_total = vectors.shape[0] * device_total
    own_vectors = lax.dynamic_update_slice(
        jnp.zeros((vector_total,), jnp.float32), vectors, (own_start,)
    )
    mask = jnp.arange(pixel_count, dtype=jnp.int32)[None, :] < visible[:, None]
    mask = jnp.broadcast_to(mask.astype(jnp.float32), (8, pixel_count))
    token_total = latents.shape[0] * latent_count * device_total
    param_total = device_total * (panel.size + down.size + vectors.size)
    threshold = clip_coeff * (token_total * param_total) ** 0.5
    latents_out, latents_grad, panel_share, down_share, vector_sum, norms = run_block(
        latents.reshape(-1, model_width),
        pixels.reshape(-1, model_width),
        mask,
        out_grad.reshape(-1, model_width),
        panel,
        down,
        own_vectors.reshape(-1, LANES),
        threshold,
    )
    vector_share = lax.dynamic_slice(vector_sum.reshape(-1), (own_start,), vectors.shape)
    grad_norm, factor = norms[0, 0, 0], norms[1, 0, 0]
    *after, latents_grad, latents_out = adam_all(
        norms,
        [panel_share, panel, panel_moment, panel_square],
        [down_share, down, down_moment, down_square],
        [latents_grad, latents_out],
    )
    return (
        latents_out.reshape(latents.shape),
        latents_grad.reshape(latents.shape),
        grad_norm,
        *after,
        *adam_update(vectors, vector_moment, vector_square, vector_share * factor, rate_vector, 0.0),
    )


def slow_gather(panel, down, vectors):
    model_width = panel.shape[1] // 12
    bf16 = jnp.bfloat16
    parts = [panel[:, k * 4 * model_width : (k + 1) * 4 * model_width].astype(bf16) for k in range(3)]
    parts += [down.astype(bf16), vectors.astype(bf16)]
    return [lax.all_gather(part, ("dp", "fsdp"), axis=0, tiled=True) for part in parts]


def slow_reduce(pieces, down_grad, vector_grad, share_length):
    shares = [
        lax.psum_scatter(grad, ("dp", "fsdp"), scatter_dimension=0, tiled=True)
        for grad in (jnp.concatenate(pieces, axis=1), down_grad, vector_grad)
    ]
    squares = lax.psum(sum(jnp.sum(share * share) for share in shares), ("dp", "fsdp"))
    return (*shares, squares)


def shards(
    gather,
    reduce,
    latents,
    pixels,
    visible,
    out_grad,
    panel,
    panel_moment,
    panel_square,
    down,
    down_moment,
    down_square,
    vectors,
    vector_moment,
    vector_square,
):
    images, latent_count, model_width = latents.shape
    pixel_count = pixels.shape[1]
    bf16 = jnp.bfloat16
    cross_columns, self_columns, up_columns, full_down, full_vector = gather(panel, down, vectors)
    vector_float = full_vector.astype(jnp.float32)
    gain_pixel = vector_slot(vector_float, 0, model_width)
    shift_pixel = vector_slot(vector_float, 1, model_width)
    gain_cross = vector_slot(vector_float, 2, model_width)
    shift_cross = vector_slot(vector_float, 3, model_width)
    gain_self = vector_slot(vector_float, 4, model_width)
    shift_self = vector_slot(vector_float, 5, model_width)
    gain_feed = vector_slot(vector_float, 6, model_width)
    shift_feed = vector_slot(vector_float, 7, model_width)
    bias_down = vector_slot(vector_float, 8, model_width)
    bias_up = vector_float[9 * model_width :]
    latent_rows = latents.reshape(-1, model_width).astype(jnp.float32)
    pixel_rows = pixels.reshape(-1, model_width).astype(jnp.float32)
    pixel_out, pixel_normed, pixel_inverse = norm_forward(pixel_rows, gain_pixel, shift_pixel)
    pixel_low = pixel_out.astype(bf16)
    cross_out, cross_normed, cross_inverse = norm_forward(latent_rows, gain_cross, shift_cross)
    cross_low = cross_out.astype(bf16)
    cross_queries = matmul_low(cross_low, cross_columns[:, :model_width]).astype(bf16)
    pair_rows = matmul_low(pixel_low, cross_columns[:, model_width : 3 * model_width]).astype(bf16)
    visible_mask = jnp.arange(pixel_count, dtype=jnp.int32)[None, :] < visible[:, None]
    query_heads = to_heads(cross_queries, images, HEADS)
    key_heads = to_heads(pair_rows[:, :model_width], images, HEADS)
    value_heads = to_heads(pair_rows[:, model_width:], images, HEADS)
    cross_mix, cross_top, cross_total = attend_forward(
        query_heads, key_heads, value_heads, visible_mask
    )
    cross_mixed = cross_mix.reshape(-1, model_width)
    first_sum = latent_rows + matmul_low(
        cross_mixed, cross_columns[:, 3 * model_width :]
    )
    forward_saved = self_forward(first_sum, self_columns, gain_self, shift_self, images)
    second_sum = first_sum + matmul_low(forward_saved[6], self_columns[:, 3 * model_width :])
    feed_out, feed_normed, feed_inverse = norm_forward(second_sum, gain_feed, shift_feed)
    feed_low = feed_out.astype(bf16)
    upper_in = matmul_low(feed_low, up_columns) + bias_up
    hidden_float, gelu_back = jax.vjp(gelu_exact, upper_in)
    hidden = hidden_float.astype(bf16)
    result = second_sum + (matmul_low(hidden, full_down) + bias_down)
    latents_out = result.astype(bf16).reshape(latents.shape)
    grad_three = out_grad.reshape(-1, model_width).astype(jnp.float32)
    grad_branch = grad_three.astype(bf16)
    grad_down = rows_inner(hidden, grad_branch)
    grad_bias_down = jnp.sum(grad_branch.astype(jnp.float32), axis=0)
    grad_upper = gelu_back(times_transposed(grad_branch, full_down))[0].astype(bf16)
    grad_up = rows_inner(feed_low, grad_upper)
    grad_bias_up = jnp.sum(grad_upper.astype(jnp.float32), axis=0)
    grad_feed, grad_gain_feed, grad_shift_feed = norm_backward(
        times_transposed(grad_upper, up_columns),
        feed_normed,
        feed_inverse,
        gain_feed,
    )
    grad_two = grad_three + grad_feed
    (
        self_normed,
        self_inverse,
        self_low,
        self_queries,
        self_keys,
        self_values,
        self_mixed,
        self_top,
        self_total,
    ) = forward_saved
    grad_self_branch = grad_two.astype(bf16)
    grad_self_out = rows_inner(self_mixed, grad_self_branch)
    grad_self_mix = times_transposed(grad_self_branch, self_columns[:, 3 * model_width :]).astype(
        bf16
    )
    grad_query_heads, grad_key_heads, grad_value_heads = attend_backward(
        to_heads(grad_self_mix, images, HEADS),
        self_queries,
        self_keys,
        self_values,
        None,
        self_top,
        self_total,
    )
    grad_triple = jnp.concatenate(
        [
            grad_query_heads.reshape(-1, model_width),
            grad_key_heads.reshape(-1, model_width),
            grad_value_heads.reshape(-1, model_width),
        ],
        axis=1,
    ).astype(bf16)
    grad_self_in = rows_inner(self_low, grad_triple)
    grad_first, grad_gain_self, grad_shift_self = norm_backward(
        times_transposed(grad_triple, self_columns[:, : 3 * model_width]),
        self_normed,
        self_inverse,
        gain_self,
    )
    grad_one = grad_two + grad_first
    grad_cross_branch = grad_one.astype(bf16)
    grad_cross_out = rows_inner(cross_mixed, grad_cross_branch)
    grad_cross_mix = times_transposed(
        grad_cross_branch, cross_columns[:, 3 * model_width :]
    ).astype(bf16)
    cross_query_grad, cross_key_grad, cross_value_grad = attend_backward(
        to_heads(grad_cross_mix, images, HEADS),
        query_heads,
        key_heads,
        value_heads,
        visible_mask,
        cross_top,
        cross_total,
    )
    grad_queries = cross_query_grad.reshape(-1, model_width).astype(bf16)
    grad_pair = jnp.concatenate(
        [cross_key_grad.reshape(-1, model_width), cross_value_grad.reshape(-1, model_width)], axis=1
    ).astype(bf16)
    grad_cross_query = rows_inner(cross_low, grad_queries)
    grad_cross_pair = rows_inner(pixel_low, grad_pair)
    grad_input_norm, grad_gain_cross, grad_shift_cross = norm_backward(
        times_transposed(grad_queries, cross_columns[:, :model_width]),
        cross_normed,
        cross_inverse,
        gain_cross,
    )
    pixel_unused, grad_gain_pixel, grad_shift_pixel = norm_backward(
        times_transposed(grad_pair, cross_columns[:, model_width : 3 * model_width]),
        pixel_normed,
        pixel_inverse,
        gain_pixel,
    )
    latents_grad = (grad_one + grad_input_norm).reshape(latents.shape)
    vector_grad = jnp.concatenate(
        [
            grad_gain_pixel,
            grad_shift_pixel,
            grad_gain_cross,
            grad_shift_cross,
            grad_gain_self,
            grad_shift_self,
            grad_gain_feed,
            grad_shift_feed,
            grad_bias_down,
            grad_bias_up,
        ]
    )
    pieces = [
        grad_cross_query,
        grad_cross_pair,
        grad_cross_out,
        grad_self_in,
        grad_self_out,
        grad_up,
    ]
    panel_share, down_share, vector_share, squares = reduce(
        pieces, grad_down, vector_grad, vectors.shape[0]
    )
    grad_norm = jnp.sqrt(squares)
    device_total = lax.axis_size(("dp", "fsdp"))
    token_total = images * latent_count * device_total
    param_total = (
        model_width * panel.shape[1] + full_down.shape[0] * model_width + full_vector.shape[0]
    )
    threshold = clip_coeff * (token_total * param_total) ** 0.5
    factor = threshold / jnp.maximum(grad_norm, threshold)
    panel_after, panel_moment_after, panel_square_after = adam_update(
        panel, panel_moment, panel_square, panel_share * factor, rate_matrix, weight_decay
    )
    down_after, down_moment_after, down_square_after = adam_update(
        down, down_moment, down_square, down_share * factor, rate_matrix, weight_decay
    )
    vectors_after, vector_moment_after, vector_square_after = adam_update(
        vectors, vector_moment, vector_square, vector_share * factor, rate_vector, 0.0
    )
    return (
        latents_out,
        latents_grad,
        grad_norm,
        panel_after,
        panel_moment_after,
        panel_square_after,
        down_after,
        down_moment_after,
        down_square_after,
        vectors_after,
        vector_moment_after,
        vector_square_after,
    )


def solution(mesh):
    placed = (
        P(("dp", "fsdp"), None, None),
        P(("dp", "fsdp"), None, None),
        P(("dp", "fsdp")),
        P(("dp", "fsdp"), None, None),
        P(("dp", "fsdp"), None),
        P(("dp", "fsdp"), None),
        P(("dp", "fsdp"), None),
        P(("dp", "fsdp"), None),
        P(("dp", "fsdp"), None),
        P(("dp", "fsdp"), None),
        P(("dp", "fsdp")),
        P(("dp", "fsdp")),
        P(("dp", "fsdp")),
    )
    fast = (mesh.shape["dp"], mesh.shape["fsdp"]) == (LONG * SHORT * SHORT, SHORT)
    step = fast_step if fast else functools.partial(shards, slow_gather, slow_reduce)
    return jax.shard_map(
        step,
        mesh=mesh,
        in_specs=placed,
        out_specs=(
            P(("dp", "fsdp"), None, None),
            P(("dp", "fsdp"), None, None),
            P(),
            P(("dp", "fsdp"), None),
            P(("dp", "fsdp"), None),
            P(("dp", "fsdp"), None),
            P(("dp", "fsdp"), None),
            P(("dp", "fsdp"), None),
            P(("dp", "fsdp"), None),
            P(("dp", "fsdp")),
            P(("dp", "fsdp")),
            P(("dp", "fsdp")),
        ),
        check_vma=False,
    )
```

```python
import functools
import math
import types

import jax
import jax.numpy as jnp
from jax import lax
from jax.experimental import pallas as pl
from jax.experimental.pallas import tpu as pltpu
from jax.sharding import PartitionSpec as P

HEADS = 8
STEP = 10


norm_eps = 1e-05
beta_first = 0.9
beta_second = 0.999
adam_eps = 1e-08
rate_matrix = 0.05
rate_vector = 0.5
weight_decay = 0.1
clip_coeff = 0.01
masked_fill = -1e30


def matmul_low(left, right):
    return jnp.dot(left, right, preferred_element_type=jnp.float32)


def rows_inner(left, right):
    return lax.dot_general(
        left, right, (((0,), (0,)), ((), ())), preferred_element_type=jnp.float32
    )


def times_transposed(left, right):
    return lax.dot_general(
        left, right, (((1,), (1,)), ((), ())), preferred_element_type=jnp.float32
    )


def gelu_exact(values):
    return jax.nn.gelu(values, approximate=False)


def norm_forward(values, gain_row, shift_row):
    centre = values - jnp.mean(values, axis=-1, keepdims=True)
    inverse = lax.rsqrt(jnp.mean(centre * centre, axis=-1, keepdims=True) + norm_eps)
    normed = centre * inverse
    return (normed * gain_row + shift_row, normed, inverse)


def norm_backward(grad_out, normed, inverse, gain_row):
    grad_normed = grad_out * gain_row
    grad_values = inverse * (
        grad_normed
        - jnp.mean(grad_normed, axis=-1, keepdims=True)
        - normed * jnp.mean(grad_normed * normed, axis=-1, keepdims=True)
    )
    return (grad_values, jnp.sum(grad_out * normed, axis=0), jnp.sum(grad_out, axis=0))


def to_heads(rows, images, head_count):
    return rows.reshape(images, -1, head_count, rows.shape[1] // head_count)


def masked_scores(queries, key_rows, visible_mask):
    score_scale = queries.shape[-1] ** (-0.5)
    scores = (
        jnp.einsum("bqhd,bkhd->bhqk", queries, key_rows, preferred_element_type=jnp.float32)
        * score_scale
    )
    if visible_mask is not None:
        scores = jnp.where(visible_mask[:, None, None, :], scores, masked_fill)
    return scores


def attend_forward(queries, key_rows, value_rows, visible_mask):
    scores = masked_scores(queries, key_rows, visible_mask)
    row_top = jnp.max(scores, axis=-1, keepdims=True)
    powers = jnp.exp(scores - row_top)
    row_total = jnp.sum(powers, axis=-1, keepdims=True)
    probability = (powers / row_total).astype(jnp.bfloat16)
    mixture = jnp.einsum(
        "bhqk,bkhd->bqhd", probability, value_rows, preferred_element_type=jnp.float32
    )
    return (mixture.astype(jnp.bfloat16), row_top, row_total)


def attend_backward(grad_mix, queries, key_rows, value_rows, visible_mask, row_top, row_total):
    score_scale = queries.shape[-1] ** (-0.5)
    scores = masked_scores(queries, key_rows, visible_mask)
    probability = jnp.exp(scores - row_top) / row_total
    grad_prob = jnp.einsum(
        "bqhd,bkhd->bhqk", grad_mix, value_rows, preferred_element_type=jnp.float32
    )
    inner_sum = jnp.sum(grad_prob * probability, axis=-1, keepdims=True)
    grad_scores = (probability * (grad_prob - inner_sum)).astype(jnp.bfloat16)
    grad_queries = (
        jnp.einsum("bhqk,bkhd->bqhd", grad_scores, key_rows, preferred_element_type=jnp.float32)
        * score_scale
    )
    grad_keys = (
        jnp.einsum("bhqk,bqhd->bkhd", grad_scores, queries, preferred_element_type=jnp.float32)
        * score_scale
    )
    grad_values = jnp.einsum(
        "bhqk,bqhd->bkhd",
        probability.astype(jnp.bfloat16),
        grad_mix,
        preferred_element_type=jnp.float32,
    )
    return (grad_queries, grad_keys, grad_values)


def vector_slot(vector_float, index, model_width):
    return vector_float[index * model_width : (index + 1) * model_width]


def self_forward(first_sum, self_columns, gain_self, shift_self, images):
    model_width = first_sum.shape[1]
    normed_out, normed, inverse = norm_forward(first_sum, gain_self, shift_self)
    self_low = normed_out.astype(jnp.bfloat16)
    triple = matmul_low(self_low, self_columns[:, : 3 * model_width]).astype(jnp.bfloat16)
    self_queries = to_heads(triple[:, :model_width], images, HEADS)
    self_keys = to_heads(triple[:, model_width : 2 * model_width], images, HEADS)
    self_values = to_heads(triple[:, 2 * model_width :], images, HEADS)
    mixture, row_top, row_total = attend_forward(self_queries, self_keys, self_values, None)
    self_mixed = mixture.reshape(-1, model_width)
    return (
        normed,
        inverse,
        self_low,
        self_queries,
        self_keys,
        self_values,
        self_mixed,
        row_top,
        row_total,
    )


def adam_update(weight, moment, square, grad, rate, decay):
    moment_after = beta_first * moment + (1.0 - beta_first) * grad
    square_after = beta_second * square + (1.0 - beta_second) * grad * grad
    step_count = STEP
    fixed_moment = moment_after / (1.0 - beta_first**step_count)
    fixed_square = square_after / (1.0 - beta_second**step_count)
    weight_after = weight - rate * (
        fixed_moment / (jnp.sqrt(fixed_square) + adam_eps) + decay * weight
    )
    return (weight_after, moment_after, square_after)


MESH = pl.DeviceIdType.MESH
LONG, SHORT = 4, 2
CUT = (LONG, SHORT, SHORT, SHORT)
PLANE = SHORT * SHORT * SHORT
VMEM_LIMIT = 60 * 1024 * 1024


class Place:
    def __init__(self):
        row, self.y = lax.axis_index("dp"), lax.axis_index("fsdp")
        self.z, self.x, self.core = row // 4, (row // 2) % 2, row % 2
        even = self.core == 0
        x, y = self.x, self.y
        self.near = (jnp.where(even, 1 - x, x), jnp.where(even, y, 1 - y))
        self.far = (jnp.where(even, x, 1 - x), jnp.where(even, 1 - y, y))
        self.first, self.second = jnp.where(even, x, y), jnp.where(even, y, x)
        self.near_device = self.device(self.z, self.near[0], self.core, self.near[1])
        self.far_device = self.device(self.z, self.far[0], self.core, self.far[1])
        self.twin_device = self.device(self.z, x, 1 - self.core, y)
        self.up_device = self.device(self.z + 1, x, self.core, y)
        self.down_device = self.device(self.z - 1, x, self.core, y)

    def device(self, z, x, core, y):
        return (z * 4 + x * 2 + core, y)

    def along(self, step):
        return self.device((self.z + step) % LONG, self.x, self.core, self.y)

    def across(self, away):
        flip_x, flip_core, flip_y = away // 4, away // 2 % 2, away % 2
        return self.device(
            self.z,
            1 - self.x if flip_x else self.x,
            1 - self.core if flip_core else self.core,
            1 - self.y if flip_y else self.y,
        )

    def greet(self):
        barrier = pltpu.get_barrier_semaphore()
        partners = [self.along(step) for step in range(1, LONG)]
        partners += [self.across(away) for away in range(1, PLANE)]
        for partner in partners:
            pl.semaphore_signal(barrier, inc=1, device_id=partner, device_id_type=MESH)
        pl.semaphore_wait(barrier, len(partners))


def remote(source, target, send, receive, device):
    return pltpu.make_async_remote_copy(
        src_ref=source,
        dst_ref=target,
        send_sem=send,
        recv_sem=receive,
        device_id=device,
        device_id_type=MESH,
    )


GATHER_KINDS = 4 * (LONG - 1) + 4 + 1 + 2
GATHER_STAGES = 6
SPLIT = 2
SPREAD = 2
START, RECEIVE, SENT = range(3)


class Gather:
    def __init__(self, here, chunks, send, receive):
        self.here, self.chunks, self.send, self.receive = here, chunks, send, receive
        self.count = len(chunks)
        self.sets = ((here.x, here.y), here.near, here.far, (1 - here.x, 1 - here.y))

    def line_first(self, n):
        return n % 3 == 0

    def block(self, n, which, z=slice(None)):
        x, y = self.sets[which]
        return self.chunks[n].at[z, x, self.here.core, y]

    def copy(self, n, kind, block, device):
        return remote(block, block, self.send.at[n, kind], self.receive.at[n, kind], device)

    def hop(self, n, step, action):
        here, z = self.here, self.here.z
        for piece in (0,) if self.line_first(n) else (0, 1):
            kind = 6 * piece + 2 * (step - 1)

            def upward(origin, device):
                return self.copy(n, kind, self.block(n, piece, origin), device)

            def downward(origin, device):
                return self.copy(n, kind + 1, self.block(n, piece, origin), device)

            if action == RECEIVE:

                @pl.when(z - step >= 0)
                def _():
                    upward(z - step, here.down_device).wait_recv()

                @pl.when(z + step <= LONG - 1)
                def _():
                    downward(z + step, here.up_device).wait_recv()

            else:

                @pl.when(jnp.logical_and(z - step + 1 >= 0, z < LONG - 1))
                def _():
                    copy = upward(z - step + 1, here.up_device)
                    copy.start() if action == START else copy.wait_send()

                @pl.when(jnp.logical_and(z + step - 1 <= LONG - 1, z > 0))
                def _():
                    copy = downward(z + step - 1, here.down_device)
                    copy.start() if action == START else copy.wait_send()

    def twin(self, n, which):
        return self.copy(n, 12 + which, self.block(n, which), self.here.twin_device)

    def twin_back(self, n, which):
        x, y = self.sets[(0, 2, 1, 3)[which]]
        block = self.chunks[n].at[:, x, 1 - self.here.core, y]
        return self.copy(n, 12 + which, block, self.here.twin_device)

    def near(self, n, which):
        z = slice(None) if self.line_first(n) else self.here.z
        return self.copy(n, 16, self.block(n, which, z), self.here.near_device)

    def far(self, n, which, back=False):
        return self.copy(
            n, 17 + which, self.block(n, which + 2 * back), self.here.far_device
        )

    def stage(self, n, step):
        if not 0 <= n < self.count:
            return
        if step == 5:
            for which in range(2):
                self.far(n, which, True).wait_recv()
                self.twin(n, 2 + which).start()
        elif self.line_first(n):
            if step in (1, 2, 3):
                self.hop(n, step, RECEIVE)
            if step < 3:
                self.hop(n, step + 1, START)
            elif step == 3:
                self.near(n, 0).start()
                self.far(n, 0).start()
                self.twin(n, 0).start()
            else:
                self.near(n, 1).wait_recv()
                self.far(n, 1).start()
                self.twin(n, 1).start()
        elif step == 0:
            self.near(n, 0).start()
        else:
            if step == 1:
                self.near(n, 1).wait_recv()
            else:
                self.hop(n, step - 1, RECEIVE)
            if step < 4:
                self.hop(n, step, START)
            else:
                for which in range(2):
                    self.far(n, which).start()
                    self.twin(n, which).start()

    def whole(self, n):
        for which in range(4):
            self.twin_back(n, which).wait_recv()

    def finish(self):
        for n in range(self.count):
            for step in range(1, LONG):
                self.hop(n, step, SENT)
            self.near(n, 0).wait_send()
            for which in range(2):
                self.far(n, which).wait_send()
            for which in range(4):
                self.twin(n, which).wait_send()


REDUCE_KINDS = 1 + 1 + 2 * (LONG - 1)
REDUCE_STAGES = 6
RING = 9
STAGED = 3
DIRECT = 2


class Reduce:
    def __init__(self, here, r, count, put):
        self.here, self.r, self.count, self.put = here, r, count, put

    def line_last(self, n):
        return n % 3 == 0

    def direct(self, n):
        return n >= self.count - DIRECT

    def at(self, n):
        slot = n % RING
        return slot, slot // 3 if self.line_last(n) else slot // 3 * 2 + slot % 3 - 1

    def copy(self, n, kind, source, target, device):
        r = self.r
        return remote(source, target, r.reduce_send.at[n, kind], r.reduce_receive.at[n, kind], device)

    def far(self, n):
        r, here = self.r, self.here
        source = r.staged.at[n % STAGED, :, :, 1 - here.second]
        return self.copy(n, 0, source, r.from_far.at[n % RING], here.far_device)

    def near(self, n):
        r, here = self.r, self.here
        slot, index = self.at(n)
        if self.direct(n):
            source = r.from_far.at[slot, :, 1 - here.first]
            target = r.direct_near.at[n - self.count + DIRECT]
        elif self.line_last(n):
            source, target = r.from_far.at[slot, :, 1 - here.first], r.from_near_line.at[index]
        else:
            source, target = r.from_far.at[slot, here.z, 1 - here.first], r.from_near.at[index]
        return self.copy(n, 1, source, target, here.near_device)

    def along(self, n, step):
        r, here, index = self.r, self.here, n - self.count + DIRECT
        source = r.direct_near.at[index, (here.z + step) % LONG]
        return self.copy(n, 1 + step, source, r.direct_line.at[index, step - 1], here.along(step))

    def stage_direct(self, n, step):
        r, here, index = self.r, self.here, n - self.count + DIRECT
        slot = n % RING
        if step == 1:
            self.credit(n, 1)
            self.credit(n, 3, here.z < LONG - 1)
            self.credit(n, 2, here.z > 0)
            self.near(n).start()
        elif step == 2:
            self.near(n).wait_recv()

            def one(at, carry):
                add_up(r.direct_near.at[index, at], r.from_far.at[slot, at, here.first])
                return carry

            lax.fori_loop(0, LONG, one, 0)
            for away in range(1, LONG):
                self.along(n, away).start()
        elif step == 3:
            value = r.direct_near[index, here.z].astype(jnp.float32)
            for away in range(1, LONG):
                self.along(n, away).wait_recv()
                value = value + r.direct_line[index, away - 1].astype(jnp.float32)
            self.put(n, value)

    def line(self, n, place):
        r = self.r
        slot, index = self.at(n)
        return r.from_near_line.at[index, place] if self.line_last(n) else r.from_far.at[slot, place]

    def landing(self, n, kind):
        r = self.r
        index = self.at(n)[1]
        return r.from_line_short.at[index, kind] if self.line_last(n) else r.from_line.at[index, kind]

    def hop(self, n, step, action):
        here, z, away = self.here, self.here.z, LONG - step
        kind = 2 * (step - 1)

        @pl.when(z - away >= 0)
        def _():
            copy = self.copy(
                n, 2 + kind, self.line(n, z - away), self.landing(n, kind), here.down_device
            )
            copy.start() if action == START else copy.wait_send()

        @pl.when(z + away <= LONG - 1)
        def _():
            copy = self.copy(
                n, 3 + kind, self.line(n, z + away), self.landing(n, kind + 1), here.up_device
            )
            copy.start() if action == START else copy.wait_send()

    def hop_in(self, n, step):
        here, z, away = self.here, self.here.z, LONG - step
        kind = 2 * (step - 1)
        for side, place, there, device in (
            (0, z - away + 1, jnp.logical_and(z < LONG - 1, z - away + 1 >= 0), here.up_device),
            (1, z + away - 1, jnp.logical_and(z > 0, z + away - 1 <= LONG - 1), here.down_device),
        ):

            @pl.when(there)
            def _():
                landed = self.landing(n, kind + side)
                self.copy(n, 2 + kind + side, landed, landed, device).wait_recv()
                total = self.line(n, place)
                if self.line_last(n):
                    add_up(total, landed)
                else:
                    for part in range(SHORT):
                        add_up(total.at[part], landed.at[part])

    def credit(self, n, kind, condition=None):
        if n < RING:
            return

        def take():
            pl.semaphore_wait(self.r.credit.at[n - RING, kind], 1)

        take() if condition is None else pl.when(condition)(take)

    def give(self, n):
        if n + RING >= self.count:
            return
        here, r = self.here, self.r

        def signal(kind, device):
            pl.semaphore_signal(r.credit.at[n, kind], inc=1, device_id=device, device_id_type=MESH)

        self.near(n).wait_send()
        for step in range(1, LONG):
            self.hop(n, step, SENT)
        signal(0, here.far_device)
        signal(1, here.near_device)
        pl.when(here.z < LONG - 1)(lambda: signal(2, here.up_device))
        pl.when(here.z > 0)(lambda: signal(3, here.down_device))

    def first_hop(self, n):
        self.credit(n, 3, self.here.z < LONG - 1)
        self.credit(n, 2, self.here.z > 0)
        self.hop(n, 1, START)

    def free(self, n):
        if n >= STAGED:
            self.far(n - STAGED).wait_send()

    def stage(self, n, step):
        if not 0 <= n < self.count:
            return
        r, here = self.r, self.here
        slot, index = self.at(n)
        if step == 0:
            self.credit(n, 0)
            self.far(n).start()
            return
        if step == 1:
            self.far(n).wait_recv()

            def one(at, carry):
                add_up(
                    r.from_far.at[slot, at // 2, at % 2],
                    r.staged.at[n % STAGED, at // 2, at % 2, here.second],
                )
                return carry

            lax.fori_loop(0, LONG * SHORT, one, 0)
            if self.direct(n):
                self.stage_direct(n, step)
            elif self.line_last(n):
                self.credit(n, 1)
                self.near(n).start()
            else:
                self.first_hop(n)
        elif self.direct(n):
            self.stage_direct(n, step)
        elif self.line_last(n):
            if step == 2:
                self.near(n).wait_recv()

                def one(at, carry):
                    add_up(r.from_near_line.at[index, at], r.from_far.at[slot, at, here.first])
                    return carry

                lax.fori_loop(0, LONG, one, 0)
                self.first_hop(n)
            else:
                self.hop_in(n, step - 2)
                if step < 5:
                    self.hop(n, step - 1, START)
                else:
                    self.put(n, r.from_near_line[index, here.z].astype(jnp.float32))
                    self.give(n)
        elif step < 5:
            self.hop_in(n, step - 1)
            if step < 4:
                self.hop(n, step, START)
            else:
                self.credit(n, 1)
                self.near(n).start()
        else:
            self.near(n).wait_recv()
            own = r.from_far[slot, here.z, here.first].astype(jnp.float32)
            self.put(n, own + r.from_near[index].astype(jnp.float32))
            self.give(n)

    def tick(self, n):
        for step in range(REDUCE_STAGES):
            self.stage(n - step, step)

    def finish(self):
        for n in range(max(0, self.count - STAGED), self.count):
            self.far(n).wait_send()
        for n in range(max(0, self.count - RING), self.count):
            self.near(n).wait_send()
            for step in range(1, LONG):
                if self.direct(n):
                    self.along(n, step).wait_send()
                else:
                    self.hop(n, step, SENT)


def add_up(target, source):
    total = target[...].astype(jnp.float32) + source[...].astype(jnp.float32)
    target[...] = total.astype(target.dtype)


class Meeting:
    def __init__(self, here, value, line, plane, send, receive):
        self.here, self.value, self.line, self.plane = here, value, line, plane
        self.send, self.receive = send, receive
        self.place = here.x * 4 + here.core * 2 + here.y

    def along(self, step, back=False):
        here = self.here
        place = (here.z - step) % LONG if back else here.z
        return remote(
            self.line.at[place] if back else self.value,
            self.line.at[place],
            self.send.at[step - 1],
            self.receive.at[step - 1],
            here.along(step),
        )

    def across(self, away, back=False):
        here = self.here
        place = self.place
        if back:
            x = 1 - here.x if away // 4 else here.x
            core = 1 - here.core if away // 2 % 2 else here.core
            y = 1 - here.y if away % 2 else here.y
            place = x * 4 + core * 2 + y
        block = self.plane.at[place]
        number = LONG - 2 + away
        return remote(
            block, block, self.send.at[number], self.receive.at[number], here.across(away)
        )

    def step(self, k):
        if k == 0:
            self.line[self.here.z] = self.value[...]
            for away in range(1, LONG):
                self.along(away).start()
            return None
        if k == 1:
            for away in range(1, LONG):
                self.along(away).wait_send()
                self.along(away, True).wait_recv()
            total = self.line[0]
            for place in range(1, LONG):
                total = total + self.line[place]
            self.plane[self.place] = total
            for away in range(1, PLANE):
                self.across(away).start()
            return None
        for away in range(1, PLANE):
            self.across(away).wait_send()
            self.across(away, True).wait_recv()
        total = self.plane[0]
        for place in range(1, PLANE):
            total = total + self.plane[place]
        return total


TILE = 256
LANES = 128
FORWARD_BUDGET = 1.5
VECTOR_TICKS = (0, 7, 9)
TURNED, LANDED = "turned_", "landed_"
BAND = 32
CROSS_Q, CROSS_K, CROSS_V, CROSS_O, SELF_Q, SELF_K, SELF_V, SELF_O, UP = range(9)


def tile(start, size):
    return pl.ds(pl.multiple_of(start, size), size)


def bands(rows, body, carry=0):
    return lax.fori_loop(0, rows // BAND, lambda k, c: body(tile(k * BAND, BAND), c), carry, unroll=4)


def normalised(values):
    centre = values - jnp.mean(values, axis=-1, keepdims=True)
    inverse = lax.rsqrt(jnp.mean(centre * centre, axis=-1, keepdims=True) + norm_eps)
    return centre * inverse, inverse


def block_kernel(names, sizes, *refs):
    r = types.SimpleNamespace(**dict(zip(names, refs, strict=True)))
    width, lat, pix, hidden_parts, threshold = sizes
    f32, bf16 = jnp.float32, jnp.bfloat16
    here = Place()
    core = here.core
    scale = (width // HEADS) ** (-0.5)
    panel_blocks = UP + hidden_parts
    gather_order = [CROSS_K, CROSS_V, CROSS_Q, CROSS_O, SELF_Q, SELF_K, SELF_V, SELF_O]
    gather_order += list(range(UP, panel_blocks))
    share_rows = r.panel.shape[0]

    meet_in = Meeting(here, r.vectors, r.meet_line, r.meet_plane, r.meet_send, r.meet_receive)
    meet_out = Meeting(here, r.vector_grad, r.sum_line, r.sum_plane, r.sum_send, r.sum_receive)
    meet_last = Meeting(here, r.squares, r.last_line, r.last_plane, r.last_send, r.last_receive)

    chunks, keep = [], []

    def keep_own(low, whole):
        own = whole.at[here.z, here.x, core, here.y]
        keep.append(pltpu.make_async_copy(low, own, r.own.at[len(keep)]))
        keep[-1].start()

    for block in gather_order:
        columns = pl.ds(block * width, width)
        r.low_panel[:, columns] = r.panel[:, columns].astype(bf16)
        keep_own(r.low_panel.at[:, columns], r.whole_panel.at[:, :, :, :, :, columns])
        for part in range(SPLIT):
            columns = pl.ds(block * width + part * width // SPLIT, width // SPLIT)
            chunks.append(r.whole_panel.at[:, :, :, :, :, columns])
    for block in range(hidden_parts):
        rows = pl.ds(block * share_rows, share_rows)
        r.low_down[rows, :] = r.down[rows, :].astype(bf16)
        keep_own(r.low_down.at[rows], r.whole_down.at[:, :, :, :, rows])
        for part in range(SPLIT):
            rows = pl.ds(block * share_rows + part * share_rows // SPLIT, share_rows // SPLIT)
            chunks.append(r.whole_down.at[:, :, :, :, rows])
    gather = Gather(here, chunks, r.gather_send, r.gather_receive)
    here.greet()

    def gather_tick(tick):
        if tick % SPLIT == 0 and tick < len(chunks):
            keep[tick // SPLIT].wait()
        for step in range(GATHER_STAGES):
            gather.stage(tick - SPREAD * step, step)

    twins = {}

    def to_twin(source, target):
        number = len(twins)
        copy = remote(
            source, target, r.twin_send.at[number], r.twin_receive.at[number], here.twin_device
        )
        copy.start()
        twins[number] = copy
        return number

    def from_twin(number):
        twins[number].wait_recv()

    flat_panel = r.whole_panel.reshape(-1, panel_blocks * width)
    flat_down = r.whole_down.reshape(-1, width)
    loads = []

    def fetch(part):
        if isinstance(part, tuple):
            source = flat_down.at[pl.ds(part[1] * width, width)]
        else:
            source = flat_panel.at[:, pl.ds(part * width, width)]
        slot = len(loads) % 2
        copy = pltpu.make_async_copy(source, r.weights.at[slot], r.load.at[slot])
        copy.start()
        loads.append(copy)
        return len(loads) - 1

    def fetched(number):
        loads[number].wait()
        return number % 2

    def put(n, value):
        if n < hidden_parts:
            r.down_share[n * share_rows : (n + 1) * share_rows, :] = value
        else:
            block = reduce_order[n]
            r.panel_share[:, block * width : (block + 1) * width] = value
        square = value * value
        gained = r.squares[...]
        for across in range(0, width, LANES):
            for at in range(0, share_rows, 8):
                gained = gained + square[at : at + 8, across : across + LANES]
        r.squares[...] = gained

    reduce_order = [None] * hidden_parts + list(range(UP, panel_blocks))
    reduce_order += [SELF_O, SELF_Q, SELF_K, SELF_V, CROSS_O, CROSS_Q, CROSS_K, CROSS_V]
    reduce = Reduce(here, r, len(reduce_order), put)

    def vector(k):
        return r.rows[k : k + 1, :]

    def times(left, slot, emit):
        def one(k, carry):
            columns = tile(k * TILE, TILE)
            emit(columns, jnp.dot(left[...], r.weights[slot, :, columns], preferred_element_type=f32))
            return carry

        lax.fori_loop(0, width // TILE, one, 0, unroll=4)

    def times_back(left, slot, emit):
        def one(k, carry):
            columns = tile(k * TILE, TILE)
            emit(columns, times_transposed(left[...], r.weights[slot, columns, :]))
            return carry

        lax.fori_loop(0, width // TILE, one, 0, unroll=4)

    def norm_rows(read, count, gain, shift, target):
        def one(rows, carry):
            normed, _ = normalised(read(rows))
            target[rows, :] = (normed * vector(gain) + vector(shift)).astype(bf16)
            return carry

        bands(count, one)

    def keep_vector(k, value):
        for at in range(width // LANES):
            row = k * (width // LANES) + at
            r.vector_grad[row : row + 1, :] = value[:, at * LANES : (at + 1) * LANES]

    def folded(value):
        total = value[0:8]
        for at in range(8, BAND, 8):
            total = total + value[at : at + 8]
        return total

    def norm_back(read, grad, count, gain, shift, emit):
        def one(rows, carry):
            gain_sum, shift_sum = carry
            normed, inverse = normalised(read(rows))
            out = grad[rows, :]
            if emit is not None:
                inner = out * vector(gain)
                emit(
                    rows,
                    inverse
                    * (
                        inner
                        - jnp.mean(inner, axis=-1, keepdims=True)
                        - normed * jnp.mean(inner * normed, axis=-1, keepdims=True)
                    ),
                )
            return gain_sum + folded(out * normed), shift_sum + folded(out)

        empty = jnp.zeros((8, width), f32)
        gain_sum, shift_sum = bands(count, one, (empty, empty))
        keep_vector(gain, jnp.sum(gain_sum, axis=0, keepdims=True))
        keep_vector(shift, jnp.sum(shift_sum, axis=0, keepdims=True))

    head = width // HEADS

    def probabilities(queries, keys, masked):
        scores = times_transposed(queries, keys) * scale
        if masked:
            scores = jnp.where(r.mask[0:1, :] > 0.5, scores, masked_fill)
        powers = jnp.exp(scores - jnp.max(scores, axis=-1, keepdims=True))
        return powers / jnp.sum(powers, axis=-1, keepdims=True)

    def attend(heads, queries, keys, key_start, values, value_start, masked, target):
        def one(k, carry):
            columns = tile(k * head, head)
            probability = probabilities(
                queries[:, columns], keys[:, tile(key_start + k * head, head)], masked
            )
            value_rows = values[:, tile(value_start + k * head, head)]
            target[:, columns] = matmul_low(probability.astype(bf16), value_rows).astype(bf16)
            return carry

        lax.fori_loop(*heads, one, 0, unroll=HEADS // 2)

    def attend_back(grad, queries, keys, key_start, values, value_start, masked, targets):
        query_grad, key_grad, key_at, value_grad, value_at = targets

        def one(k, carry):
            columns = tile(k * head, head)
            key_columns = tile(key_start + k * head, head)
            value_columns = tile(value_start + k * head, head)
            query_rows, key_rows = queries[:, columns], keys[:, key_columns]
            probability = probabilities(query_rows, key_rows, masked)
            grad_mix = grad[:, columns]
            grad_prob = times_transposed(grad_mix, values[:, value_columns])
            inner = jnp.sum(grad_prob * probability, axis=-1, keepdims=True)
            grad_scores = (probability * (grad_prob - inner)).astype(bf16)
            query_grad[:, columns] = (matmul_low(grad_scores, key_rows) * scale).astype(bf16)
            key_grad[:, tile(key_at + k * head, head)] = (
                rows_inner(grad_scores, query_rows) * scale
            ).astype(bf16)
            value_grad[:, tile(value_at + k * head, head)] = rows_inner(
                probability.astype(bf16), grad_mix
            ).astype(bf16)
            return carry

        lax.fori_loop(0, HEADS, one, 0, unroll=4)

    row_id = lax.broadcasted_iota(jnp.int32, (LANES, LANES), 0)
    unit = (row_id == lax.broadcasted_iota(jnp.int32, (LANES, LANES), 1)).astype(bf16)

    def turn(source, target, landing):
        def one(k, carry):
            turned = times_transposed(unit, source[:, tile(k * LANES, LANES)]).astype(bf16)
            for side in range(2):
                target[side, k] = turned[side * LANES // 2 : (side + 1) * LANES // 2]
            return carry

        lax.fori_loop(0, width // LANES, one, 0, unroll=8)
        return to_twin(target.at[1 - core], landing)

    def weight_grad(n, own, other, grad, grad_other, start):
        reduce.free(n)
        slot = n % STAGED

        def one(k, carry):
            columns = tile(start + k * TILE, TILE)
            total = matmul_low(own(), grad[:, columns]) + matmul_low(other(), grad_other[:, columns])
            total = total.astype(bf16).reshape(LONG, SHORT, SHORT, share_rows, TILE)
            into = tile(k * TILE, TILE)
            for to_x in range(SHORT):
                for to_y in range(SHORT):
                    first = jnp.where(core == 0, to_x, to_y)
                    second = jnp.where(core == 0, to_y, to_x)
                    r.staged[slot, :, first, second, :, into] = total[:, to_x, to_y]
            return carry

        lax.fori_loop(0, width // TILE, one, 0, unroll=4)

    def turned_pair(target, landing):
        rows = target.shape[3]
        return (
            lambda: target[core].reshape(-1, rows),
            lambda: landing[...].reshape(-1, rows),
        )

    marks = types.SimpleNamespace()

    def set_rows(total):
        per = width // LANES
        for row in range(r.rows.shape[0]):
            for at in range(per):
                line = total[row * per + at : row * per + at + 1, :]
                r.rows[row : row + 1, at * LANES : (at + 1) * LANES] = line.astype(bf16).astype(f32)

    def after_vectors():
        yield 0.5, lambda: norm_rows(
            lambda rows: r.pixels[rows, :].astype(f32), pix, 0, 1, r.pixel_low
        )
        yield 0.9, lambda: norm_rows(
            lambda rows: r.latents[rows, :].astype(f32), lat, 2, 3, r.left
        )
        yield 0.4, lambda: mark_turn("pixel", r.pixel_low)
        yield 0.5, lambda: mark_turn("cross", r.left)

    def to_columns(target, start=0):
        def emit(columns, value):
            where = pl.ds(pl.multiple_of(columns.start + start, TILE), TILE)
            target[:, where] = value.astype(bf16)

        return emit

    def add_columns(target, base):
        def emit(columns, value):
            target[:, columns] = base[:, columns].astype(f32) + value

        return emit

    def mark_turn(name, source):
        landing = getattr(r, LANDED + name)
        setattr(marks, name, turn(source, getattr(r, TURNED + name), landing))

    halves = ((0, HEADS // 2), (HEADS // 2, HEADS))

    def forward(block, number):
        if block in (CROSS_K, CROSS_V):
            emit = to_columns(r.pair, (block - CROSS_K) * width)
            yield 0.6, lambda: times(r.pixel_low, fetched(number), emit)
        elif block == CROSS_Q:
            yield 0.8, lambda: times(r.left, fetched(number), to_columns(r.cross_query))
            for heads in halves:
                yield 1.0, functools.partial(
                    attend, heads, r.cross_query, r.pair, 0, r.pair, width, True, r.mixed
                )
            yield 0.5, lambda: mark_turn("cross_mix", r.mixed)
        elif block == CROSS_O:
            yield 0.8, lambda: times(r.mixed, fetched(number), add_columns(r.first, r.latents))
            yield 0.8, lambda: norm_rows(lambda rows: r.first[rows, :], lat, 4, 5, r.left)
            yield 0.5, lambda: mark_turn("self", r.left)
        elif block in (SELF_Q, SELF_K, SELF_V):
            emit = to_columns(r.triple, (block - SELF_Q) * width)
            yield 0.8, lambda: times(r.left, fetched(number), emit)
            if block == SELF_V:
                for heads in halves:
                    yield 1.5, functools.partial(
                        attend, heads, r.triple, r.triple, width, r.triple, 2 * width, False, r.mixed
                    )
                yield 0.5, lambda: mark_turn("self_mix", r.mixed)
        elif block == SELF_O:
            yield 0.8, lambda: times(r.mixed, fetched(number), add_columns(r.second, r.first))
            yield 0.8, lambda: norm_rows(lambda rows: r.second[rows, :], lat, 6, 7, r.left)
            yield 0.5, lambda: mark_turn("feed", r.left)
        else:
            part = block - UP

            def emit(columns, value):
                upper = value + r.rows[9 + part : 10 + part, columns]
                below = 0.5 + 0.5 * lax.erf(upper * (0.5**0.5))
                where = pl.ds(pl.multiple_of(columns.start + part * width, TILE), TILE)
                r.hidden[:, where] = (upper * below).astype(bf16)
                density = jnp.exp(-0.5 * upper * upper) * ((2.0 * math.pi) ** -0.5)
                r.slope[:, where] = below + upper * density

            def one(k, carry):
                block_at = part * (width // LANES) + k
                turned = times_transposed(unit, r.hidden[:, tile(block_at * LANES, LANES)])
                turned = turned.astype(bf16).reshape(hidden_parts, share_rows, lat)
                side = (k // 2) % 2
                r.turned_hidden[side, block_at // 4 * 2 + k % 2] = turned
                return carry

            yield 1.5, lambda: times(r.left, fetched(number), emit)
            yield 0.6, lambda: lax.fori_loop(0, width // LANES, one, 0, unroll=8)

    forward_blocks = len(gather_order)
    ticks = len(chunks) + SPREAD * (GATHER_STAGES - 1)
    arrival = SPLIT - 1 + SPREAD * (GATHER_STAGES - 1) + 1
    todo, taken = [], 0

    def work(budget, until=None):
        nonlocal taken
        spent = 0.0
        while taken < len(todo) and (spent < budget or (until is not None and taken < until)):
            cost, step = todo[taken]
            taken += 1
            step()
            spent += cost

    tick, fetch_next, ends = 0, 0, []
    while fetch_next < forward_blocks:
        gather_tick(tick)
        if tick in VECTOR_TICKS:
            total = meet_in.step(VECTOR_TICKS.index(tick))
            if tick == VECTOR_TICKS[2]:
                set_rows(total)
                todo.extend(after_vectors())
        elif tick == VECTOR_TICKS[2] + 1:
            marks.dz = to_twin(r.out_grad, r.landed_dz)
        if tick >= SPLIT * fetch_next + arrival:
            if len(ends) > 1:
                work(0.0, ends[-2])
            for n in range(SPLIT * fetch_next, SPLIT * fetch_next + SPLIT):
                gather.whole(n)
            number = fetch(gather_order[fetch_next])
            work(FORWARD_BUDGET)
            todo.extend(forward(gather_order[fetch_next], number))
            ends.append(len(todo))
            fetch_next += 1
        else:
            work(FORWARD_BUDGET)
        tick += 1
    work(1e9)
    marks.hidden = to_twin(r.turned_hidden.at[1 - core], r.landed_hidden)

    r.squares[...] = jnp.zeros_like(r.squares)
    gather_tick(tick)
    tick += 1
    from_twin(marks.dz)
    from_twin(marks.hidden)

    def hidden_grad(part):
        weight_grad(
            part,
            lambda: r.turned_hidden[core, :, part].reshape(-1, lat),
            lambda: r.landed_hidden[:, part].reshape(-1, lat),
            r.out_grad,
            r.landed_dz,
            0,
        )
        reduce.tick(part)

    part = 0
    while tick < ticks:
        if part < 3:
            hidden_grad(part)
            part += 1
        for _ in range(2):
            if tick < ticks:
                gather_tick(tick)
                tick += 1
    hidden_next = part
    for n in range(SPLIT * forward_blocks, len(chunks)):
        gather.whole(n)
    number = fetch(("down", 0))

    def start_out(rows, carry):
        r.total[rows, :] = r.second[rows, :] + vector(8)
        return carry + folded(r.out_grad[rows, :].astype(f32))

    shift_sum = bands(lat, start_out, jnp.zeros((8, width), f32))
    keep_vector(8, jnp.sum(shift_sum, axis=0, keepdims=True))
    du_marks = []

    def out_and_du(part, slot):
        hidden_part = r.hidden.at[:, pl.ds(part * width, width)]

        def emit(columns, value):
            r.total[:, columns] += value

        times(hidden_part, slot, emit)

        def emit_du(columns, value):
            where = pl.ds(pl.multiple_of(columns.start + part * width, TILE), TILE)
            low = (value * r.slope[:, where]).astype(bf16)
            r.hidden[:, where] = low
            column_sum = jnp.sum(low.astype(f32), axis=0, keepdims=True)
            at = 9 * (width // LANES) + part * (width // LANES) + lax.div(columns.start, LANES)
            for k in range(TILE // LANES):
                r.vector_grad[pl.ds(at + k, 1), :] = column_sum[:, k * LANES : (k + 1) * LANES]

        times_back(r.out_grad, slot, emit_du)
        du_marks.append(to_twin(hidden_part, r.landed_du.at[:, pl.ds(part * width, width)]))

    for part in range(hidden_parts):
        slot = fetched(number)
        number = fetch(("down", part + 1) if part + 1 < hidden_parts else UP)
        out_and_du(part, slot)
        if hidden_next + part < hidden_parts:
            hidden_grad(hidden_next + part)

    def finish_out(rows, carry):
        r.latents_out[rows, :] = r.total[rows, :].astype(bf16)
        r.total[rows, :] = jnp.zeros((BAND, width), f32)
        return carry

    bands(lat, finish_out)

    def add_total(columns, value):
        r.total[:, columns] += value

    from_twin(marks.feed)
    own, other = turned_pair(r.turned_feed, r.landed_feed)
    for part in range(hidden_parts):
        slot = fetched(number)
        number = fetch(UP + part + 1 if part + 1 < hidden_parts else SELF_O)
        times_back(r.hidden.at[:, pl.ds(part * width, width)], slot, add_total)
        from_twin(du_marks[part])
        n = hidden_parts + part
        weight_grad(n, own, other, r.hidden, r.landed_du, part * width)
        if part + 1 == hidden_parts:

            def into_second(rows, value):
                value = value + r.out_grad[rows, :].astype(f32)
                r.second[rows, :] = value
                r.grad_low[rows, :] = value.astype(bf16)

            norm_back(lambda rows: r.second[rows, :], r.total, lat, 6, 7, into_second)
            marks.ds = to_twin(r.grad_low, r.landed_ds)
        reduce.tick(n)

    def branch_out(n, slot, grad_low, landed, mark, turned, landed_turned, turned_mark):
        times_back(grad_low, slot, to_columns(r.mixed))
        from_twin(mark)
        from_twin(turned_mark)
        weight_grad(n, *turned_pair(turned, landed_turned), grad_low, landed, 0)

    n = 2 * hidden_parts
    slot = fetched(number)
    number = fetch(SELF_Q)
    branch_out(
        n, slot, r.grad_low, r.landed_ds, marks.ds, r.turned_self_mix, r.landed_self_mix, marks.self_mix
    )
    reduce.stage(n, 0)
    attend_back(
        r.mixed,
        r.triple,
        r.triple,
        width,
        r.triple,
        2 * width,
        False,
        (r.triple_grad, r.triple_grad, width, r.triple_grad, 2 * width),
    )
    triple_marks = []
    for part in range(3):
        columns = pl.ds(part * width, width)
        triple_marks.append(to_twin(r.triple_grad.at[:, columns], r.landed_triple.at[:, columns]))
    for step in range(1, REDUCE_STAGES):
        reduce.stage(n - step, step)

    def clear(rows, carry):
        r.total[rows, :] = jnp.zeros((BAND, width), f32)
        return carry

    bands(lat, clear)
    from_twin(marks.self)
    own, other = turned_pair(r.turned_self, r.landed_self)
    for part in range(3):
        slot = fetched(number)
        number = fetch((SELF_K, SELF_V, CROSS_O)[part])
        times_back(r.triple_grad.at[:, pl.ds(part * width, width)], slot, add_total)
        from_twin(triple_marks[part])
        n += 1
        weight_grad(n, own, other, r.triple_grad, r.landed_triple, part * width)
        if part == 2:

            def into_first(rows, value):
                value = value + r.second[rows, :]
                r.second[rows, :] = value
                r.cross_low[rows, :] = value.astype(bf16)

            norm_back(lambda rows: r.first[rows, :], r.total, lat, 4, 5, into_first)
            marks.dc = to_twin(r.cross_low, r.landed_dc)
        reduce.tick(n)

    n += 1
    slot = fetched(number)
    number = fetch(CROSS_Q)
    branch_out(
        n, slot, r.cross_low, r.landed_dc, marks.dc, r.turned_cross_mix, r.landed_cross_mix, marks.cross_mix
    )
    reduce.stage(n, 0)
    attend_back(
        r.mixed,
        r.cross_query,
        r.pair,
        0,
        r.pair,
        width,
        True,
        (r.query_grad, r.pair_grad, 0, r.pair_grad, width),
    )
    query_mark = to_twin(r.query_grad, r.landed_query)
    pair_marks = []
    for part in range(2):
        columns = pl.ds(part * width, width)
        pair_marks.append(to_twin(r.pair_grad.at[:, columns], r.landed_pair.at[:, columns]))
    for step in range(1, REDUCE_STAGES):
        reduce.stage(n - step, step)

    slot = fetched(number)
    number = fetch(CROSS_K)

    def set_total(columns, value):
        r.total[:, columns] = value

    times_back(r.query_grad, slot, set_total)
    from_twin(query_mark)
    from_twin(marks.cross)
    n += 1
    weight_grad(n, *turned_pair(r.turned_cross, r.landed_cross), r.query_grad, r.landed_query, 0)
    reduce.stage(n, 0)

    def into_latents(rows, value):
        r.latents_grad[rows, :] = value + r.second[rows, :]

    norm_back(lambda rows: r.latents[rows, :].astype(f32), r.total, lat, 2, 3, into_latents)
    for step in range(1, REDUCE_STAGES):
        reduce.stage(n - step, step)
    from_twin(marks.pixel)
    own, other = turned_pair(r.turned_pixel, r.landed_pixel)
    pixel_total = r.total.at[pl.ds(0, pix)]

    for part in range(2):
        slot = fetched(number)
        if part == 0:
            number = fetch(CROSS_V)

        def emit_pixel(columns, value):
            if part == 0:
                pixel_total[:, columns] = value
            else:
                pixel_total[:, columns] += value

        times_back(r.pair_grad.at[:, pl.ds(part * width, width)], slot, emit_pixel)
        from_twin(pair_marks[part])
        n += 1
        weight_grad(n, own, other, r.pair_grad, r.landed_pair, part * width)
        reduce.stage(n, 0)
        if part == 1:
            norm_back(lambda rows: r.pixels[rows, :].astype(f32), pixel_total, pix, 0, 1, None)
            meet_out.step(0)
        for step in range(1, REDUCE_STAGES):
            reduce.stage(n - step, step)
    for k in range(1, REDUCE_STAGES - DIRECT):
        if k == 1:
            meet_out.step(1)
        elif k == 2:
            total = meet_out.step(2)
            r.vector_share[...] = total
            vector_squares = jnp.sum(total * total)
        reduce.tick(n + k)
    for k in range(3):
        total = meet_last.step(k)
    norm = jnp.sqrt(jnp.zeros((8, LANES), f32) + (jnp.sum(total) + vector_squares))
    r.norms[0] = norm
    r.norms[1] = threshold / jnp.maximum(norm, threshold)
    reduce.finish()
    gather.finish()
    for copy in twins.values():
        copy.wait_send()


def run_block(latents, pixels, mask, out_grad, panel, down, vectors, threshold):
    f32, bf16 = jnp.float32, jnp.bfloat16
    lat, width = latents.shape
    pix = pixels.shape[0]
    share_rows = panel.shape[0]
    hidden_parts = down.shape[0] // share_rows
    wide = hidden_parts * width
    half = LANES // 2
    blocks = panel.shape[1] // width
    chunks = blocks + hidden_parts
    unit = (share_rows, width)
    vmem = pltpu.VMEM
    dma, any_space = pltpu.SemaphoreType.DMA, pl.BlockSpec(memory_space=pl.ANY)
    in_vmem = pl.BlockSpec(memory_space=pltpu.VMEM)
    inputs = dict(
        latents=latents,
        pixels=pixels,
        mask=mask,
        out_grad=out_grad,
        panel=panel,
        down=down,
        vectors=vectors,
    )
    outputs = dict(
        latents_out=((lat, width), bf16),
        latents_grad=((lat, width), f32),
        panel_share=(panel.shape, f32),
        down_share=(down.shape, f32),
        vector_share=(vectors.shape, f32),
        norms=((2, 8, LANES), f32),
        whole_panel=(CUT + panel.shape, bf16),
        whole_down=(CUT + down.shape, bf16),
    )
    groups = width // LANES
    lines = -(-RING // 3)
    scratch = dict(
        low_panel=vmem(panel.shape, bf16),
        low_down=vmem(down.shape, bf16),
        weights=vmem((2, width, width), bf16),
        rows=vmem((vectors.shape[0] // groups, width), f32),
        pixel_low=vmem((pix, width), bf16),
        left=vmem((lat, width), bf16),
        mixed=vmem((lat, width), bf16),
        cross_query=vmem((lat, width), bf16),
        pair=vmem((pix, 2 * width), bf16),
        first=vmem((lat, width), f32),
        triple=vmem((lat, 3 * width), bf16),
        second=vmem((lat, width), f32),
        hidden=vmem((lat, wide), bf16),
        slope=vmem((lat, wide), f32),
        total=vmem((lat, width), f32),
        grad_low=vmem((lat, width), bf16),
        cross_low=vmem((lat, width), bf16),
        triple_grad=vmem((lat, 3 * width), bf16),
        query_grad=vmem((lat, width), bf16),
        pair_grad=vmem((pix, 2 * width), bf16),
        vector_grad=vmem(vectors.shape, f32),
        squares=vmem((8, LANES), f32),
        turned_pixel=vmem((2, groups, half, pix), bf16),
        landed_pixel=vmem((groups, half, pix), bf16),
        turned_hidden=vmem((2, wide // LANES // 2, hidden_parts, share_rows, lat), bf16),
        landed_hidden=vmem((wide // LANES // 2, hidden_parts, share_rows, lat), bf16),
        landed_dz=vmem((lat, width), bf16),
        landed_du=vmem((lat, wide), bf16),
        landed_ds=vmem((lat, width), bf16),
        landed_triple=vmem((lat, 3 * width), bf16),
        landed_dc=vmem((lat, width), bf16),
        landed_query=vmem((lat, width), bf16),
        landed_pair=vmem((pix, 2 * width), bf16),
        staged=vmem((STAGED, LONG, SHORT, SHORT) + unit, bf16),
        from_far=vmem((RING, LONG, SHORT) + unit, bf16),
        from_near_line=vmem((lines, LONG) + unit, bf16),
        from_near=vmem((RING - lines,) + unit, bf16),
        from_line_short=vmem((lines, 2 * (LONG - 1)) + unit, bf16),
        from_line=vmem((RING - lines, 2 * (LONG - 1), SHORT) + unit, bf16),
        direct_near=vmem((DIRECT, LONG) + unit, bf16),
        direct_line=vmem((DIRECT, LONG - 1) + unit, bf16),
        own=dma((chunks,)),
        load=dma((2,)),
        gather_send=dma((chunks * SPLIT, GATHER_KINDS)),
        gather_receive=dma((chunks * SPLIT, GATHER_KINDS)),
        reduce_send=dma((chunks, REDUCE_KINDS)),
        reduce_receive=dma((chunks, REDUCE_KINDS)),
        twin_send=dma((16 + hidden_parts,)),
        twin_receive=dma((16 + hidden_parts,)),
        credit=pltpu.SemaphoreType.REGULAR((chunks - RING, 4)),
    )
    for name in ("cross", "cross_mix", "self", "self_mix", "feed"):
        scratch[TURNED + name] = vmem((2, groups, half, lat), bf16)
        scratch[LANDED + name] = vmem((groups, half, lat), bf16)
    for name, shape in (("meet", vectors.shape), ("sum", vectors.shape), ("last", (8, LANES))):
        scratch[name + "_line"] = vmem((LONG,) + shape, f32)
        scratch[name + "_plane"] = vmem((PLANE,) + shape, f32)
        scratch[name + "_send"] = dma((LONG + PLANE - 2,))
        scratch[name + "_receive"] = dma((LONG + PLANE - 2,))
    names = tuple(inputs) + tuple(outputs) + tuple(scratch)
    sizes = (width, lat, pix, hidden_parts, threshold)
    results = pl.pallas_call(
        functools.partial(block_kernel, names, sizes),
        out_shape=[jax.ShapeDtypeStruct(*spec) for spec in outputs.values()],
        in_specs=[in_vmem] * len(inputs),
        out_specs=[in_vmem] * 6 + [any_space] * 2,
        scratch_shapes=list(scratch.values()),
        compiler_params=pltpu.CompilerParams(
            collective_id=0, has_side_effects=True, vmem_limit_bytes=VMEM_LIMIT
        ),
    )(*inputs.values())
    return results[:6]


ADAM_STEPS = 4


def adam_kernel(norms, *refs):
    factor = norms[1, 0:1, 0:1]
    ins, outs = refs[:10], refs[10:]
    for at in range(2):
        grad, weight, moment, square = ins[4 * at : 4 * at + 4]
        after = adam_update(
            weight[...], moment[...], square[...], grad[...] * factor, rate_matrix, weight_decay
        )
        for out, value in zip(outs[3 * at : 3 * at + 3], after):
            out[...] = value
    for out, value in zip(outs[6:], ins[8:]):
        out[...] = value[...]


def adam_all(norms, panels, downs, passed):
    columns = panels[0].shape[1] // ADAM_STEPS
    in_columns = pl.BlockSpec((panels[0].shape[0], columns), lambda k: (0, k))

    def in_rows(array):
        return pl.BlockSpec((array.shape[0] // ADAM_STEPS, array.shape[1]), lambda k: (k, 0))

    arrays = panels + downs + passed
    specs = [in_columns] * 4 + [in_rows(array) for array in downs + passed]
    keep = [1, 2, 3, 5, 6, 7, 8, 9]
    return pl.pallas_call(
        adam_kernel,
        grid=(ADAM_STEPS,),
        out_shape=[jax.ShapeDtypeStruct(arrays[k].shape, arrays[k].dtype) for k in keep],
        in_specs=[pl.BlockSpec(norms.shape, lambda k: (0, 0, 0))] + specs,
        out_specs=[specs[k] for k in keep],
    )(norms, *arrays)


def fast_step(
    latents,
    pixels,
    visible,
    out_grad,
    panel,
    panel_moment,
    panel_square,
    down,
    down_moment,
    down_square,
    vectors,
    vector_moment,
    vector_square,
):
    latent_count, model_width = latents.shape[1:]
    pixel_count = pixels.shape[1]
    device_total = lax.axis_size(("dp", "fsdp"))
    own_start = lax.axis_index(("dp", "fsdp")) * vectors.shape[0]
    vector_total = vectors.shape[0] * device_total
    own_vectors = lax.dynamic_update_slice(
        jnp.zeros((vector_total,), jnp.float32), vectors, (own_start,)
    )
    mask = jnp.arange(pixel_count, dtype=jnp.int32)[None, :] < visible[:, None]
    mask = jnp.broadcast_to(mask.astype(jnp.float32), (8, pixel_count))
    token_total = latents.shape[0] * latent_count * device_total
    param_total = device_total * (panel.size + down.size + vectors.size)
    threshold = clip_coeff * (token_total * param_total) ** 0.5
    latents_out, latents_grad, panel_share, down_share, vector_sum, norms = run_block(
        latents.reshape(-1, model_width),
        pixels.reshape(-1, model_width),
        mask,
        out_grad.reshape(-1, model_width),
        panel,
        down,
        own_vectors.reshape(-1, LANES),
        threshold,
    )
    vector_share = lax.dynamic_slice(vector_sum.reshape(-1), (own_start,), vectors.shape)
    grad_norm, factor = norms[0, 0, 0], norms[1, 0, 0]
    *after, latents_grad, latents_out = adam_all(
        norms,
        [panel_share, panel, panel_moment, panel_square],
        [down_share, down, down_moment, down_square],
        [latents_grad, latents_out],
    )
    return (
        latents_out.reshape(latents.shape),
        latents_grad.reshape(latents.shape),
        grad_norm,
        *after,
        *adam_update(vectors, vector_moment, vector_square, vector_share * factor, rate_vector, 0.0),
    )


def slow_gather(panel, down, vectors):
    model_width = panel.shape[1] // 12
    bf16 = jnp.bfloat16
    parts = [panel[:, k * 4 * model_width : (k + 1) * 4 * model_width].astype(bf16) for k in range(3)]
    parts += [down.astype(bf16), vectors.astype(bf16)]
    return [lax.all_gather(part, ("dp", "fsdp"), axis=0, tiled=True) for part in parts]


def slow_reduce(pieces, down_grad, vector_grad, share_length):
    shares = [
        lax.psum_scatter(grad, ("dp", "fsdp"), scatter_dimension=0, tiled=True)
        for grad in (jnp.concatenate(pieces, axis=1), down_grad, vector_grad)
    ]
    squares = lax.psum(sum(jnp.sum(share * share) for share in shares), ("dp", "fsdp"))
    return (*shares, squares)


def shards(
    gather,
    reduce,
    latents,
    pixels,
    visible,
    out_grad,
    panel,
    panel_moment,
    panel_square,
    down,
    down_moment,
    down_square,
    vectors,
    vector_moment,
    vector_square,
):
    images, latent_count, model_width = latents.shape
    pixel_count = pixels.shape[1]
    bf16 = jnp.bfloat16
    cross_columns, self_columns, up_columns, full_down, full_vector = gather(panel, down, vectors)
    vector_float = full_vector.astype(jnp.float32)
    gain_pixel = vector_slot(vector_float, 0, model_width)
    shift_pixel = vector_slot(vector_float, 1, model_width)
    gain_cross = vector_slot(vector_float, 2, model_width)
    shift_cross = vector_slot(vector_float, 3, model_width)
    gain_self = vector_slot(vector_float, 4, model_width)
    shift_self = vector_slot(vector_float, 5, model_width)
    gain_feed = vector_slot(vector_float, 6, model_width)
    shift_feed = vector_slot(vector_float, 7, model_width)
    bias_down = vector_slot(vector_float, 8, model_width)
    bias_up = vector_float[9 * model_width :]
    latent_rows = latents.reshape(-1, model_width).astype(jnp.float32)
    pixel_rows = pixels.reshape(-1, model_width).astype(jnp.float32)
    pixel_out, pixel_normed, pixel_inverse = norm_forward(pixel_rows, gain_pixel, shift_pixel)
    pixel_low = pixel_out.astype(bf16)
    cross_out, cross_normed, cross_inverse = norm_forward(latent_rows, gain_cross, shift_cross)
    cross_low = cross_out.astype(bf16)
    cross_queries = matmul_low(cross_low, cross_columns[:, :model_width]).astype(bf16)
    pair_rows = matmul_low(pixel_low, cross_columns[:, model_width : 3 * model_width]).astype(bf16)
    visible_mask = jnp.arange(pixel_count, dtype=jnp.int32)[None, :] < visible[:, None]
    query_heads = to_heads(cross_queries, images, HEADS)
    key_heads = to_heads(pair_rows[:, :model_width], images, HEADS)
    value_heads = to_heads(pair_rows[:, model_width:], images, HEADS)
    cross_mix, cross_top, cross_total = attend_forward(
        query_heads, key_heads, value_heads, visible_mask
    )
    cross_mixed = cross_mix.reshape(-1, model_width)
    first_sum = latent_rows + matmul_low(
        cross_mixed, cross_columns[:, 3 * model_width :]
    )
    forward_saved = self_forward(first_sum, self_columns, gain_self, shift_self, images)
    second_sum = first_sum + matmul_low(forward_saved[6], self_columns[:, 3 * model_width :])
    feed_out, feed_normed, feed_inverse = norm_forward(second_sum, gain_feed, shift_feed)
    feed_low = feed_out.astype(bf16)
    upper_in = matmul_low(feed_low, up_columns) + bias_up
    hidden_float, gelu_back = jax.vjp(gelu_exact, upper_in)
    hidden = hidden_float.astype(bf16)
    result = second_sum + (matmul_low(hidden, full_down) + bias_down)
    latents_out = result.astype(bf16).reshape(latents.shape)
    grad_three = out_grad.reshape(-1, model_width).astype(jnp.float32)
    grad_branch = grad_three.astype(bf16)
    grad_down = rows_inner(hidden, grad_branch)
    grad_bias_down = jnp.sum(grad_branch.astype(jnp.float32), axis=0)
    grad_upper = gelu_back(times_transposed(grad_branch, full_down))[0].astype(bf16)
    grad_up = rows_inner(feed_low, grad_upper)
    grad_bias_up = jnp.sum(grad_upper.astype(jnp.float32), axis=0)
    grad_feed, grad_gain_feed, grad_shift_feed = norm_backward(
        times_transposed(grad_upper, up_columns),
        feed_normed,
        feed_inverse,
        gain_feed,
    )
    grad_two = grad_three + grad_feed
    (
        self_normed,
        self_inverse,
        self_low,
        self_queries,
        self_keys,
        self_values,
        self_mixed,
        self_top,
        self_total,
    ) = forward_saved
    grad_self_branch = grad_two.astype(bf16)
    grad_self_out = rows_inner(self_mixed, grad_self_branch)
    grad_self_mix = times_transposed(grad_self_branch, self_columns[:, 3 * model_width :]).astype(
        bf16
    )
    grad_query_heads, grad_key_heads, grad_value_heads = attend_backward(
        to_heads(grad_self_mix, images, HEADS),
        self_queries,
        self_keys,
        self_values,
        None,
        self_top,
        self_total,
    )
    grad_triple = jnp.concatenate(
        [
            grad_query_heads.reshape(-1, model_width),
            grad_key_heads.reshape(-1, model_width),
            grad_value_heads.reshape(-1, model_width),
        ],
        axis=1,
    ).astype(bf16)
    grad_self_in = rows_inner(self_low, grad_triple)
    grad_first, grad_gain_self, grad_shift_self = norm_backward(
        times_transposed(grad_triple, self_columns[:, : 3 * model_width]),
        self_normed,
        self_inverse,
        gain_self,
    )
    grad_one = grad_two + grad_first
    grad_cross_branch = grad_one.astype(bf16)
    grad_cross_out = rows_inner(cross_mixed, grad_cross_branch)
    grad_cross_mix = times_transposed(
        grad_cross_branch, cross_columns[:, 3 * model_width :]
    ).astype(bf16)
    cross_query_grad, cross_key_grad, cross_value_grad = attend_backward(
        to_heads(grad_cross_mix, images, HEADS),
        query_heads,
        key_heads,
        value_heads,
        visible_mask,
        cross_top,
        cross_total,
    )
    grad_queries = cross_query_grad.reshape(-1, model_width).astype(bf16)
    grad_pair = jnp.concatenate(
        [cross_key_grad.reshape(-1, model_width), cross_value_grad.reshape(-1, model_width)], axis=1
    ).astype(bf16)
    grad_cross_query = rows_inner(cross_low, grad_queries)
    grad_cross_pair = rows_inner(pixel_low, grad_pair)
    grad_input_norm, grad_gain_cross, grad_shift_cross = norm_backward(
        times_transposed(grad_queries, cross_columns[:, :model_width]),
        cross_normed,
        cross_inverse,
        gain_cross,
    )
    pixel_unused, grad_gain_pixel, grad_shift_pixel = norm_backward(
        times_transposed(grad_pair, cross_columns[:, model_width : 3 * model_width]),
        pixel_normed,
        pixel_inverse,
        gain_pixel,
    )
    latents_grad = (grad_one + grad_input_norm).reshape(latents.shape)
    vector_grad = jnp.concatenate(
        [
            grad_gain_pixel,
            grad_shift_pixel,
            grad_gain_cross,
            grad_shift_cross,
            grad_gain_self,
            grad_shift_self,
            grad_gain_feed,
            grad_shift_feed,
            grad_bias_down,
            grad_bias_up,
        ]
    )
    pieces = [
        grad_cross_query,
        grad_cross_pair,
        grad_cross_out,
        grad_self_in,
        grad_self_out,
        grad_up,
    ]
    panel_share, down_share, vector_share, squares = reduce(
        pieces, grad_down, vector_grad, vectors.shape[0]
    )
    grad_norm = jnp.sqrt(squares)
    device_total = lax.axis_size(("dp", "fsdp"))
    token_total = images * latent_count * device_total
    param_total = (
        model_width * panel.shape[1] + full_down.shape[0] * model_width + full_vector.shape[0]
    )
    threshold = clip_coeff * (token_total * param_total) ** 0.5
    factor = threshold / jnp.maximum(grad_norm, threshold)
    panel_after, panel_moment_after, panel_square_after = adam_update(
        panel, panel_moment, panel_square, panel_share * factor, rate_matrix, weight_decay
    )
    down_after, down_moment_after, down_square_after = adam_update(
        down, down_moment, down_square, down_share * factor, rate_matrix, weight_decay
    )
    vectors_after, vector_moment_after, vector_square_after = adam_update(
        vectors, vector_moment, vector_square, vector_share * factor, rate_vector, 0.0
    )
    return (
        latents_out,
        latents_grad,
        grad_norm,
        panel_after,
        panel_moment_after,
        panel_square_after,
        down_after,
        down_moment_after,
        down_square_after,
        vectors_after,
        vector_moment_after,
        vector_square_after,
    )


def solution(mesh):
    placed = (
        P(("dp", "fsdp"), None, None),
        P(("dp", "fsdp"), None, None),
        P(("dp", "fsdp")),
        P(("dp", "fsdp"), None, None),
        P(("dp", "fsdp"), None),
        P(("dp", "fsdp"), None),
        P(("dp", "fsdp"), None),
        P(("dp", "fsdp"), None),
        P(("dp", "fsdp"), None),
        P(("dp", "fsdp"), None),
        P(("dp", "fsdp")),
        P(("dp", "fsdp")),
        P(("dp", "fsdp")),
    )
    fast = (mesh.shape["dp"], mesh.shape["fsdp"]) == (LONG * SHORT * SHORT, SHORT)
    step = fast_step if fast else functools.partial(shards, slow_gather, slow_reduce)
    return jax.shard_map(
        step,
        mesh=mesh,
        in_specs=placed,
        out_specs=(
            P(("dp", "fsdp"), None, None),
            P(("dp", "fsdp"), None, None),
            P(),
            P(("dp", "fsdp"), None),
            P(("dp", "fsdp"), None),
            P(("dp", "fsdp"), None),
            P(("dp", "fsdp"), None),
            P(("dp", "fsdp"), None),
            P(("dp", "fsdp"), None),
            P(("dp", "fsdp")),
            P(("dp", "fsdp")),
            P(("dp", "fsdp")),
        ),
        check_vma=False,
    )
```
